128 devices in a mesh: dp: 32 (over x, y, core), fsdp: 4 (over z).
Axes of the slice: x: 4, y: 4, z: 4, core: 2. Of those that a mesh axis runs over, the one named last changes fastest.
Arguments:
- tokens: bfloat16 [32768, 1024], P(('dp', 'fsdp')), may hold values from -6 to 6
- cotangent: bfloat16 [32768, 1024], P(('dp', 'fsdp')), may hold values from -6 to 6
- seg_counts: int32 [32, 3], P('dp'), may hold values from 1 to 1022, as said below
- qkv_master: float32 [1024, 3072], P(('fsdp', 'dp'))
- out_master: float32 [1024, 1024], P(('fsdp', 'dp'))
- up_master: float32 [1024, 4096], P(('fsdp', 'dp'))
- down_master: float32 [4096, 1024], P(('fsdp', 'dp'))
- qkv_first: float32 [1024, 3072], P(('fsdp', 'dp'))
- out_first: float32 [1024, 1024], P(('fsdp', 'dp'))
- up_first: float32 [1024, 4096], P(('fsdp', 'dp'))
- down_first: float32 [4096, 1024], P(('fsdp', 'dp'))
- qkv_second: float32 [1024, 3072], P(('fsdp', 'dp'))
- out_second: float32 [1024, 1024], P(('fsdp', 'dp'))
- up_second: float32 [1024, 4096], P(('fsdp', 'dp'))
- down_second: float32 [4096, 1024], P(('fsdp', 'dp'))
- vec_master: float32 [1024, 12], P(('fsdp', 'dp'))
- vec_first: float32 [1024, 12], P(('fsdp', 'dp'))
- vec_second: float32 [1024, 12], P(('fsdp', 'dp'))
Outputs:
- layer_out: bfloat16 [32768, 1024], P(('dp', 'fsdp'))
- input_grad: bfloat16 [32768, 1024], P(('dp', 'fsdp'))
- qkv_new: float32 [1024, 3072], P(('fsdp', 'dp'))
- out_new: float32 [1024, 1024], P(('fsdp', 'dp'))
- up_new: float32 [1024, 4096], P(('fsdp', 'dp'))
- down_new: float32 [4096, 1024], P(('fsdp', 'dp'))
- qkv_first_new: float32 [1024, 3072], P(('fsdp', 'dp'))
- out_first_new: float32 [1024, 1024], P(('fsdp', 'dp'))
- up_first_new: float32 [1024, 4096], P(('fsdp', 'dp'))
- down_first_new: float32 [4096, 1024], P(('fsdp', 'dp'))
- qkv_second_new: float32 [1024, 3072], P(('fsdp', 'dp'))
- out_second_new: float32 [1024, 1024], P(('fsdp', 'dp'))
- up_second_new: float32 [1024, 4096], P(('fsdp', 'dp'))
- down_second_new: float32 [4096, 1024], P(('fsdp', 'dp'))
- vec_new: float32 [1024, 12], P(('fsdp', 'dp'))
- vec_first_new: float32 [1024, 12], P(('fsdp', 'dp'))
- vec_second_new: float32 [1024, 12], P(('fsdp', 'dp'))
- matrix_norms: float32 [4, 2], replicated
The draws below stay inside these ranges and needn't reach their ends.
Inputs may be any that keep to these rules, and one draw needn't show every extreme that they name: `seg_counts`: row g holds the patch counts of the 3 images of data group g in the order in which they lie in its 1024 rows, and sums to 1024; its first and last counts are at most 128, and some row reaches that bound in both.
All inputs are finite; a program needn't handle non-finite values.
Results may differ from the reference program's by a relative error of at most 0.013.
The reference program's roundings to bfloat16 on the way count: a program that leaves them out, or rounds other values in their place, can miss the bound.
Values may be sent and summed in bfloat16 or wider, within the bound.
No kernel may reach another device: no remote copies, remote signals or barrier semaphores. Data moves between devices by JAX's collectives and lax.ppermute only.
A program may use at most 192 MiB of HBM per device.

```python
import math
import jax
import jax.numpy as jnp
from jax import lax

D = 1024
HEADS = 16
HEAD_DIM = 64
FF = 4096
TOK_DEV = 256
VCOLS = 12
STEP = 4
GROUPS = 32
CAP = 1024
TOKENS = 32768
N_DP = 32


def shaped(base, top, scale):
    row_total = base.shape[0]
    line = 1.0 + (top - 1.0) * jnp.arange(row_total, dtype=jnp.float32) / (row_total - 1)
    return base * (line * (2.0 * scale / (1.0 + top)))[:, None]


def second_moment(key, shape, size):
    factor = jnp.exp(jax.random.uniform(key, shape, jnp.float32, 0.0, math.log(4.0)))
    return size * size * factor


def grad_size():
    return math.sqrt(CAP / GROUPS)


def draw_seg_counts(key, part):
    key = jax.random.fold_in(key, 17)
    key_first, key_last, key_pick, key_other = jax.random.split(key, 4)
    half = TOK_DEV // 2
    first = jax.random.randint(key_first, (GROUPS,), 1, half + 1)
    last = jax.random.randint(key_last, (GROUPS,), 1, half + 1)
    pick = jax.random.randint(key_pick, (), 0, GROUPS)
    other = (pick + 1 + jax.random.randint(key_other, (), 0, GROUPS - 1)) % GROUPS
    places = jnp.arange(GROUPS)
    first = jnp.where(places == pick, 1, jnp.where(places == other, half, first))
    last = jnp.where(places == pick, 1, jnp.where(places == other, half, last))
    middle = CAP - first - last
    return jnp.stack([first, middle, last], axis=1).astype(jnp.int32)


def draw_qkv_master(key, part):
    key = jax.random.fold_in(key, 1)
    return shaped(jax.random.normal(key, (D, 3 * D), jnp.float32), 3.0, D ** (-0.5))


def draw_out_master(key, part):
    key = jax.random.fold_in(key, 2)
    return shaped(jax.random.normal(key, (D, D), jnp.float32), 3.0, math.sqrt(CAP / (3.0 * D)))


def draw_up_master(key, part):
    key = jax.random.fold_in(key, 3)
    return shaped(jax.random.normal(key, (D, FF), jnp.float32), 3.0, D ** (-0.5))


def draw_down_master(key, part):
    key = jax.random.fold_in(key, 4)
    return shaped(jax.random.normal(key, (FF, D), jnp.float32), 3.0, FF ** (-0.5))


def draw_qkv_first(key, part):
    key = jax.random.fold_in(key, 5)
    return shaped(jax.random.normal(key, (D, 3 * D), jnp.float32), 3.0, 0.7 * grad_size())


def draw_out_first(key, part):
    key = jax.random.fold_in(key, 6)
    return shaped(jax.random.normal(key, (D, D), jnp.float32), 3.0, math.sqrt(3.0 / CAP) * grad_size())


def draw_up_first(key, part):
    key = jax.random.fold_in(key, 7)
    return shaped(jax.random.normal(key, (D, FF), jnp.float32), 3.0, 0.25 * grad_size())


def draw_down_first(key, part):
    key = jax.random.fold_in(key, 8)
    return shaped(jax.random.normal(key, (FF, D), jnp.float32), 3.0, 0.6 * grad_size())


def draw_qkv_second(key, part):
    key = jax.random.fold_in(key, 9)
    return second_moment(key, (D, 3 * D), 0.7 * grad_size())


def draw_out_second(key, part):
    key = jax.random.fold_in(key, 10)
    return second_moment(key, (D, D), math.sqrt(3.0 / CAP) * grad_size())


def draw_up_second(key, part):
    key = jax.random.fold_in(key, 11)
    return second_moment(key, (D, FF), 0.25 * grad_size())


def draw_down_second(key, part):
    key = jax.random.fold_in(key, 12)
    return second_moment(key, (FF, D), 0.6 * grad_size())


def draw_vec_master(key, part):
    key = jax.random.fold_in(key, 13)
    base = jax.random.normal(key, (D, VCOLS), jnp.float32)
    columns = jnp.arange(VCOLS)[None, :]
    gain_cols = (columns == 0) | (columns == 5)
    spread = jnp.where(gain_cols, 0.2, jnp.where(columns == 3, 0.02, 0.1))
    return jnp.where(gain_cols, 1.0, 0.0) + base * spread


def draw_vec_first(key, part):
    key = jax.random.fold_in(key, 14)
    return jax.random.normal(key, (D, VCOLS), jnp.float32) * grad_size()


def draw_vec_second(key, part):
    key = jax.random.fold_in(key, 15)
    return second_moment(key, (D, VCOLS), grad_size())


def block_scale(rng, shape, cuts, least, largest):
    def one(axis_at, blocks):
        draws = jax.random.uniform(jax.random.fold_in(jax.random.fold_in(rng, 6), axis_at), (blocks,), jnp.float32, least / len(cuts), largest / len(cuts))
        return jnp.repeat(jnp.exp(draws), shape[axis_at] // blocks).reshape((-1,) + (1,) * (len(shape) - axis_at - 1))

    factor_of = one(*cuts[0])
    for cut in cuts[1:]:
        factor_of = factor_of * one(*cut)
    return factor_of


def bell_draw(own_key, extent, scale, limit, shards=(), kind=jnp.bfloat16):
    entries = scale * jax.random.normal(own_key, extent, jnp.float32)
    if shards:
        entries = entries * block_scale(own_key, extent, shards, -0.22, 0.18)
    return jnp.clip(entries, -limit, limit).astype(kind)


def setup_inputs(seed: int = 0) -> dict:
    seeds = jax.random.split(jax.random.key(seed), 19)
    tokens = bell_draw(seeds[0], (TOKENS, D), 1.0, 6.0, ((0, 128),))
    cotangent = bell_draw(seeds[1], (TOKENS, D), 1.0, 6.0, ((0, 128),))
    seg_counts = draw_seg_counts(jax.random.fold_in(seeds[18], 71), 0)
    qkv_master = draw_qkv_master(jax.random.fold_in(seeds[18], 71), 0)
    out_master = draw_out_master(jax.random.fold_in(seeds[18], 71), 0)
    up_master = draw_up_master(jax.random.fold_in(seeds[18], 71), 0)
    down_master = draw_down_master(jax.random.fold_in(seeds[18], 71), 0)
    qkv_first = draw_qkv_first(jax.random.fold_in(seeds[18], 71), 0)
    out_first = draw_out_first(jax.random.fold_in(seeds[18], 71), 0)
    up_first = draw_up_first(jax.random.fold_in(seeds[18], 71), 0)
    down_first = draw_down_first(jax.random.fold_in(seeds[18], 71), 0)
    qkv_second = draw_qkv_second(jax.random.fold_in(seeds[18], 71), 0)
    out_second = draw_out_second(jax.random.fold_in(seeds[18], 71), 0)
    up_second = draw_up_second(jax.random.fold_in(seeds[18], 71), 0)
    down_second = draw_down_second(jax.random.fold_in(seeds[18], 71), 0)
    vec_master = draw_vec_master(jax.random.fold_in(seeds[18], 71), 0)
    vec_first = draw_vec_first(jax.random.fold_in(seeds[18], 71), 0)
    vec_second = draw_vec_second(jax.random.fold_in(seeds[18], 71), 0)
    return dict(tokens=tokens, cotangent=cotangent, seg_counts=seg_counts, qkv_master=qkv_master, out_master=out_master, up_master=up_master, down_master=down_master, qkv_first=qkv_first, out_first=out_first, up_first=up_first, down_first=down_first, qkv_second=qkv_second, out_second=out_second, up_second=up_second, down_second=down_second, vec_master=vec_master, vec_first=vec_first, vec_second=vec_second)


LN_EPS = 1e-06
BETA = 0.5
ADAM_EPS = 1e-06
DECAY = 0.01
RATE = 0.5
VEC_RATE = 0.2

@jax.custom_vjp
def low(v):
    return lax.optimization_barrier(v.astype(jnp.bfloat16)).astype(jnp.float32)

@jax.custom_vjp
def low_back(v):
    return v

def low_keep(v):
    return (low(v), None)

def low_pass(kept, grad):
    return (grad,)

def back_keep(v):
    return (v, None)

def back_low(kept, grad):
    return (low(grad),)
low.defvjp(low_keep, low_pass)
low_back.defvjp(back_keep, back_low)

def layer_norm(values, gain_vec, shift_vec):
    centre = lax.optimization_barrier(jnp.mean(values, -1, keepdims=True))
    centred = values - centre
    spread = lax.optimization_barrier(jnp.mean(centred * centred, -1, keepdims=True))
    return centred * lax.rsqrt(spread + LN_EPS) * gain_vec + shift_vec

def product(left, right):
    return jnp.dot(left, right, precision=lax.Precision.HIGHEST, preferred_element_type=jnp.float32)

def segment_ids(counts, length):
    places = jnp.arange(length, dtype=jnp.int32)
    first = counts[0].astype(jnp.int32)
    second = first + counts[1].astype(jnp.int32)
    return (places >= first).astype(jnp.int32) + (places >= second).astype(jnp.int32)

def block_forward(inputs, counts, w_qkv, w_out, w_up, w_down, vectors):
    length = inputs.shape[0]
    width = inputs.shape[1]
    normed = low(layer_norm(inputs, vectors[:, 0], vectors[:, 1]))
    qkv_bias = jnp.concatenate([vectors[:, 2], jnp.zeros_like(vectors[:, 2]), vectors[:, 3]])
    qkv_rows = low(low_back(product(normed, w_qkv) + qkv_bias))
    query_heads = qkv_rows[:, :width].reshape(length, HEADS, HEAD_DIM)
    key_heads = qkv_rows[:, width:2 * width].reshape(length, HEADS, HEAD_DIM)
    value_heads = qkv_rows[:, 2 * width:].reshape(length, HEADS, HEAD_DIM)
    image_of = segment_ids(counts, length)
    same_image = (image_of[:, None] == image_of[None, :])[None]
    scores = jnp.einsum('qhd,khd->hqk', query_heads, key_heads, precision=lax.Precision.HIGHEST) * HEAD_DIM ** (-0.5)
    scores = low_back(scores)
    probs = jax.nn.softmax(jnp.where(same_image, scores, -1e+30), axis=-1)
    attended = jnp.einsum('hqk,khd->qhd', low(probs), value_heads, precision=lax.Precision.HIGHEST)
    attended = low(low_back(attended.reshape(length, width)))
    middle = inputs + low_back(product(attended, w_out) + vectors[:, 4])
    normed_mid = low(layer_norm(middle, vectors[:, 5], vectors[:, 6]))
    up_bias = vectors[:, 7:11].T.reshape(-1)
    pre_act = low_back(product(normed_mid, w_up) + up_bias)
    hidden = low(jax.nn.gelu(pre_act, approximate=False))
    return middle + low_back(product(hidden, w_down) + vectors[:, 11])

def adam_step(grad_mean, moment, square, weight, decay_rate):
    moment_new = BETA * moment + (1.0 - BETA) * grad_mean
    square_new = BETA * square + (1.0 - BETA) * grad_mean * grad_mean
    correct = 1.0 - BETA ** STEP
    direction = moment_new / correct / (jnp.sqrt(square_new / correct) + ADAM_EPS) + decay_rate * weight
    return (moment_new, square_new, direction)

def reference(tokens, cotangent, seg_counts, qkv_master, out_master, up_master, down_master, qkv_first, out_first, up_first, down_first, qkv_second, out_second, up_second, down_second, vec_master, vec_first, vec_second):
    grouped = tokens.astype(jnp.float32).reshape(GROUPS, CAP, D)

    def forward(inputs, master_qkv, master_out, master_up, master_down, master_vec):
        low_qkv = low(master_qkv)
        low_out = low(master_out)
        low_up = low(master_up)
        low_down = low(master_down)
        low_vec = low(master_vec)

        def one_group(item):
            return block_forward(item[0], item[1], low_qkv, low_out, low_up, low_down, low_vec)
        return lax.map(jax.checkpoint(one_group), (inputs, seg_counts))
    outputs, pullback = jax.vjp(forward, grouped, qkv_master, out_master, up_master, down_master, vec_master)
    grads = pullback(cotangent.astype(jnp.float32).reshape(GROUPS, CAP, D))
    layer_out = outputs.reshape(TOKENS, D).astype(jnp.bfloat16)
    input_grad = grads[0].reshape(TOKENS, D).astype(jnp.bfloat16)
    masters = (qkv_master, out_master, up_master, down_master)
    firsts = (qkv_first, out_first, up_first, down_first)
    seconds = (qkv_second, out_second, up_second, down_second)
    results = [adam_step(grad_sum / N_DP, moment, square, weight, DECAY) for grad_sum, moment, square, weight in zip(grads[1:5], firsts, seconds, masters)]
    weight_norm = jnp.stack([jnp.sqrt(jnp.sum(weight * weight)) for weight in masters])
    update_norm = jnp.stack([jnp.sqrt(jnp.sum(parts[2] * parts[2])) for parts in results])
    ratio = weight_norm / update_norm
    new_mats = [weight - RATE * ratio[place] * parts[2] for place, (weight, parts) in enumerate(zip(masters, results))]
    vec_moment, vec_square, vec_dir = adam_step(grads[5] / N_DP, vec_first, vec_second, vec_master, 0.0)
    vec_new = vec_master - VEC_RATE * vec_dir
    matrix_norms = jnp.stack([weight_norm, update_norm], axis=1)
    return (layer_out, input_grad, new_mats[0], new_mats[1], new_mats[2], new_mats[3], results[0][0], results[1][0], results[2][0], results[3][0], results[0][1], results[1][1], results[2][1], results[3][1], vec_new, vec_moment, vec_square, matrix_norms)
```

```python
import jax
import jax.numpy as jnp
from jax import lax
from jax.sharding import Mesh
from jax.sharding import PartitionSpec as P

HEADS = 16
HEAD_DIM = 64
STEP = 4

LN_EPS = 1e-06
BETA = 0.5
ADAM_EPS = 1e-06
DECAY = 0.01
RATE = 0.5
VEC_RATE = 0.2

LOW = jnp.bfloat16
WIDE = jnp.float32
DATA = ("x", "y", "c")
EVERY = ("x", "y", "c", "z")
RING = 4
VEC_PAD = 128


def send(block, axis, step):
    size = lax.axis_size(axis)
    return lax.ppermute(block, axis, [(i, (i + step) % size) for i in range(size)])


def gather_z(block):
    half = block.shape[0] // 2
    from_prev = send(block, "z", 1)
    from_next = send(block, "z", -1)
    far = jnp.concatenate([send(from_prev[:half], "z", 1), send(from_next[half:], "z", -1)])
    return jnp.concatenate([block, from_next, far, from_prev])


def scatter_z(partial):
    rows = partial.shape[0] // RING
    half = rows // 2
    own, after, far, before = (partial[k * rows : (k + 1) * rows] for k in range(RING))
    far = far.astype(LOW)
    from_prev = send(far[:half], "z", 1).astype(WIDE)
    from_next = send(far[half:], "z", -1).astype(WIDE)
    after = jnp.concatenate([after[:half] + from_prev, after[half:]])
    before = jnp.concatenate([before[:half], before[half:] + from_next])
    return (
        own
        + send(after.astype(LOW), "z", 1).astype(WIDE)
        + send(before.astype(LOW), "z", -1).astype(WIDE)
    )


def swap_z(pieces):
    place = lax.axis_index("z")

    def piece(step):
        return lax.dynamic_index_in_dim(pieces, (place + step) % RING, 0, keepdims=False)

    arrived = jnp.stack([piece(0), send(piece(3), "z", 3), send(piece(2), "z", 2), send(piece(1), "z", 1)])
    return jnp.roll(arrived, place, axis=0)


def sum_everywhere(values):
    for axis in ("c", "x", "y", "z"):
        size = lax.axis_size(axis)
        apart = 1
        while apart < size:
            values = values + lax.ppermute(values, axis, [(i, i ^ apart) for i in range(size)])
            apart *= 2
    return values


def normalise(values):
    centre = jnp.mean(values, -1, keepdims=True)
    centred = values - centre
    spread = jnp.mean(centred * centred, -1, keepdims=True)
    scale = lax.rsqrt(spread + LN_EPS)
    return centred * scale, scale


def normalise_back(grad, unit, scale, gain):
    grad_unit = grad * gain
    return scale * (
        grad_unit
        - jnp.mean(grad_unit, -1, keepdims=True)
        - unit * jnp.mean(grad_unit * unit, -1, keepdims=True)
    )


def adam_step(grad_mean, moment, square, weight, decay_rate):
    moment_new = BETA * moment + (1.0 - BETA) * grad_mean
    square_new = BETA * square + (1.0 - BETA) * grad_mean * grad_mean
    correct = 1.0 - BETA**STEP
    direction = (
        moment_new / correct / (jnp.sqrt(square_new / correct) + ADAM_EPS) + decay_rate * weight
    )
    return (moment_new, square_new, direction)


def dot(left, right, dims):
    return lax.dot_general(left, right, (dims, ((), ())), preferred_element_type=WIDE)


def on_device(
    tokens,
    cotangent,
    seg_counts,
    qkv_master,
    out_master,
    up_master,
    down_master,
    qkv_first,
    out_first,
    up_first,
    down_first,
    qkv_second,
    out_second,
    up_second,
    down_second,
    vec_master,
    vec_first,
    vec_second,
):
    masters = (qkv_master, out_master, up_master, down_master)
    place = lax.axis_index("z")
    rows, width = tokens.shape
    own = qkv_master.shape[0]
    lanes = width // RING
    hidden_lanes = up_master.shape[1] // RING
    data = lax.axis_size("x") * lax.axis_size("y") * lax.axis_size("c")
    heads = HEADS // RING
    group = rows * RING

    qkv_parts = (
        qkv_master.astype(LOW)
        .reshape(own, 3, RING, lanes)
        .transpose(2, 0, 1, 3)
        .reshape(RING, own, 3 * lanes)
    )
    vec_low = jnp.pad(vec_master.astype(LOW), ((0, 0), (0, VEC_PAD - vec_master.shape[1])))
    up_parts = up_master.astype(LOW).reshape(own, RING, hidden_lanes).transpose(1, 0, 2)
    weight_parts = jnp.concatenate(
        [qkv_parts, jnp.broadcast_to(vec_low, (RING, own, VEC_PAD)), up_parts], axis=2
    )
    arrived = swap_z(weight_parts)
    att_columns = 3 * lanes + VEC_PAD
    first_pack = lax.all_gather(arrived[:, :, :att_columns], DATA, axis=0)
    first_pack = first_pack.transpose(1, 0, 2, 3).reshape(width, att_columns)
    w_qkv = first_pack[:, : 3 * lanes]
    vectors = first_pack[:, 3 * lanes : 3 * lanes + vec_master.shape[1]].astype(WIDE)

    inputs = gather_z(tokens)
    w_out = lax.all_gather(out_master.astype(LOW), DATA, axis=0, tiled=True)
    w_up = lax.all_gather(arrived[:, :, att_columns:], DATA, axis=0)
    w_up = w_up.transpose(1, 0, 2, 3).reshape(width, hidden_lanes)
    w_down = lax.all_gather(down_master.astype(LOW), DATA, axis=0, tiled=True)
    cotangents = gather_z(cotangent)

    unit_first, scale_first = normalise(inputs.astype(WIDE))
    normed = (unit_first * vectors[:, 0] + vectors[:, 1]).astype(LOW)
    query_bias = lax.dynamic_slice_in_dim(vectors[:, 2], place * lanes, lanes)
    value_bias = lax.dynamic_slice_in_dim(vectors[:, 3], place * lanes, lanes)
    qkv_bias = jnp.concatenate([query_bias, jnp.zeros((lanes,), WIDE), value_bias])
    qkv_rows = (dot(normed, w_qkv, ((1,), (0,))) + qkv_bias).astype(LOW)
    query_heads = qkv_rows[:, :lanes].reshape(group, heads, HEAD_DIM)
    key_heads = qkv_rows[:, lanes : 2 * lanes].reshape(group, heads, HEAD_DIM)
    value_heads = qkv_rows[:, 2 * lanes :].reshape(group, heads, HEAD_DIM)

    index = jnp.arange(group, dtype=jnp.int32)
    places = (place + index // rows) % RING * rows + index % rows
    first_end = seg_counts[0, 0]
    second_end = first_end + seg_counts[0, 1]
    image = (places >= first_end).astype(jnp.int32) + (places >= second_end).astype(jnp.int32)
    same_image = (image[:, None] == image[None, :])[None]
    score_scale = HEAD_DIM ** (-0.5)
    scores = (
        jnp.einsum("qhd,khd->hqk", query_heads, key_heads, preferred_element_type=WIDE) * score_scale
    )
    scores = jnp.where(same_image, scores, -1e30)
    row_max = jnp.max(scores, -1, keepdims=True)
    exponent = jnp.exp(scores - row_max)
    row_total = jnp.sum(exponent, -1, keepdims=True)
    probs = exponent / row_total
    attended = jnp.einsum("hqk,khd->qhd", probs.astype(LOW), value_heads, preferred_element_type=WIDE)
    attended = attended.reshape(group, lanes).astype(LOW)
    att_out = scatter_z(dot(attended, w_out, ((1,), (0,))))
    middle = tokens.astype(WIDE) + (att_out + vectors[:, 4])

    unit_mid, scale_mid = normalise(middle)
    normed_mid = gather_z((unit_mid * vectors[:, 5] + vectors[:, 6]).astype(LOW))
    up_bias = lax.dynamic_index_in_dim(vectors[:, 7:11], place, 1, keepdims=False)
    pre_act = dot(normed_mid, w_up, ((1,), (0,))) + up_bias
    below = 0.5 * (1.0 + lax.erf(pre_act * (0.5**0.5)))
    hidden = (pre_act * below).astype(LOW)
    slope = below + pre_act * (jnp.exp(-0.5 * pre_act * pre_act) * 0.3989422804014327)

    grad_hidden = dot(cotangents, w_down, ((1,), (1,)))
    grad_pre_wide = grad_hidden * slope
    grad_pre = grad_pre_wide.astype(LOW)
    grad_normed_mid = scatter_z(dot(grad_pre, w_up, ((1,), (1,))))
    ffn_out = scatter_z(dot(hidden, w_down, ((1,), (0,))))
    layer_out = (middle + (ffn_out + vectors[:, 11])).astype(LOW)
    grad_up = dot(normed_mid, grad_pre, ((0,), (0,)))
    grad_down = dot(hidden, cotangents, ((0,), (0,)))

    def scatter_data(grad):
        return lax.psum_scatter(grad, DATA, scatter_dimension=0, tiled=True)

    def by_owner(grad):
        columns = grad.shape[1]
        return (
            grad.reshape(RING, data, own, columns)
            .transpose(1, 0, 2, 3)
            .reshape(data * RING * own, columns)
        )

    up_sum = scatter_data(by_owner(grad_up)).reshape(RING, own, hidden_lanes)
    down_sum = scatter_data(grad_down)

    grad_middle = cotangent.astype(WIDE) + normalise_back(
        grad_normed_mid, unit_mid, scale_mid, vectors[:, 5]
    )
    grad_mid_own = grad_middle.astype(LOW)
    grad_mid_low = gather_z(grad_mid_own)
    grad_out = dot(attended, grad_mid_low, ((0,), (0,)))
    out_sum = scatter_data(grad_out)

    grad_att = dot(grad_mid_low, w_out, ((1,), (1,))).astype(LOW).reshape(group, heads, HEAD_DIM)
    grad_probs = jnp.einsum("qhd,khd->hqk", grad_att, value_heads, preferred_element_type=WIDE)
    row_inner = jnp.sum(probs * grad_probs, -1, keepdims=True)
    grad_scores = (probs * (grad_probs - row_inner)).astype(LOW)
    grad_query = (
        jnp.einsum("hqk,khd->qhd", grad_scores, key_heads, preferred_element_type=WIDE) * score_scale
    )
    grad_key = (
        jnp.einsum("hqk,qhd->khd", grad_scores, query_heads, preferred_element_type=WIDE)
        * score_scale
    )
    grad_value = jnp.einsum("hqk,qhd->khd", probs.astype(LOW), grad_att, preferred_element_type=WIDE)
    grad_qkv = jnp.concatenate(
        [grad.reshape(group, lanes).astype(LOW) for grad in (grad_query, grad_key, grad_value)],
        axis=1,
    )
    grad_qkv_w = dot(normed, grad_qkv, ((0,), (0,)))
    grad_normed_part = dot(grad_qkv, w_qkv, ((1,), (1,)))

    def in_place(values, length):
        return lax.dynamic_update_slice_in_dim(
            jnp.zeros((length,), WIDE), values, place * lanes, 0
        )

    bias_sums = jnp.sum(grad_qkv, axis=0, dtype=WIDE)
    up_column = jnp.sum(grad_pre, axis=0, dtype=WIDE)
    vec_rows = jnp.stack(
        [
            jnp.sum(grad_normed_part * unit_first, axis=0),
            jnp.sum(grad_normed_part, axis=0),
            in_place(bias_sums[:lanes], width),
            in_place(bias_sums[2 * lanes :], width),
            jnp.sum(grad_mid_own, axis=0, dtype=WIDE),
            jnp.sum(grad_normed_mid * unit_mid, axis=0),
            jnp.sum(grad_normed_mid, axis=0),
        ]
        + [jnp.where(place == k, up_column, 0.0) for k in range(RING)]
        + [jnp.sum(cotangent, axis=0, dtype=WIDE)]
    )
    vec_columns = jnp.pad(vec_rows, ((0, VEC_PAD - vec_rows.shape[0]), (0, 0))).T
    att_sum = scatter_data(by_owner(jnp.concatenate([grad_qkv_w, vec_columns], axis=1)))
    att_sum = att_sum.reshape(RING, own, att_columns)

    grad_normed = scatter_z(grad_normed_part)
    input_grad = (
        grad_middle
        + normalise_back(grad_normed, unit_first[:rows], scale_first[:rows], vectors[:, 0])
    ).astype(LOW)

    home = swap_z(jnp.concatenate([att_sum, up_sum], axis=2))
    qkv_sum = (
        home[:, :, : 3 * lanes]
        .reshape(RING, own, 3, lanes)
        .transpose(1, 2, 0, 3)
        .reshape(own, 3 * width)
    )
    vec_sum = jnp.sum(home[:, :, 3 * lanes : 3 * lanes + vec_master.shape[1]], axis=0)
    up_sum = home[:, :, att_columns:].transpose(1, 0, 2).reshape(own, RING * hidden_lanes)

    firsts = (qkv_first, out_first, up_first, down_first)
    seconds = (qkv_second, out_second, up_second, down_second)
    results = [
        adam_step(grad_sum / data, moment, square, weight, DECAY)
        for grad_sum, moment, square, weight in zip(
            (qkv_sum, out_sum, up_sum, down_sum), firsts, seconds, masters
        )
    ]
    squares = jnp.stack(
        [jnp.sum(matrix * matrix) for matrix in masters]
        + [jnp.sum(parts[2] * parts[2]) for parts in results]
    )
    tile = jnp.broadcast_to(squares[:, None], (8, 128))
    totals = jnp.sqrt(sum_everywhere(tile)[:, 0])
    weight_norm = totals[:4]
    update_norm = totals[4:]
    ratio = weight_norm / update_norm
    new_mats = [
        weight - RATE * ratio[k] * parts[2] for k, (weight, parts) in enumerate(zip(masters, results))
    ]
    vec_moment, vec_square, vec_dir = adam_step(
        vec_sum / data, vec_first, vec_second, vec_master, 0.0
    )
    vec_new = vec_master - VEC_RATE * vec_dir
    matrix_norms = jnp.stack([weight_norm, update_norm], axis=1)
    return (
        layer_out,
        input_grad,
        *new_mats,
        *(parts[0] for parts in results),
        *(parts[1] for parts in results),
        vec_new,
        vec_moment,
        vec_square,
        matrix_norms,
    )


def solution(mesh):
    sizes = (4, 4, 2, 4)
    physical = Mesh(mesh.devices.reshape(sizes), EVERY)
    patches = P(EVERY, None)
    shards = P(("z", *DATA), None)
    return jax.shard_map(
        on_device,
        mesh=physical,
        in_specs=(patches, patches, P(DATA, None)) + (shards,) * 15,
        out_specs=(patches, patches) + (shards,) * 15 + (P(),),
        check_vma=False,
    )
```

```python
import jax
import jax.numpy as jnp
from jax import lax
from jax.experimental import pallas as pl
from jax.experimental.pallas import tpu as pltpu
from jax.sharding import Mesh
from jax.sharding import PartitionSpec as P

HEADS = 16
HEAD_DIM = 64
STEP = 4

LN_EPS = 1e-06
BETA = 0.5
ADAM_EPS = 1e-06
DECAY = 0.01
RATE = 0.5
VEC_RATE = 0.2

LOW = jnp.bfloat16
WIDE = jnp.float32
DATA = ("x", "y", "c")
EVERY = ("x", "y", "c", "z")
RING = 4
VEC_PAD = 128


def send(block, axis, step):
    size = lax.axis_size(axis)
    return lax.ppermute(block, axis, [(i, (i + step) % size) for i in range(size)])


def gather_z(block):
    half = block.shape[0] // 2
    from_prev = send(block, "z", 1)
    from_next = send(block, "z", -1)
    far = jnp.concatenate([send(from_prev[:half], "z", 1), send(from_next[half:], "z", -1)])
    return jnp.concatenate([block, from_next, far, from_prev])


def scatter_z(partial):
    rows = partial.shape[0] // RING
    half = rows // 2
    own, after, far, before = (partial[k * rows : (k + 1) * rows] for k in range(RING))
    far = far.astype(LOW)
    from_prev = send(far[:half], "z", 1).astype(WIDE)
    from_next = send(far[half:], "z", -1).astype(WIDE)
    after = jnp.concatenate([after[:half] + from_prev, after[half:]])
    before = jnp.concatenate([before[:half], before[half:] + from_next])
    return (
        own
        + send(after.astype(LOW), "z", 1).astype(WIDE)
        + send(before.astype(LOW), "z", -1).astype(WIDE)
    )


def swap_z(pieces):
    place = lax.axis_index("z")

    def piece(step):
        return lax.dynamic_index_in_dim(pieces, (place + step) % RING, 0, keepdims=False)

    arrived = jnp.stack([piece(0), send(piece(3), "z", 3), send(piece(2), "z", 2), send(piece(1), "z", 1)])
    return jnp.roll(arrived, place, axis=0)


def send_split(block, phase, step):
    sizes = [lax.axis_size(axis) for axis in DATA]
    pairs = []
    for x in range(sizes[0]):
        for y in range(sizes[1]):
            for c in range(sizes[2]):
                if c == phase:
                    to = ((x + step) % sizes[0], y)
                else:
                    to = (x, (y + step) % sizes[1])
                pairs.append(
                    ((x * sizes[1] + y) * sizes[2] + c, (to[0] * sizes[1] + to[1]) * sizes[2] + c)
                )
    return lax.ppermute(block, DATA, pairs)


def chip_of(where, first, second):
    x, y, c = where[0], where[1], where[2]
    along_x = (x + jnp.where(c == 0, first, second)) % RING
    along_y = (y + jnp.where(c == 0, second, first)) % RING
    return along_x * RING + along_y


def place_kernel(where, pieces, out):
    for second in range(RING):
        for first in range(RING):
            out[:, chip_of(where, first, second)] = pieces[second, first]


def place_by_chip(pieces, where):
    shape = pieces.shape
    return pl.pallas_call(
        place_kernel,
        out_shape=jax.ShapeDtypeStruct((shape[2], RING * RING, *shape[3:]), pieces.dtype),
        in_specs=[
            pl.BlockSpec(memory_space=pltpu.SMEM),
            pl.BlockSpec(memory_space=pltpu.VMEM),
        ],
        out_specs=pl.BlockSpec(memory_space=pltpu.VMEM),
        compiler_params=pltpu.CompilerParams(vmem_limit_bytes=32 << 20),
    )(where, pieces)


def gather_chips(shard, where):
    core = where[2]
    other = send(shard, "c", 1)
    both = jnp.where(
        core == 0, jnp.concatenate([shard, other], 1), jnp.concatenate([other, shard], 1)
    )
    half = both.shape[0] // 2
    block = lax.dynamic_slice_in_dim(both, core * half, half, 0)
    for phase in range(2):
        block = jnp.stack(
            [block] + [send_split(block, phase, -distance) for distance in range(1, RING)]
        )
    mine = place_by_chip(block, where)
    theirs = send(mine, "c", 1)
    return jnp.concatenate(
        [jnp.where(core == 0, mine, theirs), jnp.where(core == 0, theirs, mine)]
    )


def arrange_kernel(where, grad, arrived, own, *gone):
    for second in range(RING):
        for first in range(RING):
            chip = chip_of(where, first, second)
            total = grad[:, chip] + arrived[:, chip].astype(WIDE)
            if first == 0:
                own[second] = total
            else:
                gone[first - 1][second] = total.astype(LOW)


def scatter_chips(grad, where):
    depth, chips, rows, columns = grad.shape
    half = depth // 2
    core = where[2]
    arrived = send(lax.dynamic_slice_in_dim(grad, (1 - core) * half, half, 0).astype(LOW), "c", 1)
    piece = (RING, half, rows, columns)
    own, *gone = pl.pallas_call(
        arrange_kernel,
        out_shape=[jax.ShapeDtypeStruct(piece, WIDE)] + [jax.ShapeDtypeStruct(piece, LOW)] * 3,
        grid_spec=pltpu.PrefetchScalarGridSpec(
            num_scalar_prefetch=1,
            grid=(1,),
            in_specs=[
                pl.BlockSpec((half, chips, rows, columns), lambda i, where: (where[2], 0, 0, 0)),
                pl.BlockSpec((half, chips, rows, columns), lambda i, where: (0, 0, 0, 0)),
            ],
            out_specs=[pl.BlockSpec(piece, lambda i, where: (0, 0, 0, 0))] * 4,
        ),
        compiler_params=pltpu.CompilerParams(vmem_limit_bytes=48 << 20),
    )(where, grad, arrived)
    total = own
    for distance in range(1, RING):
        total = total + send_split(gone[distance - 1], 0, distance).astype(WIDE)
    own, low = total[0], total.astype(LOW)
    for distance in range(1, RING):
        own = own + send_split(low[distance], 1, distance).astype(WIDE)
    return own


def sum_everywhere(values):
    for axis in ("c", "x", "y", "z"):
        size = lax.axis_size(axis)
        apart = 1
        while apart < size:
            values = values + lax.ppermute(values, axis, [(i, i ^ apart) for i in range(size)])
            apart *= 2
    return values


def normalise(values):
    centre = jnp.mean(values, -1, keepdims=True)
    centred = values - centre
    spread = jnp.mean(centred * centred, -1, keepdims=True)
    scale = lax.rsqrt(spread + LN_EPS)
    return centred * scale, scale


def normalise_back(grad, unit, scale, gain):
    grad_unit = grad * gain
    return scale * (
        grad_unit
        - jnp.mean(grad_unit, -1, keepdims=True)
        - unit * jnp.mean(grad_unit * unit, -1, keepdims=True)
    )


def adam_step(grad_mean, moment, square, weight, decay_rate):
    moment_new = BETA * moment + (1.0 - BETA) * grad_mean
    square_new = BETA * square + (1.0 - BETA) * grad_mean * grad_mean
    correct = 1.0 - BETA**STEP
    direction = (
        moment_new / correct / (jnp.sqrt(square_new / correct) + ADAM_EPS) + decay_rate * weight
    )
    return (moment_new, square_new, direction)


def dot(left, right, dims):
    return lax.dot_general(left, right, (dims, ((), ())), preferred_element_type=WIDE)


def on_device(
    tokens,
    cotangent,
    seg_counts,
    qkv_master,
    out_master,
    up_master,
    down_master,
    qkv_first,
    out_first,
    up_first,
    down_first,
    qkv_second,
    out_second,
    up_second,
    down_second,
    vec_master,
    vec_first,
    vec_second,
):
    masters = (qkv_master, out_master, up_master, down_master)
    place = lax.axis_index("z")
    core = lax.axis_index("c")
    where = jnp.stack([lax.axis_index(axis) for axis in DATA]).astype(jnp.int32)
    rows, width = tokens.shape
    own = qkv_master.shape[0]
    lanes = width // RING
    hidden_lanes = up_master.shape[1] // RING
    data = lax.axis_size("x") * lax.axis_size("y") * lax.axis_size("c")
    heads = HEADS // RING
    group = rows * RING

    qkv_parts = (
        qkv_master.astype(LOW)
        .reshape(own, 3, RING, lanes)
        .transpose(2, 0, 1, 3)
        .reshape(RING, own, 3 * lanes)
    )
    vec_low = jnp.pad(vec_master.astype(LOW), ((0, 0), (0, VEC_PAD - vec_master.shape[1])))
    up_parts = up_master.astype(LOW).reshape(own, RING, hidden_lanes).transpose(1, 0, 2)
    weight_parts = jnp.concatenate(
        [qkv_parts, jnp.broadcast_to(vec_low, (RING, own, VEC_PAD)), up_parts], axis=2
    )
    inputs = gather_z(tokens)
    arrived = swap_z(weight_parts)
    att_columns = 3 * lanes + VEC_PAD
    out_parts = out_master.astype(LOW).reshape(own, RING, lanes).transpose(1, 0, 2)
    att_weights = gather_chips(
        jnp.concatenate([arrived[:, :, :att_columns], out_parts], axis=2), where
    )
    att_rows = att_weights.reshape(width, att_columns + lanes)
    w_qkv = att_rows[:, : 3 * lanes]
    vectors = att_rows[:, 3 * lanes : 3 * lanes + vec_master.shape[1]].astype(WIDE)
    w_out = (
        att_weights.reshape(RING, lanes, att_columns + lanes)[:, :, att_columns:]
        .transpose(1, 0, 2)
        .reshape(lanes, width)
    )

    ffn_shard = jnp.concatenate(
        [arrived[:, :, att_columns:].reshape(RING * own, hidden_lanes), down_master.astype(LOW)]
    )
    ffn_weights = lax.all_gather(ffn_shard, DATA, axis=0)
    w_up = (
        ffn_weights[:, : RING * own]
        .reshape(data, RING, own, hidden_lanes)
        .transpose(1, 0, 2, 3)
        .reshape(width, hidden_lanes)
    )
    w_down = ffn_weights[:, RING * own :].reshape(hidden_lanes, width)
    cotangents = gather_z(cotangent)

    unit_first, scale_first = normalise(inputs.astype(WIDE))
    normed = (unit_first * vectors[:, 0] + vectors[:, 1]).astype(LOW)
    query_bias = lax.dynamic_slice_in_dim(vectors[:, 2], place * lanes, lanes)
    value_bias = lax.dynamic_slice_in_dim(vectors[:, 3], place * lanes, lanes)
    qkv_bias = jnp.concatenate([query_bias, jnp.zeros((lanes,), WIDE), value_bias])
    qkv_rows = (dot(normed, w_qkv, ((1,), (0,))) + qkv_bias).astype(LOW)
    query_heads = qkv_rows[:, :lanes].reshape(group, heads, HEAD_DIM)
    key_heads = qkv_rows[:, lanes : 2 * lanes].reshape(group, heads, HEAD_DIM)
    value_heads = qkv_rows[:, 2 * lanes :].reshape(group, heads, HEAD_DIM)

    index = jnp.arange(group, dtype=jnp.int32)
    places = (place + index // rows) % RING * rows + index % rows
    first_end = seg_counts[0, 0]
    second_end = first_end + seg_counts[0, 1]
    image = (places >= first_end).astype(jnp.int32) + (places >= second_end).astype(jnp.int32)
    same_image = (image[:, None] == image[None, :])[None]
    score_scale = HEAD_DIM ** (-0.5)
    scores = (
        jnp.einsum("qhd,khd->hqk", query_heads, key_heads, preferred_element_type=WIDE) * score_scale
    )
    scores = jnp.where(same_image, scores, -1e30)
    row_max = jnp.max(scores, -1, keepdims=True)
    exponent = jnp.exp(scores - row_max)
    row_total = jnp.sum(exponent, -1, keepdims=True)
    probs = exponent / row_total
    attended = jnp.einsum("hqk,khd->qhd", probs.astype(LOW), value_heads, preferred_element_type=WIDE)
    attended = attended.reshape(group, lanes).astype(LOW)
    att_out = scatter_z(dot(attended, w_out, ((1,), (0,))))
    middle = tokens.astype(WIDE) + (att_out + vectors[:, 4])

    unit_mid, scale_mid = normalise(middle)
    normed_mid = gather_z((unit_mid * vectors[:, 5] + vectors[:, 6]).astype(LOW))
    up_bias = lax.dynamic_index_in_dim(vectors[:, 7:11], place, 1, keepdims=False)
    pre_act = dot(normed_mid, w_up, ((1,), (0,))) + up_bias
    below = 0.5 * (1.0 + lax.erf(pre_act * (0.5**0.5)))
    hidden = (pre_act * below).astype(LOW)
    slope = below + pre_act * (jnp.exp(-0.5 * pre_act * pre_act) * 0.3989422804014327)

    grad_hidden = dot(cotangents, w_down, ((1,), (1,)))
    grad_pre_wide = grad_hidden * slope
    grad_pre = grad_pre_wide.astype(LOW)
    grad_normed_mid = scatter_z(dot(grad_pre, w_up, ((1,), (1,))))
    ffn_out = scatter_z(dot(hidden, w_down, ((1,), (0,))))
    layer_out = (middle + (ffn_out + vectors[:, 11])).astype(LOW)
    grad_up = dot(normed_mid, grad_pre, ((0,), (0,)))
    grad_down = dot(hidden, cotangents, ((0,), (0,)))

    ffn_grads = jnp.concatenate(
        [
            grad_up.astype(LOW)
            .reshape(RING, data, own, hidden_lanes)
            .transpose(1, 0, 2, 3)
            .reshape(data, RING * own, hidden_lanes),
            grad_down.astype(LOW).reshape(data, RING * own, width),
        ],
        axis=1,
    )
    ffn_sum = lax.psum_scatter(ffn_grads, DATA, scatter_dimension=0).astype(WIDE)
    up_sum = ffn_sum[: RING * own].reshape(RING, own, hidden_lanes)
    down_sum = ffn_sum[RING * own :]

    grad_middle = cotangent.astype(WIDE) + normalise_back(
        grad_normed_mid, unit_mid, scale_mid, vectors[:, 5]
    )
    grad_mid_own = grad_middle.astype(LOW)
    grad_mid_low = gather_z(grad_mid_own)
    grad_out = dot(attended, grad_mid_low, ((0,), (0,)))

    grad_att = dot(grad_mid_low, w_out, ((1,), (1,))).astype(LOW).reshape(group, heads, HEAD_DIM)
    grad_probs = jnp.einsum("qhd,khd->hqk", grad_att, value_heads, preferred_element_type=WIDE)
    row_inner = jnp.sum(probs * grad_probs, -1, keepdims=True)
    grad_scores = (probs * (grad_probs - row_inner)).astype(LOW)
    grad_query = (
        jnp.einsum("hqk,khd->qhd", grad_scores, key_heads, preferred_element_type=WIDE) * score_scale
    )
    grad_key = (
        jnp.einsum("hqk,qhd->khd", grad_scores, query_heads, preferred_element_type=WIDE)
        * score_scale
    )
    grad_value = jnp.einsum("hqk,qhd->khd", probs.astype(LOW), grad_att, preferred_element_type=WIDE)
    grad_qkv = jnp.concatenate(
        [grad.reshape(group, lanes).astype(LOW) for grad in (grad_query, grad_key, grad_value)],
        axis=1,
    )
    grad_qkv_w = dot(normed, grad_qkv, ((0,), (0,)))
    grad_normed_part = dot(grad_qkv, w_qkv, ((1,), (1,)))

    def in_place(values, length):
        return lax.dynamic_update_slice_in_dim(
            jnp.zeros((length,), WIDE), values, place * lanes, 0
        )

    bias_sums = jnp.sum(grad_qkv, axis=0, dtype=WIDE)
    up_column = jnp.sum(grad_pre, axis=0, dtype=WIDE)
    vec_rows = jnp.stack(
        [
            jnp.sum(grad_normed_part * unit_first, axis=0),
            jnp.sum(grad_normed_part, axis=0),
            in_place(bias_sums[:lanes], width),
            in_place(bias_sums[2 * lanes :], width),
            jnp.sum(grad_mid_own, axis=0, dtype=WIDE),
            jnp.sum(grad_normed_mid * unit_mid, axis=0),
            jnp.sum(grad_normed_mid, axis=0),
        ]
        + [jnp.where(place == k, up_column, 0.0) for k in range(RING)]
        + [jnp.sum(cotangent, axis=0, dtype=WIDE)]
    )
    vec_columns = jnp.pad(vec_rows, ((0, VEC_PAD - vec_rows.shape[0]), (0, 0))).T
    out_blocks = grad_out.reshape(lanes, RING, lanes).transpose(1, 0, 2).reshape(width, lanes)
    att_grads = jnp.concatenate([grad_qkv_w, vec_columns, out_blocks], axis=1)
    chips = data // 2
    att_sum = scatter_chips(
        att_grads.reshape(RING, chips, 2 * own, att_columns + lanes), where
    ).reshape(RING // 2, 2, own, att_columns + lanes)
    kept = lax.dynamic_index_in_dim(att_sum, core, 1, keepdims=False)
    given = send(lax.dynamic_index_in_dim(att_sum, 1 - core, 1, keepdims=False), "c", 1)
    att_sum = jnp.concatenate(
        [jnp.where(core == 0, kept, given), jnp.where(core == 0, given, kept)]
    )
    out_sum = att_sum[:, :, att_columns:].transpose(1, 0, 2).reshape(own, width)
    att_sum = att_sum[:, :, :att_columns]

    grad_normed = scatter_z(grad_normed_part)
    input_grad = (
        grad_middle
        + normalise_back(grad_normed, unit_first[:rows], scale_first[:rows], vectors[:, 0])
    ).astype(LOW)

    home = swap_z(jnp.concatenate([att_sum, up_sum], axis=2))
    qkv_sum = (
        home[:, :, : 3 * lanes]
        .reshape(RING, own, 3, lanes)
        .transpose(1, 2, 0, 3)
        .reshape(own, 3 * width)
    )
    vec_sum = jnp.sum(home[:, :, 3 * lanes : 3 * lanes + vec_master.shape[1]], axis=0)
    up_sum = home[:, :, att_columns:].transpose(1, 0, 2).reshape(own, RING * hidden_lanes)

    firsts = (qkv_first, out_first, up_first, down_first)
    seconds = (qkv_second, out_second, up_second, down_second)
    results = [
        adam_step(grad_sum / data, moment, square, weight, DECAY)
        for grad_sum, moment, square, weight in zip(
            (qkv_sum, out_sum, up_sum, down_sum), firsts, seconds, masters
        )
    ]
    squares = jnp.stack(
        [jnp.sum(matrix * matrix) for matrix in masters]
        + [jnp.sum(parts[2] * parts[2]) for parts in results]
    )
    tile = jnp.broadcast_to(squares[:, None], (8, 128))
    totals = jnp.sqrt(sum_everywhere(tile)[:, 0])
    weight_norm = totals[:4]
    update_norm = totals[4:]
    ratio = weight_norm / update_norm
    new_mats = [
        weight - RATE * ratio[k] * parts[2] for k, (weight, parts) in enumerate(zip(masters, results))
    ]
    vec_moment, vec_square, vec_dir = adam_step(
        vec_sum / data, vec_first, vec_second, vec_master, 0.0
    )
    vec_new = vec_master - VEC_RATE * vec_dir
    matrix_norms = jnp.stack([weight_norm, update_norm], axis=1)
    return (
        layer_out,
        input_grad,
        *new_mats,
        *(parts[0] for parts in results),
        *(parts[1] for parts in results),
        vec_new,
        vec_moment,
        vec_square,
        matrix_norms,
    )


def solution(mesh):
    sizes = (4, 4, 2, 4)
    physical = Mesh(mesh.devices.reshape(sizes), EVERY)
    patches = P(EVERY, None)
    shards = P(("z", *DATA), None)
    return jax.shard_map(
        on_device,
        mesh=physical,
        in_specs=(patches, patches, P(DATA, None)) + (shards,) * 15,
        out_specs=(patches, patches) + (shards,) * 15 + (P(),),
        check_vma=False,
    )
```

```python
import jax
import jax.numpy as jnp
from jax import lax
from jax.experimental import pallas as pl
from jax.experimental.pallas import tpu as pltpu
from jax.sharding import Mesh
from jax.sharding import PartitionSpec as P

HEADS = 16
HEAD_DIM = 64
STEP = 4

LN_EPS = 1e-06
BETA = 0.5
ADAM_EPS = 1e-06
DECAY = 0.01
RATE = 0.5
VEC_RATE = 0.2

LOW = jnp.bfloat16
WIDE = jnp.float32
DATA = ("x", "y", "c")
EVERY = ("x", "y", "c", "z")
RING = 4
LANES = 128
VECS = 16
SUBLANES = 8
SCORE_SCALE = HEAD_DIM ** (-0.5)
MIB = 1 << 20


def send(block, axis, step):
    size = lax.axis_size(axis)
    return lax.ppermute(block, axis, [(i, (i + step) % size) for i in range(size)])


def together(*values):
    return lax.optimization_barrier(values)


class Gather:
    def __init__(self, low, high):
        self.own = [low, high]
        self.near = [send(low, "z", 1), send(high, "z", -1)]
        self.crossed = [send(high, "z", 1), send(low, "z", -1)]

    def relay(self):
        prev_low, next_high = self.near
        self.far = [send(prev_low, "z", 1), send(next_high, "z", -1)]

    def blocks(self):
        prev_low, next_high = self.near
        prev_high, next_low = self.crossed
        return [*self.own, next_low, next_high, *self.far, prev_low, prev_high]


def scatter_direct(own, *gone):
    return [own] + [send(gone[k - 1], "z", k) for k in range(1, RING)]


def scatter_z(pieces, meanwhile):
    own, after_low, before_high, right, left = pieces
    from_prev, from_next, meanwhile = together(send(right, "z", 1), send(left, "z", -1), meanwhile)
    half = after_low.shape[0]
    prev_low = send((after_low + from_prev[:half].astype(WIDE)).astype(LOW), "z", 1)
    next_high = send((before_high + from_next[:half].astype(WIDE)).astype(LOW), "z", -1)
    return [own, from_prev, from_next, prev_low, next_high], meanwhile


def send_split(block, phase, step):
    sizes = [lax.axis_size(axis) for axis in DATA]
    pairs = []
    for x in range(sizes[0]):
        for y in range(sizes[1]):
            for c in range(sizes[2]):
                if c == phase:
                    to = ((x + step) % sizes[0], y)
                else:
                    to = (x, (y + step) % sizes[1])
                pairs.append(
                    ((x * sizes[1] + y) * sizes[2] + c, (to[0] * sizes[1] + to[1]) * sizes[2] + c)
                )
    return lax.ppermute(block, DATA, pairs)


def dot(left, right, dims):
    return lax.dot_general(left, right, (dims, ((), ())), preferred_element_type=WIDE)


NN = ((1,), (0,))
NT = ((1,), (1,))
TN = ((0,), (0,))


def shape_of(shape, dtype):
    return jax.ShapeDtypeStruct(shape, dtype)


def whole_call(kernel, out_shape, scalars, arrays, scratch=(), limit=40):
    in_specs = [pl.BlockSpec(memory_space=pltpu.SMEM)] * (scalars is not None)
    operands = ([scalars] if scalars is not None else []) + list(arrays)
    many = isinstance(out_shape, list)
    vmem = pl.BlockSpec(memory_space=pltpu.VMEM)
    return pl.pallas_call(
        kernel,
        out_shape=out_shape,
        in_specs=in_specs + [vmem] * len(arrays),
        out_specs=[vmem] * len(out_shape) if many else vmem,
        scratch_shapes=list(scratch),
        compiler_params=pltpu.CompilerParams(vmem_limit_bytes=limit * MIB),
    )(*operands)


def pick_kernel(where, qkv, up, vec, *outs):
    lanes, wide = qkv.shape[1] // (3 * RING), up.shape[1] // RING
    for step in range(RING):
        place = (where[3] + step) % RING
        for third in range(3):
            at = pl.multiple_of(third * lanes * RING + place * lanes, lanes)
            outs[step][:, third * lanes : (third + 1) * lanes] = qkv[:, pl.ds(at, lanes)]
        outs[step][:, 3 * lanes : 3 * lanes + LANES] = jnp.zeros((qkv.shape[0], LANES), WIDE)
        outs[step][:, 3 * lanes : 3 * lanes + vec.shape[1]] = vec[...]
        outs[step][:, 3 * lanes + LANES :] = up[:, pl.ds(pl.multiple_of(place * wide, wide), wide)]


def collect_kernel(where, own, first, second, third, out, keep, give, hold):
    core, place = where[2], where[3]
    columns = own.shape[1]
    for step, piece in enumerate((own, first, second, third)):
        hold[(place + step) % RING] = piece[...]
    lanes = out.shape[1] // RING
    for half in range(2):
        for target, side in ((keep, core), (give, 1 - core)):
            at = side * 2 + half
            target[half, :, :columns] = hold[at]
            target[half, :, columns:] = out[:, pl.ds(pl.multiple_of(at * lanes, lanes), lanes)]


def pair_kernel(where, mine, theirs, down, att, ffn):
    first = where[2] == 0
    wide = ffn.shape[2]
    narrow = 3 * (att.shape[2] - LANES) // 4 + LANES
    for half in range(2):
        low = jnp.where(first, mine[half], theirs[half])
        high = jnp.where(first, theirs[half], mine[half])
        block = jnp.concatenate([low, high], axis=0).astype(LOW)
        att[half, :, :narrow] = block[:, :narrow]
        att[half, :, narrow:] = block[:, narrow + wide :]
        ffn[half] = block[:, narrow : narrow + wide]
        rows = ffn.shape[1]
        ffn[2 + half] = down[half * rows : (half + 1) * rows].astype(LOW)


def chip_of(where, first, second):
    x, y, c = where[0], where[1], where[2]
    along_x = (x + jnp.where(c == 0, first, second)) % RING
    along_y = (y + jnp.where(c == 0, second, first)) % RING
    return along_x * RING + along_y


def place_kernel(where, *refs):
    out = refs[-1]
    for second in range(RING):
        for first in range(RING):
            out[:, chip_of(where, first, second)] = refs[second][first]


def weights_kernel(where, mine, theirs, qkv, out, vecs):
    first = where[2] == 0
    rows, columns = mine.shape
    lanes = out.shape[0]
    for half in range(2):
        block = (
            jnp.where(first, mine[...], theirs[...])
            if half == 0
            else jnp.where(first, theirs[...], mine[...])
        )
        qkv[half * rows : (half + 1) * rows] = block[:, : 3 * lanes]
        vec = block[:, 3 * lanes : 3 * lanes + LANES].astype(WIDE)
        vecs[:, half * rows : (half + 1) * rows] = vec.T[:VECS]
        for part in range(2):
            at = (2 * half + part) * lanes
            out[:, at : at + lanes] = block[part * lanes : (part + 1) * lanes, columns - lanes :]


def ffn_weights_kernel(where, mine, theirs, up, down):
    first = where[2] == 0
    for half in range(2):
        up[half] = jnp.where(first, mine[half], theirs[half])
        up[2 + half] = jnp.where(first, theirs[half], mine[half])
        down[:, half] = jnp.where(first, mine[2 + half], theirs[2 + half])
        down[:, 2 + half] = jnp.where(first, theirs[2 + half], mine[2 + half])


def along_ring(block, phase):
    return [block] + [send_split(block, phase, -k) for k in range(1, RING)]


def by_chip(where, blocks):
    parts, rows, columns = blocks[0].shape[1:]
    return whole_call(
        place_kernel,
        shape_of((parts, RING * RING, rows, columns), LOW),
        where,
        blocks,
        limit=6,
    )


def weight_pieces(where, qkv_master, up_master, vec_master):
    columns = 3 * (qkv_master.shape[1] // (3 * RING)) + LANES + up_master.shape[1] // RING
    pieces = whole_call(
        pick_kernel,
        [shape_of((qkv_master.shape[0], columns), WIDE)] * RING,
        where,
        [qkv_master, up_master, vec_master],
        limit=4,
    )
    return [pieces[0]] + [send(pieces[RING - k], "z", RING - k) for k in range(1, RING)]


def weight_blocks(where, arrived, out_master, down_master):
    own, columns = arrived[0].shape
    lanes = out_master.shape[1] // RING
    wide = columns - 3 * lanes - LANES
    half = shape_of((2, own, columns + lanes), WIDE)
    keep, give = whole_call(
        collect_kernel,
        [half, half],
        where,
        [*arrived, out_master],
        [pltpu.VMEM((RING, own, columns), WIDE)],
        limit=4,
    )
    return whole_call(
        pair_kernel,
        [
            shape_of((2, 2 * own, 4 * lanes + LANES), LOW),
            shape_of((4, 2 * own, wide), LOW),
        ],
        where,
        [keep, send(give, "c", 1), down_master],
        limit=4,
    )


def attention_weights(where, mine, theirs):
    halves, chips, rows, columns = mine.shape
    lanes = (columns - LANES) // 4
    flat = (halves * chips * rows, columns)
    return whole_call(
        weights_kernel,
        [
            shape_of((2 * flat[0], 3 * lanes), LOW),
            shape_of((lanes, RING * lanes), LOW),
            shape_of((VECS, RING * lanes), WIDE),
        ],
        where,
        [mine.reshape(flat), theirs.reshape(flat)],
        limit=10,
    )


def ffn_weights(where, mine, theirs):
    parts, chips, rows, columns = mine.shape
    up, down = whole_call(
        ffn_weights_kernel,
        [shape_of((parts, chips, rows, columns), LOW), shape_of((chips, parts, rows, columns), LOW)],
        where,
        [mine, theirs],
        limit=12,
    )
    flat = (parts * chips * rows, columns)
    return up.reshape(flat), down.reshape(flat)


def sum_kernel(own, first, second, third, out, *gone):
    for k in range(RING):
        total = own[k]
        for part in (first, second, third):
            total = total + part[k].astype(WIDE)
        if k == 0:
            out[...] = total
        else:
            gone[k - 1][...] = total.astype(LOW)


def split_kernel(where, own, first, second, third, kept, given):
    total = own[...]
    for part in (first, second, third):
        total = total + part[...].astype(WIDE)
    rows = kept.shape[-2]
    low, high = total[..., :rows, :], total[..., rows:, :]
    kept[...] = jnp.where(where[2] == 0, low, high)
    given[...] = jnp.where(where[2] == 0, high, low)


def back_along_ring(own, gone, phase):
    return [own] + [send_split(gone[k - 1], phase, k) for k in range(1, RING)]


def ring_sum(arrived):
    shape = arrived[0].shape[1:]
    return whole_call(
        sum_kernel, [shape_of(shape, WIDE)] + [shape_of(shape, LOW)] * 3, None, arrived, limit=18
    )


def core_sum(where, arrived):
    shape = arrived[0].shape
    half = shape_of((*shape[:-2], shape[-2] // 2, shape[-1]), WIDE)
    return whole_call(split_kernel, [half, half], where, arrived, limit=12)


def normalise(values):
    centre = jnp.mean(values, -1, keepdims=True)
    centred = values - centre
    spread = jnp.mean(centred * centred, -1, keepdims=True)
    scale = lax.rsqrt(spread + LN_EPS)
    return centred * scale, scale


def normalise_back(grad, unit, scale, gain):
    grad_unit = grad * gain
    return scale * (
        grad_unit
        - jnp.mean(grad_unit, -1, keepdims=True)
        - unit * jnp.mean(grad_unit * unit, -1, keepdims=True)
    )


def images_kernel(counts, one, penalty):
    row = lax.broadcasted_iota(jnp.int32, one.shape, 0)
    lane = lax.broadcasted_iota(jnp.int32, one.shape, 1) % HEAD_DIM
    first_end = counts[0, 0]
    second_end = first_end + counts[0, 1]
    image = (row >= first_end).astype(jnp.int32) + (row >= second_end).astype(jnp.int32)
    one[...] = jnp.where(lane == image, 1.0, 0.0).astype(LOW)
    penalty[...] = jnp.where((lane == image) | (lane >= 3), 0.0, -1e30).astype(LOW)


def both(blocks, step):
    return jnp.concatenate([blocks[2 * step][...], blocks[2 * step + 1][...]])


def first_kernel(where, vecs, weight, *refs):
    blocks, (normed, qkv) = refs[:8], refs[8:]
    rows = 2 * blocks[0].shape[0]
    lanes = weight.shape[1] // 3
    at = pl.ds(pl.multiple_of(where[3] * lanes, lanes), lanes)
    bias = jnp.concatenate([vecs[2:3, at], jnp.zeros((1, lanes), WIDE), vecs[3:4, at]], axis=1)
    for step in range(RING):
        here = rows_of(where, step, rows)
        unit, _ = normalise(both(blocks, step).astype(WIDE))
        block = (unit * vecs[0:1] + vecs[1:2]).astype(LOW)
        normed[here] = block
        qkv[here] = (dot(block, weight[...], NN) + bias).astype(LOW)


def scores_of(query, key, one, penalty, mine):
    return dot(jnp.where(mine, query, one), jnp.where(mine, key, penalty), NT)


def attend_kernel(query, key, value, one, penalty, attended, log_total):
    rows, block = query.shape[0], query.shape[0] // 4
    lane = lax.broadcasted_iota(jnp.int32, (1, LANES), 1)
    for place in range(4):
        at = pl.ds(place * block, block)
        parts, logs = [], []
        for head in range(2):
            mine = lane // HEAD_DIM == head
            scores = scores_of(
                query[at] * LOW(SCORE_SCALE), key[...], one[at], penalty[...], mine
            )
            top = jnp.max(scores, -1, keepdims=True)
            exponent = jnp.exp(scores - top)
            total = jnp.sum(exponent, -1, keepdims=True)
            parts.append(dot((exponent * (1.0 / total)).astype(LOW), value[...], NN))
            logs.append(top + jnp.log(total))
        attended[at] = jnp.where(lane < HEAD_DIM, parts[0], parts[1]).astype(LOW)
        log_total[at] = jnp.where(lane < HEAD_DIM, logs[0], logs[1])


def attend(qkv, one, penalty):
    rows, lanes = qkv.shape[0], qkv.shape[1] // 3
    pairs = lanes // LANES

    def third(k):
        return pl.BlockSpec((rows, LANES), lambda j: (0, k * pairs + j))

    fixed = pl.BlockSpec((rows, LANES), lambda j: (0, 0))
    return pl.pallas_call(
        attend_kernel,
        grid=(pairs,),
        in_specs=[third(0), third(1), third(2), fixed, fixed],
        out_specs=[third(0), third(0)],
        out_shape=[shape_of((rows, lanes), LOW), shape_of((rows, lanes), WIDE)],
        compiler_params=pltpu.CompilerParams(vmem_limit_bytes=10 * MIB),
    )(qkv, qkv, qkv, one, penalty)


def attend_back_kernel(
    query, key, value, grad, log_total, one, penalty, grad_query, grad_key, grad_value, key_sum, value_sum
):
    rows, block = query.shape[0], query.shape[0] // 4
    lane = lax.broadcasted_iota(jnp.int32, (1, LANES), 1)
    for place in range(4):
        at = pl.ds(place * block, block)
        parts = []
        for head in range(2):
            mine = lane // HEAD_DIM == head
            scaled = query[at] * LOW(SCORE_SCALE)
            scores = scores_of(scaled, key[...], one[at], penalty[...], mine)
            probs = jnp.exp(scores - log_total[at, head * HEAD_DIM : head * HEAD_DIM + 1])
            grad_probs = dot(jnp.where(mine, grad[at], LOW(0.0)), value[...], NT)
            inner = jnp.sum(probs * grad_probs, -1, keepdims=True)
            grad_scores = (probs * (grad_probs - inner)).astype(LOW)
            parts.append(dot(grad_scores, key[...], NN))
            for_value = dot(probs.astype(LOW), grad[at], TN)
            for_key = dot(grad_scores, scaled, TN)
            if place == 0:
                key_sum[head] = for_key
                value_sum[head] = for_value
            else:
                key_sum[head] += for_key
                value_sum[head] += for_value
        grad_query[at] = (jnp.where(lane < HEAD_DIM, parts[0], parts[1]) * SCORE_SCALE).astype(LOW)
    grad_key[...] = jnp.where(lane < HEAD_DIM, key_sum[0], key_sum[1]).astype(LOW)
    grad_value[...] = jnp.where(lane < HEAD_DIM, value_sum[0], value_sum[1]).astype(LOW)


def attend_back(qkv, grad, log_total, one, penalty):
    rows, lanes = qkv.shape[0], qkv.shape[1] // 3
    pairs = lanes // LANES

    def third(k):
        return pl.BlockSpec((rows, LANES), lambda j: (0, k * pairs + j))

    fixed = pl.BlockSpec((rows, LANES), lambda j: (0, 0))
    return pl.pallas_call(
        attend_back_kernel,
        grid=(pairs,),
        in_specs=[third(0), third(1), third(2), third(0), third(0), fixed, fixed],
        out_specs=[third(0)] * 3,
        out_shape=[shape_of((rows, lanes), LOW)] * 3,
        scratch_shapes=[pltpu.VMEM((2, rows, LANES), WIDE)] * 2,
        compiler_params=pltpu.CompilerParams(vmem_limit_bytes=14 * MIB),
    )(qkv, qkv, qkv, grad, log_total, one, penalty)


def piece_shapes(rows, columns):
    wide, low = shape_of((rows // 2, columns), WIDE), shape_of((rows, columns), LOW)
    return [shape_of((rows, columns), WIDE), wide, wide, low, low]


def store_pieces(block, step, pieces):
    own, after_low, before_high, right, left = pieces
    half = block.shape[0] // 2
    low, high = block[:half], block[half:]
    if step == 0:
        own[...] = block
    elif step == 1:
        after_low[...] = low
        right[half:] = high.astype(LOW)
    elif step == 2:
        right[:half] = low.astype(LOW)
        left[:half] = high.astype(LOW)
    else:
        before_high[...] = high
        left[half:] = low.astype(LOW)


def rows_of(where, step, rows):
    return pl.ds(pl.multiple_of((where[3] + step) % RING * rows, rows), rows)


def project_kernel(where, left, right, *pieces):
    rows = left.shape[0] // RING
    for step in range(RING):
        store_pieces(dot(left[rows_of(where, step, rows)], right[...], NN), step, pieces)


def project_direct_kernel(left, right, own, *gone):
    rows = left.shape[0] // RING
    for step in range(RING):
        block = dot(left[step * rows : (step + 1) * rows], right[...], NN)
        if step == 0:
            own[...] = block
        else:
            gone[step - 1][...] = block.astype(LOW)


def project(where, left, right):
    return whole_call(
        project_kernel,
        piece_shapes(left.shape[0] // RING, right.shape[1]),
        where,
        [left, right],
        limit=8,
    )


def arrived_sum(own, from_prev, from_next, prev_low, next_high):
    half = prev_low.shape[0]
    low = prev_low[...].astype(WIDE) + from_next[half:].astype(WIDE)
    high = from_prev[half:].astype(WIDE) + next_high[...].astype(WIDE)
    return own[...] + jnp.concatenate([low, high])


def middle_kernel(tokens, vecs, *refs):
    arrivals, (middle, low, high) = refs[:5], refs[5:]
    half = low.shape[0]
    middle[...] = tokens[...].astype(WIDE) + (arrived_sum(*arrivals) + vecs[4:5])
    unit, _ = normalise(middle[...])
    normed = (unit * vecs[5:6] + vecs[6:7]).astype(LOW)
    low[...] = normed[:half]
    high[...] = normed[half:]


def hidden_kernel(where, vecs, up, down, *refs):
    cotangents, pieces, (normed, hidden, grad_pre, column, *gone) = refs[:8], refs[8:16], refs[16:]
    rows = 2 * cotangents[0].shape[0]
    bias = vecs[pl.ds(7 + where[3], 1)]
    for step in range(RING):
        at = pl.ds(step * rows, rows)
        block = both(pieces, step)
        normed[at] = block
        pre_act = dot(block, up[...], NN) + bias
        below = 0.5 * (1.0 + lax.erf(pre_act * (0.5**0.5)))
        hidden[at] = (pre_act * below).astype(LOW)
        slope = below + pre_act * (jnp.exp(-0.5 * pre_act * pre_act) * 0.3989422804014327)
        grad = (dot(both(cotangents, step), down[...], NT) * slope).astype(LOW)
        grad_pre[at] = grad
        total = jnp.sum(grad.astype(WIDE), 0, keepdims=True)
        if step == 0:
            column[...] = total
        else:
            column[...] += total
        store_pieces(dot(grad, up[...], NT), step, gone)


def arrange(where, hold, own, gone, part=None):
    for second in range(RING):
        for first in range(RING):
            piece = hold[chip_of(where, first, second)]
            target, piece = (own, piece) if first == 0 else (gone[first - 1], piece.astype(LOW))
            if part is None:
                target[second] = piece
            else:
                target[second, part] = piece


def ffn_grads_kernel(where, normed, hidden, grad_pre, *refs):
    cotangents, own, gone, hold = refs[:8], refs[8], refs[9:12], refs[12]
    width = normed.shape[1]
    part = width // RING
    chips, chip_rows, _ = hold.shape
    cot = jnp.concatenate([block[...] for block in cotangents])
    for k in range(RING):
        here = slice(k * part, (k + 1) * part)
        block = dot(normed[:, here], grad_pre[...], TN)
        hold[:, :, k * width : (k + 1) * width] = block.reshape(chips, chip_rows, width)
        block = dot(hidden[:, here], cot, TN).reshape(-1, RING, SUBLANES, width)
        quarter = chips // RING
        for q in range(RING):
            hold[k * quarter : (k + 1) * quarter, :, (RING + q) * width : (RING + q + 1) * width] = (
                block[:, q].reshape(quarter, chip_rows, width)
            )
    arrange(where, hold, own, gone)


def grad_middle_kernel(middle, cotangent, vecs, *refs):
    arrivals, (grad_middle, low, high, sums) = refs[:5], refs[5:]
    half = low.shape[0]
    grad = arrived_sum(*arrivals)
    unit, scale = normalise(middle[...])
    cot = cotangent[...].astype(WIDE)
    total = cot + normalise_back(grad, unit, scale, vecs[5:6])
    grad_middle[...] = total
    rounded = total.astype(LOW)
    low[...] = rounded[:half]
    high[...] = rounded[half:]
    sums[...] = jnp.concatenate(
        [
            jnp.sum(rounded.astype(WIDE), 0, keepdims=True),
            jnp.sum(grad * unit, 0, keepdims=True),
            jnp.sum(grad, 0, keepdims=True),
            jnp.sum(cot, 0, keepdims=True),
            jnp.zeros((4, cot.shape[1]), WIDE),
        ]
    )


def grad_att_kernel(where, attended, out, *refs):
    pieces, (grad_att, grad_out) = refs[:8], refs[8:]
    rows = 2 * pieces[0].shape[0]
    for step in range(RING):
        at = rows_of(where, step, rows)
        block = both(pieces, step)
        grad_att[at] = dot(block, out[...], NT).astype(LOW)
        part = dot(attended[at], block, TN)
        if step == 0:
            grad_out[...] = part
        else:
            grad_out[...] += part


def back_product_kernel(where, weight, grad_query, grad_key, grad_value, *refs):
    blocks, own, gone, sums = refs[:8], refs[8], refs[9:12], refs[12]
    lanes = grad_query.shape[1]
    rows = own.shape[0]
    for step in range(RING):
        here = rows_of(where, step, rows)
        block = dot(grad_query[here], weight[:, :lanes], NT)
        block += dot(grad_key[here], weight[:, lanes : 2 * lanes], NT)
        block += dot(grad_value[here], weight[:, 2 * lanes :], NT)
        if step == 0:
            own[...] = block
        else:
            gone[step - 1][...] = block.astype(LOW)
        unit, _ = normalise(both(blocks, step).astype(WIDE))
        pair = jnp.concatenate(
            [
                jnp.sum(block * unit, 0, keepdims=True),
                jnp.sum(block, 0, keepdims=True),
                jnp.zeros((6, block.shape[1]), WIDE),
            ]
        )
        if step == 0:
            sums[...] = pair
        else:
            sums[...] += pair


def grads_kernel(
    where, normed, grad_query, grad_key, grad_value, grad_out, first_sums, sums, column, own, *rest
):
    gone, vecs, hold = rest[:3], rest[3], rest[4]
    lanes = grad_query.shape[1]
    thirds = (grad_query, grad_key, grad_value)
    vecs[...] = jnp.zeros(vecs.shape, WIDE)
    at = pl.ds(pl.multiple_of(where[3] * lanes, lanes), lanes)
    vecs[0:2] = first_sums[0:2]
    vecs[2:3, at] = jnp.sum(grad_query[...].astype(WIDE), 0, keepdims=True)
    vecs[3:4, at] = jnp.sum(grad_value[...].astype(WIDE), 0, keepdims=True)
    vecs[4:7] = sums[0:3]
    for k in range(RING):
        vecs[7 + k : 8 + k] = jnp.where(where[3] == k, column[...], 0.0)
    vecs[11:12] = sums[3:4]
    for part in range(RING):
        here = slice(part * lanes, (part + 1) * lanes)
        left = normed[:, here]
        block = jnp.concatenate(
            [dot(left, third[...], TN) for third in thirds]
            + [vecs[:, here].T, grad_out[:, here]],
            axis=1,
        )
        hold[...] = block.reshape(hold.shape)
        arrange(where, hold, own, gone, part)


def input_kernel(tokens, grad_middle, vecs, own, prev, far, following, out):
    unit, scale = normalise(tokens[...].astype(WIDE))
    grad = own[...] + (prev[...].astype(WIDE) + far[...].astype(WIDE) + following[...].astype(WIDE))
    out[...] = (grad_middle[...] + normalise_back(grad, unit, scale, vecs[0:1])).astype(LOW)


def layer_kernel(middle, vecs, own, prev, far, following, out):
    total = own[...] + (prev[...].astype(WIDE) + far[...].astype(WIDE) + following[...].astype(WIDE))
    out[...] = (middle[...] + (total + vecs[11:12])).astype(LOW)


def home_kernel(where, att, att_other, ffn, ffn_other, *outs):
    pieces, (out_sum, down_sum, hold) = outs[:RING], outs[RING:]
    own, columns = att.shape[1:]
    lanes = (columns - LANES) // 4
    narrow = columns - lanes
    wide = ffn.shape[1] // (2 * RING)
    sums = att[...] + att_other[...]
    for part in range(RING):
        hold[part, :, :narrow] = sums[part, :, :narrow]
        at = pl.ds(part * wide, wide)
        hold[part, :, narrow:] = ffn[:, at] + ffn_other[:, at]
        at = pl.ds((RING + part) * wide, wide)
        down_sum[part * own : (part + 1) * own] = ffn[:, at] + ffn_other[:, at]
        out_sum[:, part * lanes : (part + 1) * lanes] = sums[part, :, narrow:]
    for step in range(RING):
        pieces[step][...] = hold[(where[3] + step) % RING]


def adam_step(grad_mean, moment, square, weight, decay_rate):
    moment_new = BETA * moment + (1.0 - BETA) * grad_mean
    square_new = BETA * square + (1.0 - BETA) * grad_mean * grad_mean
    correct = 1.0 - BETA**STEP
    direction = (
        moment_new / correct / (jnp.sqrt(square_new / correct) + ADAM_EPS) + decay_rate * weight
    )
    return (moment_new, square_new, direction)


def adam_kernel(where, out_sum, down_sum, *refs):
    home, refs = refs[:RING], refs[RING:]
    weights, moments, squares = refs[0:5], refs[5:10], refs[10:15]
    moments_new, squares_new, directions = refs[15:20], refs[20:25], refs[25:29]
    vec_new, row, qkv_sum, up_sum = refs[29:33]
    lanes, wide = out_sum.shape[1] // RING, up_sum.shape[1] // RING
    for step in range(RING):
        place = (where[3] + step) % RING
        for third in range(3):
            at = pl.multiple_of(third * lanes * RING + place * lanes, lanes)
            qkv_sum[:, pl.ds(at, lanes)] = home[step][:, third * lanes : (third + 1) * lanes]
        up_sum[:, pl.ds(pl.multiple_of(place * wide, wide), wide)] = home[step][:, 3 * lanes + LANES :]
    columns = weights[4].shape[1]
    vec_sum = sum(home[step][:, 3 * lanes : 3 * lanes + LANES] for step in range(RING))
    lane = lax.broadcasted_iota(jnp.int32, (1, LANES), 1)
    totals = jnp.zeros((1, LANES), WIDE)
    sums = (qkv_sum[...], out_sum[...], up_sum[...], down_sum[...], vec_sum[:, :columns])
    groups = 32.0
    for k in range(5):
        weight = weights[k][...]
        moment, square, direction = adam_step(
            sums[k] / groups, moments[k][...], squares[k][...], weight, DECAY if k < 4 else 0.0
        )
        moments_new[k][...] = moment
        squares_new[k][...] = square
        if k < 4:
            directions[k][...] = direction
            totals = totals + jnp.where(lane == k, jnp.sum(weight * weight), 0.0)
            totals = totals + jnp.where(lane == 4 + k, jnp.sum(direction * direction), 0.0)
        else:
            vec_new[...] = weight - VEC_RATE * direction
    row[...] = totals


def update_kernel(copies, *refs):
    weights, directions, news, norms = refs[0:4], refs[4:8], refs[8:12], refs[12]
    root = jnp.sqrt(jnp.sum(copies[...], 0, keepdims=True))
    for k in range(4):
        weight_norm, update_norm = root[:, k : k + 1], root[:, 4 + k : 5 + k]
        norms[k : k + 1, 0:1] = weight_norm
        norms[k : k + 1, 1:2] = update_norm
        news[k][...] = weights[k][...] - RATE * (weight_norm / update_norm) * directions[k][...]


def on_device(
    tokens,
    cotangent,
    seg_counts,
    qkv_master,
    out_master,
    up_master,
    down_master,
    qkv_first,
    out_first,
    up_first,
    down_first,
    qkv_second,
    out_second,
    up_second,
    down_second,
    vec_master,
    vec_first,
    vec_second,
):
    where = jnp.stack([lax.axis_index(axis) for axis in EVERY]).astype(jnp.int32)
    rows, width = tokens.shape
    own = qkv_master.shape[0]
    lanes = width // RING
    hidden_lanes = up_master.shape[1] // RING
    chips = lax.axis_size("x") * lax.axis_size("y")
    group = rows * RING
    half = rows // 2
    wide_rows, half_rows = shape_of((rows, width), WIDE), shape_of((half, width), LOW)
    low_rows, group_low = shape_of((rows, width), LOW), shape_of((group, width), LOW)

    token_rows = Gather(tokens[:half], tokens[half:])
    arrived = weight_pieces(where, qkv_master, up_master, vec_master)
    arrived, token_rows.near = together(arrived, token_rows.near)
    token_rows.relay()
    att_block, ffn_block = weight_blocks(where, arrived, out_master, down_master)
    att_ring = along_ring(att_block, 0)
    att_ring, token_rows.crossed = together(att_ring, token_rows.crossed)
    att_ring = along_ring(jnp.stack(att_ring), 1)
    att_ring, token_rows.far = together(att_ring, token_rows.far)
    att_mine = by_chip(where, att_ring)
    token_blocks = token_rows.blocks()
    ffn_block, cot, att_mine = together(ffn_block, cotangent, att_mine)
    cot_rows = Gather(cot[:half], cot[half:])
    ffn_ring = along_ring(ffn_block, 0)
    w_qkv, w_out, vecs = attention_weights(where, att_mine, send(att_mine, "c", 1))
    one, penalty = whole_call(
        images_kernel, [shape_of((group, LANES), LOW)] * 2, seg_counts, [], limit=8
    )

    normed, qkv = whole_call(
        first_kernel,
        [group_low, shape_of((group, 3 * lanes), LOW)],
        where,
        [vecs, w_qkv, *token_blocks],
        limit=10,
    )
    qkv, one, penalty, ffn_ring, cot_rows.near = together(
        qkv, one, penalty, ffn_ring, cot_rows.near
    )
    cot_rows.relay()
    ffn_ring = along_ring(jnp.stack(ffn_ring), 1)
    attended, log_total = attend(qkv, one, penalty)
    attended, cot_rows.far, cot_rows.crossed = together(
        attended, cot_rows.far, cot_rows.crossed
    )
    cot_blocks = cot_rows.blocks()
    arrivals, ffn_ring = scatter_z(project(where, attended, w_out), ffn_ring)
    ffn_mine = by_chip(where, ffn_ring)
    ffn_theirs = send(ffn_mine, "c", 1)
    middle, *mid_halves = whole_call(
        middle_kernel,
        [wide_rows, half_rows, half_rows],
        None,
        [tokens, vecs, *arrivals],
        limit=6,
    )

    mid_rows = Gather(*mid_halves)
    w_up, w_down = ffn_weights(where, ffn_mine, ffn_theirs)
    w_up, w_down, mid_rows.near = together(w_up, w_down, mid_rows.near)
    mid_rows.relay()
    normed_mid, hidden, grad_pre, up_column, *gone = whole_call(
        hidden_kernel,
        [group_low, group_low, group_low, shape_of((1, hidden_lanes), WIDE)]
        + piece_shapes(rows, width),
        where,
        [vecs, w_up, w_down, *cot_blocks, *mid_rows.blocks()],
        limit=20,
    )
    ffn_piece = (RING, 2 * own, 2 * RING * width)
    ffn_grads = whole_call(
        ffn_grads_kernel,
        [shape_of(ffn_piece, WIDE)] + [shape_of(ffn_piece, LOW)] * 3,
        where,
        [normed_mid, hidden, grad_pre, *cot_blocks],
        [pltpu.VMEM((chips, *ffn_piece[1:]), WIDE)],
        limit=30,
    )
    arrivals, ffn_grads = scatter_z(gone, ffn_grads)
    grad_middle, *grad_halves, mid_sums = whole_call(
        grad_middle_kernel,
        [wide_rows, half_rows, half_rows, shape_of((8, width), WIDE)],
        None,
        [middle, cotangent, vecs, *arrivals],
        limit=8,
    )
    grad_rows = Gather(*grad_halves)
    grad_rows.relay()
    ffn_own, *ffn_gone = ffn_grads
    ffn_arrived = back_along_ring(ffn_own, ffn_gone, 0)

    out_pieces = whole_call(
        project_direct_kernel, [wide_rows] + [low_rows] * 3, None, [hidden, w_down], limit=10
    )
    grad_rows.far, out_pieces = together(grad_rows.far, out_pieces)
    grad_att, grad_out = whole_call(
        grad_att_kernel,
        [shape_of((group, lanes), LOW), shape_of((lanes, width), WIDE)],
        where,
        [attended, w_out, *grad_rows.blocks()],
        limit=10,
    )
    out_arrived = scatter_direct(*out_pieces)
    grad_qkv = attend_back(qkv, grad_att, log_total, one, penalty)
    grad_qkv, out_arrived, ffn_arrived = together(grad_qkv, out_arrived, ffn_arrived)
    *normed_pieces, first_sums = whole_call(
        back_product_kernel,
        [wide_rows] + [low_rows] * 3 + [shape_of((8, width), WIDE)],
        where,
        [w_qkv, *grad_qkv, *token_blocks],
        limit=14,
    )
    normed_arrived = scatter_direct(*normed_pieces)
    columns = 4 * lanes + LANES
    piece = (RING, RING, 2 * own, columns)
    att_own, *att_gone = whole_call(
        grads_kernel,
        [shape_of(piece, WIDE)] + [shape_of(piece, LOW)] * 3,
        where,
        [normed, *grad_qkv, grad_out, first_sums, mid_sums, up_column],
        [pltpu.VMEM((LANES, width), WIDE), pltpu.VMEM((chips, 2 * own, columns), WIDE)],
        limit=18,
    )

    att_arrived = back_along_ring(att_own, att_gone, 0)
    ffn_own, *ffn_gone = ring_sum(ffn_arrived)
    layer_out = whole_call(layer_kernel, low_rows, None, [middle, vecs, *out_arrived], limit=8)
    att_arrived, ffn_own, ffn_gone, layer_out = together(att_arrived, ffn_own, ffn_gone, layer_out)
    att_own, *att_gone = ring_sum(att_arrived)
    att_arrived = back_along_ring(att_own, att_gone, 1)
    ffn_arrived = back_along_ring(ffn_own, ffn_gone, 1)
    input_grad = whole_call(
        input_kernel, low_rows, None, [tokens, grad_middle, vecs, *normed_arrived], limit=8
    )
    att_arrived, ffn_arrived, input_grad = together(att_arrived, ffn_arrived, input_grad)
    att_kept, att_given = core_sum(where, att_arrived)
    ffn_kept, ffn_given = core_sum(where, ffn_arrived)
    home_piece = shape_of((own, 3 * lanes + LANES + hidden_lanes), WIDE)
    *pieces, out_sum, down_sum = whole_call(
        home_kernel,
        [home_piece] * RING + [shape_of((own, width), WIDE), shape_of((RING * own, width), WIDE)],
        where,
        [att_kept, send(att_given, "c", 1), ffn_kept, send(ffn_given, "c", 1)],
        [pltpu.VMEM((RING, *home_piece.shape), WIDE)],
        limit=6,
    )
    home = [pieces[0]] + [send(pieces[RING - k], "z", RING - k) for k in range(1, RING)]
    weights = [qkv_master, out_master, up_master, down_master, vec_master]
    kinds = [shape_of(weight.shape, WIDE) for weight in weights]
    state = whole_call(
        adam_kernel,
        kinds + kinds + kinds[:4] + [kinds[4], shape_of((1, LANES), WIDE)],
        where,
        [out_sum, down_sum, *home, *weights]
        + [qkv_first, out_first, up_first, down_first, vec_first]
        + [qkv_second, out_second, up_second, down_second, vec_second],
        [pltpu.VMEM(qkv_master.shape, WIDE), pltpu.VMEM(up_master.shape, WIDE)],
        limit=10,
    )
    firsts, seconds, directions, vec_new, row = (
        state[:5],
        state[5:10],
        state[10:14],
        state[14],
        state[15],
    )
    devices = 2 * chips * RING
    copies = lax.all_to_all(jnp.broadcast_to(row, (devices, LANES)), EVERY, 0, 0, tiled=True)
    *new_mats, matrix_norms = whole_call(
        update_kernel,
        kinds[:4] + [shape_of((4, 2), WIDE)],
        None,
        [copies, *weights[:4], *directions],
        limit=8,
    )
    return (
        layer_out,
        input_grad,
        *new_mats,
        *firsts[:4],
        *seconds[:4],
        vec_new,
        firsts[4],
        seconds[4],
        matrix_norms,
    )


def solution(mesh):
    sizes = (4, 4, 2, 4)
    physical = Mesh(mesh.devices.reshape(sizes), EVERY)
    patches = P(EVERY, None)
    shards = P(("z", *DATA), None)
    return jax.shard_map(
        on_device,
        mesh=physical,
        in_specs=(patches, patches, P(DATA, None)) + (shards,) * 15,
        out_specs=(patches, patches) + (shards,) * 15 + (P(),),
        check_vma=False,
    )
```

```python
import jax
import jax.numpy as jnp
from jax import lax
from jax.experimental import pallas as pl
from jax.experimental.pallas import tpu as pltpu
from jax.sharding import Mesh
from jax.sharding import PartitionSpec as P

HEADS = 16
HEAD_DIM = 64
STEP = 4

LN_EPS = 1e-06
BETA = 0.5
ADAM_EPS = 1e-06
DECAY = 0.01
RATE = 0.5
VEC_RATE = 0.2
GROUPS = 32

LOW = jnp.bfloat16
WIDE = jnp.float32
DATA = ("x", "y", "c")
EVERY = ("x", "y", "c", "z")
RING = 4
LANES = 128
VECS = 16
SUBLANES = 8
SCORE_SCALE = HEAD_DIM ** (-0.5)
MIB = 1 << 20


def send(block, axis, step):
    size = lax.axis_size(axis)
    return lax.ppermute(block, axis, [(i, (i + step) % size) for i in range(size)])


def together(*values):
    return lax.optimization_barrier(values)


class Gather:
    def __init__(self, low, high):
        self.own = [low, high]
        self.near = [send(low, "z", 1), send(high, "z", -1)]
        self.crossed = [send(high, "z", 1), send(low, "z", -1)]

    def relay(self):
        prev_low, next_high = self.near
        self.far = [send(prev_low, "z", 1), send(next_high, "z", -1)]

    def blocks(self):
        prev_low, next_high = self.near
        prev_high, next_low = self.crossed
        return [*self.own, next_low, next_high, *self.far, prev_low, prev_high]


def to_places(blocks):
    return [blocks[0]] + [send(blocks[RING - k], "z", RING - k) for k in range(1, RING)]


def scatter_z(right, left, staying, meanwhile=()):
    from_prev, from_next, staying, meanwhile = together(
        send(right, "z", 1), send(left, "z", -1), staying, meanwhile
    )
    own, after_low, before_high = staying
    half = after_low.shape[0]
    prev_low = send((after_low + from_prev[:half].astype(WIDE)).astype(LOW), "z", 1)
    next_high = send((before_high + from_next[:half].astype(WIDE)).astype(LOW), "z", -1)
    return [own, from_prev, from_next, prev_low, next_high], meanwhile


def sum_pairs(values, axis, apart, meanwhile=()):
    pairs = [(i, i ^ apart) for i in range(lax.axis_size(axis))]
    other, meanwhile = together(lax.ppermute(values, axis, pairs), meanwhile)
    return values + other, meanwhile


def send_split(block, phase, step):
    sizes = [lax.axis_size(axis) for axis in DATA]
    pairs = []
    for x in range(sizes[0]):
        for y in range(sizes[1]):
            for c in range(sizes[2]):
                if c == phase:
                    to = ((x + step) % sizes[0], y)
                else:
                    to = (x, (y + step) % sizes[1])
                pairs.append(
                    ((x * sizes[1] + y) * sizes[2] + c, (to[0] * sizes[1] + to[1]) * sizes[2] + c)
                )
    return lax.ppermute(block, DATA, pairs)


def dot(left, right, dims):
    return lax.dot_general(left, right, (dims, ((), ())), preferred_element_type=WIDE)


NN = ((1,), (0,))
NT = ((1,), (1,))
TN = ((0,), (0,))


def shape_of(shape, dtype):
    return jax.ShapeDtypeStruct(shape, dtype)


def takes(micros):
    return pl.CostEstimate(
        flops=int(micros * 1e9), bytes_accessed=int(micros * 3e6), transcendentals=0
    )


def whole_call(kernel, out_shape, scalars, arrays, scratch=(), limit=40, micros=1.0):
    in_specs = [pl.BlockSpec(memory_space=pltpu.SMEM)] * (scalars is not None)
    operands = ([scalars] if scalars is not None else []) + list(arrays)
    many = isinstance(out_shape, list)
    vmem = pl.BlockSpec(memory_space=pltpu.VMEM)
    return pl.pallas_call(
        kernel,
        out_shape=out_shape,
        in_specs=in_specs + [vmem] * len(arrays),
        out_specs=[vmem] * len(out_shape) if many else vmem,
        scratch_shapes=list(scratch),
        compiler_params=pltpu.CompilerParams(vmem_limit_bytes=limit * MIB),
        cost_estimate=takes(micros),
    )(*operands)


def staged_call(
    kernel, out_shape, scalars, arrays, scratch=(), limit=24, micros=1.0, last_rows=()
):
    count, total = len(arrays), len(arrays) + len(out_shape)
    last_rows = dict(last_rows)
    shapes = [(last_rows.get(k, array.shape[0]), *array.shape[1:]) for k, array in enumerate(arrays)]

    def body(*refs):
        scalar, refs = refs[:1], refs[1:]
        given, rest = refs[:total], refs[total:]
        held, sems, rest = rest[:total], rest[total], rest[total + 1 :]
        copies = [
            pltpu.make_async_copy(
                given[k].at[pl.ds(arrays[k].shape[0] - shapes[k][0], shapes[k][0])], held[k], sems.at[k]
            )
            if k < count
            else pltpu.make_async_copy(held[k], given[k], sems.at[k])
            for k in range(total)
        ]
        for copy in copies[:count]:
            copy.start()
        for copy in copies[:count]:
            copy.wait()
        kernel(*scalar, *held, *rest)
        for copy in copies[count:]:
            copy.start()
        for copy in copies[count:]:
            copy.wait()

    anywhere = pl.BlockSpec(memory_space=pl.ANY)
    holds = [pltpu.VMEM(shape, array.dtype) for shape, array in zip(shapes, arrays)]
    holds += [pltpu.VMEM(array.shape, array.dtype) for array in out_shape]
    return pl.pallas_call(
        body,
        out_shape=out_shape,
        in_specs=[pl.BlockSpec(memory_space=pltpu.SMEM)] + [anywhere] * count,
        out_specs=[anywhere] * len(out_shape),
        scratch_shapes=holds + [pltpu.SemaphoreType.DMA((total,))] + list(scratch),
        compiler_params=pltpu.CompilerParams(vmem_limit_bytes=limit * MIB),
        cost_estimate=takes(micros),
    )(scalars, *arrays)


def pick_kernel(where, qkv, up, vec, *outs):
    lanes, wide = qkv.shape[1] // (3 * RING), up.shape[1] // RING
    for step in range(RING):
        place = (where[3] + step) % RING
        for third in range(3):
            at = pl.multiple_of(third * lanes * RING + place * lanes, lanes)
            outs[step][:, third * lanes : (third + 1) * lanes] = qkv[:, pl.ds(at, lanes)]
        outs[step][:, 3 * lanes : 3 * lanes + LANES] = jnp.zeros((qkv.shape[0], LANES), WIDE)
        outs[step][:, 3 * lanes : 3 * lanes + vec.shape[1]] = vec[...]
        outs[step][:, 3 * lanes + LANES :] = up[:, pl.ds(pl.multiple_of(place * wide, wide), wide)]


def collect_kernel(where, own, first, second, third, out, keep, give, hold):
    core, place = where[2], where[3]
    columns = own.shape[1]
    for step, piece in enumerate((own, first, second, third)):
        hold[(place + step) % RING] = piece[...]
    lanes = out.shape[1] // RING
    for half in range(2):
        for target, side in ((keep, core), (give, 1 - core)):
            at = side * 2 + half
            target[half, :, :columns] = hold[at]
            target[half, :, columns:] = out[:, pl.ds(pl.multiple_of(at * lanes, lanes), lanes)]


def pair_kernel(where, mine, theirs, down, att, ffn):
    first = where[2] == 0
    wide = ffn.shape[2]
    narrow = 3 * (att.shape[2] - LANES) // 4 + LANES
    for half in range(2):
        low = jnp.where(first, mine[half], theirs[half])
        high = jnp.where(first, theirs[half], mine[half])
        block = jnp.concatenate([low, high], axis=0).astype(LOW)
        att[half, :, :narrow] = block[:, :narrow]
        att[half, :, narrow:] = block[:, narrow + wide :]
        ffn[half] = block[:, narrow : narrow + wide]
        rows = ffn.shape[1]
        ffn[2 + half] = down[half * rows : (half + 1) * rows].astype(LOW)


def chip_of(where, first, second):
    x, y, c = where[0], where[1], where[2]
    along_x = (x + jnp.where(c == 0, first, second)) % RING
    along_y = (y + jnp.where(c == 0, second, first)) % RING
    return along_x * RING + along_y


def place_kernel(where, *refs):
    out = refs[-1]
    for second in range(RING):
        for first in range(RING):
            out[:, chip_of(where, first, second)] = refs[second][first]


def weights_kernel(where, mine, theirs, qkv, out, vecs):
    first = where[2] == 0
    rows, columns = mine.shape
    lanes = out.shape[0]
    for half in range(2):
        block = (
            jnp.where(first, mine[...], theirs[...])
            if half == 0
            else jnp.where(first, theirs[...], mine[...])
        )
        qkv[half * rows : (half + 1) * rows] = block[:, : 3 * lanes]
        vec = block[:, 3 * lanes : 3 * lanes + LANES].astype(WIDE)
        vecs[:, half * rows : (half + 1) * rows] = vec.T[:VECS]
        for part in range(2):
            at = (2 * half + part) * lanes
            out[:, at : at + lanes] = block[part * lanes : (part + 1) * lanes, columns - lanes :]


def ffn_weights_kernel(where, mine, theirs, up, down):
    first = where[2] == 0
    for half in range(2):
        up[half] = jnp.where(first, mine[half], theirs[half])
        up[2 + half] = jnp.where(first, theirs[half], mine[half])
        down[:, half] = jnp.where(first, mine[2 + half], theirs[2 + half])
        down[:, 2 + half] = jnp.where(first, theirs[2 + half], mine[2 + half])


def along_ring(block, phase):
    return [block] + [send_split(block, phase, -k) for k in range(1, RING)]


def by_chip(where, blocks):
    parts, rows, columns = blocks[0].shape[1:]
    return whole_call(
        place_kernel,
        shape_of((parts, RING * RING, rows, columns), LOW),
        where,
        blocks,
        limit=6,
    )


def weight_pieces(where, qkv_master, up_master, vec_master):
    columns = 3 * (qkv_master.shape[1] // (3 * RING)) + LANES + up_master.shape[1] // RING
    pieces = staged_call(
        pick_kernel,
        [shape_of((qkv_master.shape[0], columns), WIDE)] * RING,
        where,
        [qkv_master, up_master, vec_master],
        limit=8,
    )
    return pieces


def weight_blocks(where, arrived, out_master, down_master):
    own, columns = arrived[0].shape
    lanes = out_master.shape[1] // RING
    wide = columns - 3 * lanes - LANES
    half = shape_of((2, own, columns + lanes), WIDE)
    keep, give = whole_call(
        collect_kernel,
        [half, half],
        where,
        [*arrived, out_master],
        [pltpu.VMEM((RING, own, columns), WIDE)],
        limit=4,
    )
    return whole_call(
        pair_kernel,
        [
            shape_of((2, 2 * own, 4 * lanes + LANES), LOW),
            shape_of((4, 2 * own, wide), LOW),
        ],
        where,
        [keep, send(give, "c", 1), down_master],
        limit=4,
    )


def attention_weights(where, mine, theirs):
    halves, chips, rows, columns = mine.shape
    lanes = (columns - LANES) // 4
    flat = (halves * chips * rows, columns)
    return whole_call(
        weights_kernel,
        [
            shape_of((2 * flat[0], 3 * lanes), LOW),
            shape_of((lanes, RING * lanes), LOW),
            shape_of((VECS, RING * lanes), WIDE),
        ],
        where,
        [mine.reshape(flat), theirs.reshape(flat)],
        limit=10,
    )


def ffn_weights(where, mine, theirs):
    parts, chips, rows, columns = mine.shape
    up, down = whole_call(
        ffn_weights_kernel,
        [shape_of((parts, chips, rows, columns), LOW), shape_of((chips, parts, rows, columns), LOW)],
        where,
        [mine, theirs],
        limit=12,
    )
    flat = (parts * chips * rows, columns)
    return up.reshape(flat), down.reshape(flat)


def arrange_kernel(where, kept, arrived, own, *gone):
    for second in range(RING):
        for first in range(RING):
            chip = chip_of(where, first, second)
            total = kept[chip] + arrived[chip].astype(WIDE)
            if first == 0:
                own[second] = total
            else:
                gone[first - 1][second] = total.astype(LOW)


def core_sum(where, kept, arrived, micros):
    piece = (RING, *kept.shape[1:])
    return whole_call(
        arrange_kernel,
        [shape_of(piece, WIDE)] + [shape_of(piece, LOW)] * 3,
        where,
        [kept, arrived],
        limit=20,
        micros=micros,
    )


def sum_kernel(*refs):
    att, ffn, out, gone = refs[0:4], refs[4:8], refs[8], refs[9:12]
    rows, wide = ffn[0].shape[1:]
    columns = att[0].shape[2]
    for k in range(RING):
        target = out if k == 0 else gone[k - 1]
        target[:, :wide] = sum(part[k].astype(WIDE) for part in ffn).astype(target.dtype)
        total = sum(part[k].astype(WIDE) for part in att).astype(target.dtype)
        target[:, wide : wide + columns] = total[:rows]
        target[:, wide + columns :] = total[rows:]


def back_along_ring(own, gone, phase):
    return [own] + [send_split(gone[k - 1], phase, k) for k in range(1, RING)]


def ring_sum(att, ffn):
    rows, wide = ffn[0].shape[1:]
    shape = (rows, wide + 2 * att[0].shape[2])
    return whole_call(
        sum_kernel,
        [shape_of(shape, WIDE)] + [shape_of(shape, LOW)] * 3,
        None,
        [*att, *ffn],
        limit=16,
        micros=1.5,
    )


def normalise(values):
    centre = jnp.mean(values, -1, keepdims=True)
    centred = values - centre
    spread = jnp.mean(centred * centred, -1, keepdims=True)
    scale = lax.rsqrt(spread + LN_EPS)
    return centred * scale, scale


def normalise_back(grad, unit, scale, gain):
    grad_unit = grad * gain
    return scale * (
        grad_unit
        - jnp.mean(grad_unit, -1, keepdims=True)
        - unit * jnp.mean(grad_unit * unit, -1, keepdims=True)
    )


def images_kernel(counts, one, penalty):
    row = lax.broadcasted_iota(jnp.int32, one.shape, 0)
    lane = lax.broadcasted_iota(jnp.int32, one.shape, 1) % HEAD_DIM
    first_end = counts[0, 0]
    second_end = first_end + counts[0, 1]
    image = (row >= first_end).astype(jnp.int32) + (row >= second_end).astype(jnp.int32)
    one[...] = jnp.where(lane == image, 1.0, 0.0).astype(LOW)
    penalty[...] = jnp.where((lane == image) | (lane >= 3), 0.0, -1e30).astype(LOW)


def both(blocks, step):
    return jnp.concatenate([blocks[2 * step][...], blocks[2 * step + 1][...]])


def first_kernel(where, vecs, weight, *refs):
    blocks, (normed, qkv) = refs[:8], refs[8:]
    rows = 2 * blocks[0].shape[0]
    lanes = weight.shape[1] // 3
    at = pl.ds(pl.multiple_of(where[3] * lanes, lanes), lanes)
    bias = jnp.concatenate([vecs[2:3, at], jnp.zeros((1, lanes), WIDE), vecs[3:4, at]], axis=1)
    for step in range(RING):
        here = rows_of(where, step, rows)
        unit, _ = normalise(both(blocks, step).astype(WIDE))
        block = (unit * vecs[0:1] + vecs[1:2]).astype(LOW)
        normed[here] = block
        qkv[here] = (dot(block, weight[...], NN) + bias).astype(LOW)


def scores_of(query, key, one, penalty, mine):
    return dot(jnp.where(mine, query, one), jnp.where(mine, key, penalty), NT)


LEAVING = ((4, 5), (3, 6))
STAYING = ((0, 1), (2, 7))
SPOT = {
    block: (call, place)
    for call, pairs in enumerate((LEAVING, STAYING))
    for place, block in enumerate(pairs[0] + pairs[1])
}


def rows_of(where, step, rows):
    return pl.ds(pl.multiple_of((where[3] + step) % RING * rows, rows), rows)


def half_block(where, ref, block):
    half = ref.shape[0] // (2 * RING)
    device = (where[3] + block // 2) % RING
    return ref[pl.ds(pl.multiple_of((2 * device + block % 2) * half, half), half)]


def attend_kernel(pairs, where, query, key, value, one, penalty, out, attended, log_total, *refs):
    pieces, total = refs[:-1], refs[-1]
    block = query.shape[0] // RING
    half = block // 2
    lane = lax.broadcasted_iota(jnp.int32, (1, LANES), 1)
    first = pl.program_id(0) == 0
    for group, blocks in enumerate(pairs):
        at = pl.ds(group * block, block)
        scaled = jnp.concatenate([half_block(where, query, k) for k in blocks]) * LOW(SCORE_SCALE)
        chosen = jnp.concatenate([half_block(where, one, k) for k in blocks])
        parts, logs = [], []
        for head in range(2):
            mine = lane // HEAD_DIM == head
            scores = scores_of(scaled, key[...], chosen, penalty[...], mine)
            top = jnp.max(scores, -1, keepdims=True)
            exponent = jnp.exp(scores - top)
            sums = jnp.sum(exponent, -1, keepdims=True)
            parts.append(dot((exponent * (1.0 / sums)).astype(LOW), value[...], NN))
            logs.append(top + jnp.log(sums))
        rounded = jnp.where(lane < HEAD_DIM, parts[0], parts[1]).astype(LOW)
        attended[at] = rounded
        log_total[at] = jnp.where(lane < HEAD_DIM, logs[0], logs[1])
        product = dot(rounded, out[...], NN)
        total[group] = jnp.where(first, product, total[group] + product)

    @pl.when(pl.program_id(0) == pl.num_programs(0) - 1)
    def _():
        if len(pieces) == 2:
            right, left = pieces
            right[:half] = total[0, :half].astype(LOW)
            left[:half] = total[0, half:].astype(LOW)
            right[half:] = total[1, :half].astype(LOW)
            left[half:] = total[1, half:].astype(LOW)
        else:
            own, after_low, before_high = pieces
            own[...] = total[0]
            after_low[...] = total[1, :half]
            before_high[...] = total[1, half:]


def by_pair(shape, offset=0):
    return pl.BlockSpec((shape[0], LANES), lambda j: (0, offset + j))


def whole(array):
    return pl.BlockSpec(array.shape, lambda j: (0,) * len(array.shape))


SCALARS = pl.BlockSpec(memory_space=pltpu.SMEM)


def attend(where, blocks, qkv, one, penalty, out):
    rows, lanes = qkv.shape[0], qkv.shape[1] // 3
    pairs, width, block = lanes // LANES, out.shape[1], rows // RING
    if blocks is LEAVING:
        pieces = [shape_of((block, width), LOW)] * 2
    else:
        pieces = [shape_of((block, width), WIDE)] + [shape_of((block // 2, width), WIDE)] * 2
    some = (2 * block, lanes)

    def kernel(*refs):
        attend_kernel(blocks, *refs)

    return pl.pallas_call(
        kernel,
        grid=(pairs,),
        in_specs=[SCALARS]
        + [by_pair(qkv.shape, k * pairs) for k in range(3)]
        + [whole(one), whole(penalty), pl.BlockSpec((LANES, width), lambda j: (j, 0))],
        out_specs=[by_pair(some)] * 2 + [whole(piece) for piece in pieces],
        out_shape=[shape_of(some, LOW), shape_of(some, WIDE)] + pieces,
        scratch_shapes=[pltpu.VMEM((2, block, width), WIDE)],
        compiler_params=pltpu.CompilerParams(vmem_limit_bytes=20 * MIB),
        cost_estimate=takes(7.0),
    )(where, qkv, qkv, qkv, one, penalty, out)


def attend_back_kernel(steps, where, query, key, value, one, penalty, out, *refs):
    log_totals, attendeds, refs = refs[0:2], refs[2:4], refs[4:]
    pieces, refs = refs[: 2 * len(steps)], refs[2 * len(steps) :]
    earlier = refs[:3] if len(refs) == 9 else None
    grad_query, grad_key, grad_value, grad_out, key_sum, value_sum = refs[-6:]
    block = query.shape[0] // RING
    half = block // 2
    lane = lax.broadcasted_iota(jnp.int32, (1, LANES), 1)

    def kept(arrays, step):
        spots = [SPOT[2 * step + k] for k in range(2)]
        return jnp.concatenate(
            [arrays[call][place * half : (place + 1) * half] for call, place in spots]
        )

    for place, step in enumerate(steps):
        here = rows_of(where, step, block)
        scaled = query[here] * LOW(SCORE_SCALE)
        grad_low = both(pieces, place)
        grad = dot(grad_low, out[...], NT).astype(LOW)
        logs = kept(log_totals, step)
        part_out = dot(kept(attendeds, step), grad_low, TN)
        parts = []
        for head in range(2):
            mine = lane // HEAD_DIM == head
            scores = scores_of(scaled, key[...], one[here], penalty[...], mine)
            probs = jnp.exp(scores - logs[:, head * HEAD_DIM : head * HEAD_DIM + 1])
            grad_probs = dot(jnp.where(mine, grad, LOW(0.0)), value[...], NT)
            inner = jnp.sum(probs * grad_probs, -1, keepdims=True)
            grad_scores = (probs * (grad_probs - inner)).astype(LOW)
            parts.append(dot(grad_scores, key[...], NN))
            for_value = dot(probs.astype(LOW), grad, TN)
            for_key = dot(grad_scores, scaled, TN)
            if place == 0:
                key_sum[head] = for_key
                value_sum[head] = for_value
            else:
                key_sum[head] += for_key
                value_sum[head] += for_value
        grad_query[place * block : (place + 1) * block] = (
            jnp.where(lane < HEAD_DIM, parts[0], parts[1]) * SCORE_SCALE
        ).astype(LOW)
        if place == 0:
            grad_out[...] = part_out
        else:
            grad_out[...] += part_out
    for_key = jnp.where(lane < HEAD_DIM, key_sum[0], key_sum[1])
    for_value = jnp.where(lane < HEAD_DIM, value_sum[0], value_sum[1])
    if earlier is not None:
        for_key = for_key + earlier[0][...]
        for_value = for_value + earlier[1][...]
        grad_out[...] += earlier[2][...]
    grad_key[...] = for_key.astype(grad_key.dtype)
    grad_value[...] = for_value.astype(grad_value.dtype)


def attend_back(where, steps, qkv, one, penalty, out, log_totals, attendeds, pieces, earlier=()):
    rows, lanes = qkv.shape[0], qkv.shape[1] // 3
    pairs, width, block = lanes // LANES, out.shape[1], rows // RING
    out_rows = pl.BlockSpec((LANES, width), lambda j: (j, 0))
    sums = LOW if earlier else WIDE
    group = (rows, lanes)
    some = (len(steps) * block, lanes)

    def kernel(*refs):
        attend_back_kernel(steps, *refs)

    return pl.pallas_call(
        kernel,
        grid=(pairs,),
        in_specs=[SCALARS]
        + [by_pair(qkv.shape, k * pairs) for k in range(3)]
        + [whole(one), whole(penalty), out_rows]
        + [by_pair(array.shape) for array in (*log_totals, *attendeds)]
        + [whole(piece) for piece in pieces]
        + ([by_pair(group)] * 2 + [out_rows] if earlier else []),
        out_specs=[by_pair(some), by_pair(group), by_pair(group), out_rows],
        out_shape=[
            shape_of(some, LOW),
            shape_of(group, sums),
            shape_of(group, sums),
            shape_of((lanes, width), WIDE),
        ],
        scratch_shapes=[pltpu.VMEM((2, rows, LANES), WIDE)] * 2,
        compiler_params=pltpu.CompilerParams(vmem_limit_bytes=24 * MIB),
        cost_estimate=takes(5.0 * len(steps)),
    )(where, qkv, qkv, qkv, one, penalty, out, *log_totals, *attendeds, *pieces, *earlier)


NEAR = (0, 1, 3)
FAR = (2,)


def project_kernel(near, far, weight, own, after_low, before_high, right, left):
    rows = far.shape[0]
    half = rows // 2
    own[...] = dot(near[:rows], weight[...], NN)
    block = dot(near[rows : 2 * rows], weight[...], NN)
    after_low[...] = block[:half]
    right[half:] = block[half:].astype(LOW)
    block = dot(near[2 * rows :], weight[...], NN)
    left[half:] = block[:half].astype(LOW)
    before_high[...] = block[half:]
    block = dot(far[...], weight[...], NN)
    right[:half] = block[:half].astype(LOW)
    left[:half] = block[half:].astype(LOW)


def arrived_sum(own, from_prev, from_next, prev_low, next_high):
    half = prev_low.shape[0]
    low = prev_low[...].astype(WIDE) + from_next[half:].astype(WIDE)
    high = from_prev[half:].astype(WIDE) + next_high[...].astype(WIDE)
    return own[...] + jnp.concatenate([low, high])


def middle_kernel(tokens, vecs, *refs):
    arrivals, (middle, low, high) = refs[:5], refs[5:]
    half = low.shape[0]
    middle[...] = tokens[...].astype(WIDE) + (arrived_sum(*arrivals) + vecs[4:5])
    unit, _ = normalise(middle[...])
    normed = (unit * vecs[5:6] + vecs[6:7]).astype(LOW)
    low[...] = normed[:half]
    high[...] = normed[half:]


def hidden_rows(where, vecs, up, down, cotangents, pieces, place, outs):
    normed, hidden, grad_pre, column = outs
    rows = 2 * pieces[0].shape[0]
    at = pl.ds(place * rows, rows)
    block = both(pieces, place)
    normed[at] = block
    pre_act = dot(block, up[...], NN) + vecs[pl.ds(7 + where[3], 1)]
    below = 0.5 * (1.0 + lax.erf(pre_act * (0.5**0.5)))
    hidden[at] = (pre_act * below).astype(LOW)
    slope = below + pre_act * (jnp.exp(-0.5 * pre_act * pre_act) * 0.3989422804014327)
    grad = (dot(both(cotangents, place), down[...], NT) * slope).astype(LOW)
    grad_pre[at] = grad
    column[...] += jnp.sum(grad.astype(WIDE), 0, keepdims=True)
    return dot(grad, up[...], NT)


def hidden_near_kernel(where, vecs, up, down, *refs):
    cotangents, pieces, outs = refs[:6], refs[6:12], refs[12:16]
    own, after_low, before_high, after_high, before_low = refs[16:]
    half = pieces[0].shape[0]
    outs[3][...] = jnp.zeros(outs[3].shape, WIDE)
    for place in range(3):
        block = hidden_rows(where, vecs, up, down, cotangents, pieces, place, outs)
        if place == 0:
            own[...] = block
        elif place == 1:
            after_low[...] = block[:half]
            after_high[...] = block[half:].astype(LOW)
        else:
            before_low[...] = block[:half].astype(LOW)
            before_high[...] = block[half:]


def hidden_far_kernel(where, vecs, up, down, *refs):
    cotangents, pieces, refs = refs[:2], refs[2:4], refs[4:]
    column, after_high, before_low, outs, (right, left) = refs[0], refs[1], refs[2], refs[3:7], refs[7:]
    half = pieces[0].shape[0]
    outs[3][...] = column[...]
    block = hidden_rows(where, vecs, up, down, cotangents, pieces, 0, outs)
    right[:half] = block[:half].astype(LOW)
    left[:half] = block[half:].astype(LOW)
    right[half:] = after_high[...]
    left[half:] = before_low[...]


def by_core(where, hold, keep, give):
    for chip in range(keep.shape[0]):
        keep[chip] = hold[2 * chip + where[2]]
        give[chip] = hold[2 * chip + 1 - where[2]].astype(LOW)


def ffn_grads_kernel(where, *refs):
    normed, hidden, grad_pre, cotangents, refs = refs[:2], refs[2:4], refs[4:6], refs[6:14], refs[14:]
    keep, give, hold = refs
    width = normed[0].shape[1]
    part = width // RING
    cot = [jnp.concatenate([block[...] for block in part]) for part in (cotangents[:6], cotangents[6:])]
    for k in range(RING):
        here = slice(k * part, (k + 1) * part)
        block = sum(dot(normed[p][:, here], grad_pre[p][...], TN) for p in range(2))
        hold[:, :SUBLANES, k * width : (k + 1) * width] = block.reshape(-1, SUBLANES, width)
        block = sum(dot(hidden[p][:, here], cot[p], TN) for p in range(2))
        block = block.reshape(-1, RING, SUBLANES, width)
        owners = block.shape[0]
        for q in range(RING):
            hold[k * owners : (k + 1) * owners, SUBLANES:, q * width : (q + 1) * width] = block[:, q]
    by_core(where, hold, keep, give)


def grad_middle_kernel(middle, cotangent, vecs, *refs):
    arrivals, (grad_middle, low, high, sums) = refs[:5], refs[5:]
    half = low.shape[0]
    grad = arrived_sum(*arrivals)
    unit, scale = normalise(middle[...])
    cot = cotangent[...].astype(WIDE)
    total = cot + normalise_back(grad, unit, scale, vecs[5:6])
    grad_middle[...] = total
    rounded = total.astype(LOW)
    low[...] = rounded[:half]
    high[...] = rounded[half:]
    sums[...] = jnp.concatenate(
        [
            jnp.sum(rounded.astype(WIDE), 0, keepdims=True),
            jnp.sum(grad * unit, 0, keepdims=True),
            jnp.sum(grad, 0, keepdims=True),
            jnp.sum(cot, 0, keepdims=True),
            jnp.zeros((4, cot.shape[1]), WIDE),
        ]
    )


def query_rows(near, far, step):
    rows = far.shape[0]
    if step in FAR:
        return far[...]
    place = NEAR.index(step)
    return near[place * rows : (place + 1) * rows]


def back_product_kernel(where, weight, query_near, query_far, grad_key, grad_value, *refs):
    blocks, (other_right, other_left), pieces, sums = refs[:8], refs[8:10], refs[10:15], refs[15]
    own, after_low, before_high, right, left = pieces
    right[own.shape[0] :] = other_right[...]
    left[own.shape[0] :] = other_left[...]
    lanes = query_far.shape[1]
    rows = own.shape[0]
    half = rows // 2
    for step in range(RING):
        here = rows_of(where, step, rows)
        block = dot(query_rows(query_near, query_far, step), weight[:, :lanes], NT)
        block += dot(grad_key[here], weight[:, lanes : 2 * lanes], NT)
        block += dot(grad_value[here], weight[:, 2 * lanes :], NT)
        if step == 0:
            own[...] = block
        elif step == 1:
            after_low[...] = block[:half]
            right[half:rows] = block[half:].astype(LOW)
        elif step == 2:
            right[:half] = block[:half].astype(LOW)
            left[:half] = block[half:].astype(LOW)
        else:
            before_high[...] = block[half:]
            left[half:rows] = block[:half].astype(LOW)
        unit, _ = normalise(both(blocks, step).astype(WIDE))
        pair = jnp.concatenate(
            [
                jnp.sum(block * unit, 0, keepdims=True),
                jnp.sum(block, 0, keepdims=True),
                jnp.zeros((6, block.shape[1]), WIDE),
            ]
        )
        if step == 0:
            sums[...] = pair
        else:
            sums[...] += pair


def grads_kernel(
    where,
    normed,
    query_near,
    query_far,
    grad_key,
    grad_value,
    grad_out,
    first_sums,
    sums,
    column,
    keep,
    give,
    vecs,
    hold,
):
    rows, lanes = query_far.shape
    queries = [query_rows(query_near, query_far, step) for step in range(RING)]
    vecs[...] = jnp.zeros(vecs.shape, WIDE)
    at = pl.ds(pl.multiple_of(where[3] * lanes, lanes), lanes)
    vecs[0:2] = first_sums[0:2]
    vecs[2:3, at] = sum(jnp.sum(block.astype(WIDE), 0, keepdims=True) for block in queries)
    vecs[3:4, at] = jnp.sum(grad_value[...].astype(WIDE), 0, keepdims=True)
    vecs[4:7] = sums[0:3]
    for k in range(RING):
        vecs[7 + k : 8 + k] = jnp.where(where[3] == k, column[...], 0.0)
    vecs[11:12] = sums[3:4]
    for part in range(RING):
        here = slice(part * lanes, (part + 1) * lanes)
        left = normed[:, here]
        block = jnp.concatenate(
            [sum(dot(normed[rows_of(where, k, rows), here], queries[k], TN) for k in range(RING))]
            + [dot(left, third[...], TN) for third in (grad_key, grad_value)]
            + [vecs[:, here].T, grad_out[:, here]],
            axis=1,
        )
        hold[:, part * SUBLANES : (part + 1) * SUBLANES] = block.reshape(
            -1, SUBLANES, block.shape[1]
        )
    by_core(where, hold, keep, give)


def relay_kernel(from_prev, from_next, after, before, other_after, other_before, forth, back):
    half = after.shape[0]
    for place, (right, left) in enumerate(((after, before), (other_after, other_before))):
        here, there = pl.ds(2 * place * half, half), pl.ds(place * half, half)
        forth[there] = (right[...] + from_prev[here].astype(WIDE)).astype(LOW)
        back[there] = (left[...] + from_next[here].astype(WIDE)).astype(LOW)


def outputs_kernel(
    tokens, grad_middle, middle, vecs, own, other, from_prev, from_next, prev, following, grad, out
):
    half = own.shape[0] // 2
    sums = []
    for place, mine in enumerate((own, other)):
        at = pl.ds((2 * place + 1) * half, half)
        here = pl.ds(place * half, half)
        low = prev[here].astype(WIDE) + from_next[at].astype(WIDE)
        high = from_prev[at].astype(WIDE) + following[here].astype(WIDE)
        sums.append(mine[...] + jnp.concatenate([low, high]))
    unit, scale = normalise(tokens[...].astype(WIDE))
    grad[...] = (grad_middle[...] + normalise_back(sums[0], unit, scale, vecs[0:1])).astype(LOW)
    out[...] = (middle[...] + (sums[1] + vecs[11:12])).astype(LOW)


def states_kernel(where, *refs):
    qkv, up, outs, hold = refs[0:3], refs[3:6], refs[6:10], refs[10]
    own, lanes, wide = qkv[0].shape[0], qkv[0].shape[1] // (3 * RING), up[0].shape[1] // RING
    hold[...] = jnp.zeros(hold.shape, WIDE)
    for step in range(RING):
        place = (where[3] + step) % RING
        for kind in range(3):
            at = pl.ds(pl.multiple_of(place * wide, wide), wide)
            hold[kind * own : (kind + 1) * own] = up[kind][:, at]
            there = slice((3 + kind) * own, (4 + kind) * own)
            for third in range(3):
                at = pl.ds(pl.multiple_of(third * lanes * RING + place * lanes, lanes), lanes)
                hold[there, third * lanes : (third + 1) * lanes] = qkv[kind][:, at]
        outs[step][...] = hold[...].astype(LOW)


def adam_step(grad_mean, moment, square, weight, decay_rate):
    moment_new = BETA * moment + (1.0 - BETA) * grad_mean
    square_new = BETA * square + (1.0 - BETA) * grad_mean * grad_mean
    correct = 1.0 - BETA**STEP
    direction = (
        moment_new / correct / (jnp.sqrt(square_new / correct) + ADAM_EPS) + decay_rate * weight
    )
    return (moment_new, square_new, direction)


def row_of(values):
    lane = lax.broadcasted_iota(jnp.int32, (1, LANES), 1)
    return sum(jnp.where(lane == k, value, 0.0) for k, value in enumerate(values))


def ring_totals(parts):
    return (parts[0][...] + parts[1][...].astype(WIDE)) + (
        parts[2][...].astype(WIDE) + parts[3][...].astype(WIDE)
    )


def rows_sums(sums, ffn_sums, lanes):
    own, wide = ffn_sums.shape[0] // 2, ffn_sums.shape[1] // RING
    out_sum = jnp.concatenate(
        [sums[part * own : (part + 1) * own, -lanes:] for part in range(RING)], axis=1
    )
    down_sum = jnp.concatenate(
        [ffn_sums[own:, part * wide : (part + 1) * wide] for part in range(RING)]
    )
    return out_sum, down_sum


def norms_kernel(where, *refs):
    arrived, states, plain = refs[0:4], refs[4:8], refs[8:14]
    pieces, outs, sums, ffn_sums = refs[14:18], refs[18:24], refs[24], refs[25]
    own, wide = ffn_sums.shape[0] // 2, ffn_sums.shape[1] // RING
    lanes = (sums.shape[1] - LANES) // 4
    narrow = sums.shape[1] - lanes
    totals = ring_totals(arrived)
    width, columns = ffn_sums.shape[1], sums.shape[1]
    ffn_sums[...] = totals[:, :width]
    sums[: 2 * own] = totals[:, width : width + columns]
    sums[2 * own :] = totals[:, width + columns :]
    squares = [jnp.zeros((1, 1), WIDE)] * 8

    def add(k, weight, moment, square, grad, targets=()):
        results = adam_step(grad / GROUPS, moment, square, weight, DECAY)
        for target, result in zip(targets, results):
            target[...] = result
        direction = results[2]
        squares[k] = squares[k] + jnp.sum(weight * weight, keepdims=True)
        squares[4 + k] = squares[4 + k] + jnp.sum(direction * direction, keepdims=True)

    for step in range(RING):
        place = (where[3] + step) % RING
        at = pl.ds(pl.multiple_of(place * wide, wide), wide)
        here = pl.ds(pl.multiple_of(place * own, own), own)
        state = states[step][...].astype(WIDE)
        for k, grad in enumerate((ffn_sums[:own, at], sums[here, : 3 * lanes])):
            kinds = (
                state[(3 * k + kind) * own : (3 * k + kind + 1) * own, : grad.shape[1]]
                for kind in range(3)
            )
            add(2 - 2 * k, *kinds, grad)
    for k, grad in enumerate(rows_sums(sums, ffn_sums, lanes)):
        kinds = (plain[3 * k + kind][...] for kind in range(3))
        add(1 + 2 * k, *kinds, grad, outs[3 * k : 3 * k + 3])
    row = row_of([jnp.zeros((1, 1), WIDE)] * VECS + squares)
    for step in range(RING):
        place = (where[3] + step) % RING
        at = pl.ds(pl.multiple_of(place * wide, wide), wide)
        here = pl.ds(pl.multiple_of(place * own, own), own)
        pieces[step][:, :narrow] = sums[here, :narrow]
        pieces[step][:, 3 * lanes : narrow] += row
        pieces[step][:, narrow:] = ffn_sums[:own, at]


def row_kernel(where, *refs):
    pieces, row, hold = refs[:RING], refs[RING], refs[RING + 1]
    for step, piece in enumerate(pieces):
        lanes = (piece.shape[1] - LANES) // 7
        hold[(where[3] + step) % RING] = piece[0:1, 3 * lanes : 3 * lanes + LANES]
    row[...] = (hold[0] + hold[1]) + (hold[2] + hold[3])


def adam_kernel(where, *refs):
    home, refs = refs[:RING], refs[RING:]
    weights, moments, squares, outs = refs[0:3], refs[3:6], refs[6:9], refs[9:18]
    sums = refs[18:20]
    lanes, wide = sums[0].shape[1] // (3 * RING), sums[1].shape[1] // RING
    for step in range(RING):
        place = (where[3] + step) % RING
        for third in range(3):
            at = pl.multiple_of(third * lanes * RING + place * lanes, lanes)
            sums[0][:, pl.ds(at, lanes)] = home[step][:, third * lanes : (third + 1) * lanes]
        at = pl.ds(pl.multiple_of(place * wide, wide), wide)
        sums[1][:, at] = home[step][:, 3 * lanes + LANES :]
    columns = weights[2].shape[1]
    vec_sum = sum(home[step][:, 3 * lanes : 3 * lanes + LANES] for step in range(RING))
    for k, grad in enumerate((sums[0][...], sums[1][...], vec_sum[:, :columns])):
        weight = weights[k][...]
        moment, square, direction = adam_step(
            grad / GROUPS, moments[k][...], squares[k][...], weight, DECAY if k < 2 else 0.0
        )
        outs[3 * k][...] = moment
        outs[3 * k + 1][...] = square
        outs[3 * k + 2][...] = direction if k < 2 else weight - VEC_RATE * direction


def update_kernel(where, row, *refs):
    weights, directions, news, norms = refs[0:4], refs[4:8], refs[8:12], refs[12]
    root = jnp.sqrt(row[...])
    for k in range(4):
        weight_norm, update_norm = root[:, VECS + k : VECS + k + 1], root[:, VECS + 4 + k : VECS + 5 + k]
        norms[k : k + 1, 0:1] = weight_norm
        norms[k : k + 1, 1:2] = update_norm
        news[k][...] = weights[k][...] - RATE * (weight_norm / update_norm) * directions[k][...]


def on_device(
    tokens,
    cotangent,
    seg_counts,
    qkv_master,
    out_master,
    up_master,
    down_master,
    qkv_first,
    out_first,
    up_first,
    down_first,
    qkv_second,
    out_second,
    up_second,
    down_second,
    vec_master,
    vec_first,
    vec_second,
):
    where = jnp.stack([lax.axis_index(axis) for axis in EVERY]).astype(jnp.int32)
    rows, width = tokens.shape
    own = qkv_master.shape[0]
    lanes = width // RING
    hidden_lanes = up_master.shape[1] // RING
    chips = lax.axis_size("x") * lax.axis_size("y")
    group = rows * RING
    half = rows // 2
    wide_rows, half_rows = shape_of((rows, width), WIDE), shape_of((half, width), LOW)
    low_rows, group_low = shape_of((rows, width), LOW), shape_of((group, width), LOW)

    token_rows = Gather(tokens[:half], tokens[half:])
    arrived = to_places(weight_pieces(where, qkv_master, up_master, vec_master))
    arrived, token_rows.near = together(arrived, token_rows.near)
    token_rows.relay()
    att_block, ffn_block = weight_blocks(where, arrived, out_master, down_master)
    att_ring = along_ring(att_block, 0)
    states = staged_call(
        states_kernel,
        [shape_of((6 * own, width), LOW)] * RING,
        where,
        [qkv_master, qkv_first, qkv_second, up_master, up_first, up_second],
        [pltpu.VMEM((6 * own, width), WIDE)],
        limit=12,
    )
    states = to_places(together(att_block, states)[1])
    att_ring, token_rows.crossed, token_rows.far, ffn_block, cot = together(
        att_ring, token_rows.crossed, token_rows.far, ffn_block, cotangent
    )
    token_blocks = token_rows.blocks()
    att_ring = along_ring(jnp.stack(att_ring), 1)
    cot_rows = Gather(cot[:half], cot[half:])
    ffn_ring = along_ring(ffn_block, 0)
    att_ring, ffn_ring, states = together(att_ring, ffn_ring, states)
    att_mine = by_chip(where, att_ring)
    att_theirs = send(att_mine, "c", 1)
    ffn_ring = along_ring(jnp.stack(ffn_ring), 1)
    w_qkv, w_out, vecs = attention_weights(where, att_mine, att_theirs)
    w_qkv, cot_rows.near = together(w_qkv, cot_rows.near)
    cot_rows.relay()
    one, penalty = whole_call(
        images_kernel, [shape_of((group, LANES), LOW)] * 2, seg_counts, [], limit=8
    )

    normed, qkv = whole_call(
        first_kernel,
        [group_low, shape_of((group, 3 * lanes), LOW)],
        where,
        [vecs, w_qkv, *token_blocks],
        limit=10,
        micros=3.0,
    )
    attended, log_total, right, left = attend(where, LEAVING, qkv, one, penalty, w_out)
    right, left, qkv_again, ffn_ring, cot_rows.far, cot_rows.crossed = together(
        right, left, qkv, ffn_ring, cot_rows.far, cot_rows.crossed
    )
    cot_blocks = cot_rows.blocks()
    attended_too, log_total_too, *staying = attend(where, STAYING, qkv_again, one, penalty, w_out)
    arrivals, _ = scatter_z(right, left, staying)
    ffn_mine = by_chip(where, ffn_ring)
    ffn_theirs = send(ffn_mine, "c", 1)
    middle, *mid_halves = whole_call(
        middle_kernel,
        [wide_rows, half_rows, half_rows],
        None,
        [tokens, vecs, *arrivals],
        limit=6,
    )

    mid_rows = Gather(*mid_halves)
    w_up, w_down = ffn_weights(where, ffn_mine, ffn_theirs)
    w_up, w_down, mid_rows.near = together(w_up, w_down, mid_rows.near)
    mid_rows.relay()
    mid_blocks = mid_rows.blocks()
    near, far = [0, 1, 2, 3, 6, 7], [4, 5]
    wide_half = shape_of((half, width), WIDE)
    some = shape_of((3 * rows, hidden_lanes), LOW)
    column = shape_of((1, hidden_lanes), WIDE)
    near_outs = whole_call(
        hidden_near_kernel,
        [some] * 3 + [column, wide_rows, wide_half, wide_half, half_rows, half_rows],
        where,
        [vecs, w_up, w_down, *(cot_blocks[k] for k in near), *(mid_blocks[k] for k in near)],
        limit=20,
        micros=6.5,
    )
    near_outs, far_blocks = together(near_outs, [mid_blocks[k] for k in far])
    *near_rows, up_column, wide_own, after_low, before_high, after_high, before_low = near_outs
    *far_rows, up_column, right, left = whole_call(
        hidden_far_kernel,
        [low_rows] * 3 + [column, low_rows, low_rows],
        where,
        [vecs, w_up, w_down, *(cot_blocks[k] for k in far), *far_blocks]
        + [up_column, after_high, before_low],
        limit=14,
        micros=3.0,
    )
    ffn_piece = (chips, 2 * own, RING * width)
    ffn_keep, ffn_give = whole_call(
        ffn_grads_kernel,
        [shape_of(ffn_piece, WIDE), shape_of(ffn_piece, LOW)],
        where,
        [block for pair in zip(near_rows, far_rows) for block in pair]
        + [cot_blocks[k] for k in near + far],
        [pltpu.VMEM((2 * chips, *ffn_piece[1:]), WIDE)],
        limit=32,
        micros=6.5,
    )
    arrivals, (ffn_keep, ffn_give) = scatter_z(
        right, left, [wide_own, after_low, before_high], (ffn_keep, ffn_give)
    )
    ffn_own, *ffn_gone = core_sum(where, ffn_keep, send(ffn_give, "c", 1), 2.0)
    ffn_arrived = back_along_ring(ffn_own, ffn_gone, 0)
    arrivals, ffn_own = together(arrivals, ffn_own)
    grad_middle, *grad_halves, mid_sums = whole_call(
        grad_middle_kernel,
        [wide_rows, half_rows, half_rows, shape_of((8, width), WIDE)],
        None,
        [middle, cotangent, vecs, *arrivals],
        limit=8,
    )
    grad_rows = Gather(*grad_halves)
    out_own, out_after, out_before, out_right, out_left = whole_call(
        project_kernel,
        [wide_rows, wide_half, wide_half, low_rows, low_rows],
        None,
        [near_rows[1], far_rows[1], w_down],
        limit=12,
        micros=2.5,
    )
    grad_rows.near, out_own = together(grad_rows.near, out_own)
    grad_rows.relay()

    grad_blocks = grad_rows.blocks()
    logs, attendeds = (log_total, log_total_too), (attended, attended_too)
    near_outs = attend_back(
        where, NEAR, qkv, one, penalty, w_out, logs, attendeds, [grad_blocks[k] for k in near]
    )
    near_outs, far_blocks = together(near_outs, [grad_blocks[k] for k in far])
    query_near, *earlier = near_outs
    query_far, grad_key, grad_value, grad_out = attend_back(
        where, FAR, qkv, one, penalty, w_out, logs, attendeds, far_blocks, earlier
    )
    query_far, ffn_arrived = together(query_far, ffn_arrived)
    two_low = shape_of((2 * rows, width), LOW)
    normed_own, normed_after, normed_before, right, left, first_sums = whole_call(
        back_product_kernel,
        [wide_rows, wide_half, wide_half, two_low, two_low, shape_of((8, width), WIDE)],
        where,
        [w_qkv, query_near, query_far, grad_key, grad_value, *token_blocks, out_right, out_left],
        limit=14,
        micros=3.0,
    )
    columns = 4 * lanes + LANES
    piece = (chips, RING * own, columns)
    att_keep, att_give = whole_call(
        grads_kernel,
        [shape_of(piece, WIDE), shape_of(piece, LOW)],
        where,
        [normed, query_near, query_far, grad_key, grad_value]
        + [grad_out, first_sums, mid_sums, up_column],
        [pltpu.VMEM((LANES, width), WIDE), pltpu.VMEM((2 * chips, *piece[1:]), WIDE)],
        limit=24,
        micros=3.0,
    )

    att_got = send(att_give, "c", 1)
    right, left, att_keep = together(right, left, att_keep)
    from_prev, from_next = send(right, "z", 1), send(left, "z", -1)
    att_own, *att_gone = core_sum(where, att_keep, att_got, 1.0)
    att_arrived = back_along_ring(att_own, att_gone, 0)
    sums_own, *sums_gone = ring_sum(att_arrived, ffn_arrived)
    sums_arrived = back_along_ring(sums_own, sums_gone, 1)
    home_piece = shape_of((own, 3 * lanes + LANES + hidden_lanes), WIDE)
    kinds = [
        shape_of(weight.shape, WIDE)
        for weight in (qkv_master, out_master, up_master, down_master, vec_master)
    ]
    *pieces, out_first_new, out_second_new, out_dir, down_first_new, down_second_new, down_dir = (
        staged_call(
            norms_kernel,
            [home_piece] * RING + [kinds[1]] * 3 + [kinds[3]] * 3,
            where,
            [*sums_arrived, *states]
            + [out_master, out_first, out_second, down_master, down_first, down_second],
            [pltpu.VMEM(piece[1:], WIDE), pltpu.VMEM(ffn_piece[1:], WIDE)],
            limit=12,
            micros=3.0,
        )
    )
    home = to_places(pieces)
    from_prev, from_next, pieces = together(from_prev, from_next, pieces)
    forth, back = whole_call(
        relay_kernel,
        [low_rows, low_rows],
        None,
        [from_prev, from_next, normed_after, normed_before, out_after, out_before],
        limit=10,
    )
    home, forth, back = together(home, forth, back)
    forth, back = send(forth, "z", 1), send(back, "z", -1)
    row = whole_call(
        row_kernel,
        shape_of((1, LANES), WIDE),
        where,
        home,
        [pltpu.VMEM((RING, 1, LANES), WIDE)],
        limit=4,
    )
    row, _ = sum_pairs(row, "x", 1)
    stepped =whole_call(
        adam_kernel,
        [kinds[0]] * 3 + [kinds[2]] * 3 + [kinds[4]] * 3,
        where,
        [*home, qkv_master, up_master, vec_master, qkv_first, up_first, vec_first]
        + [qkv_second, up_second, vec_second],
        [pltpu.VMEM(qkv_master.shape, WIDE), pltpu.VMEM(up_master.shape, WIDE)],
        limit=10,
    )
    row, stepped = sum_pairs(row, "x", 2, stepped)
    (
        qkv_first_new,
        qkv_second_new,
        qkv_dir,
        up_first_new,
        up_second_new,
        up_dir,
        vec_first_new,
        vec_second_new,
        vec_new,
    ) = stepped
    outputs = whole_call(
        outputs_kernel,
        [low_rows, low_rows],
        None,
        [tokens, grad_middle, middle, vecs, normed_own, out_own, from_prev, from_next, forth, back],
        limit=14,
    )
    row, _ = sum_pairs(row, "y", 1)
    row, outputs = sum_pairs(row, "y", 2, outputs)
    row, _ = sum_pairs(row, "c", 1)
    input_grad, layer_out = outputs
    *new_mats, matrix_norms = whole_call(
        update_kernel,
        kinds[:4] + [shape_of((4, 2), WIDE)],
        where,
        [row, qkv_master, out_master, up_master, down_master, qkv_dir, out_dir, up_dir, down_dir],
        limit=8,
    )
    return (
        layer_out,
        input_grad,
        *new_mats,
        qkv_first_new,
        out_first_new,
        up_first_new,
        down_first_new,
        qkv_second_new,
        out_second_new,
        up_second_new,
        down_second_new,
        vec_new,
        vec_first_new,
        vec_second_new,
        matrix_norms,
    )


def solution(mesh):
    sizes = (4, 4, 2, 4)
    physical = Mesh(mesh.devices.reshape(sizes), EVERY)
    patches = P(EVERY, None)
    shards = P(("z", *DATA), None)
    return jax.shard_map(
        on_device,
        mesh=physical,
        in_specs=(patches, patches, P(DATA, None)) + (shards,) * 15,
        out_specs=(patches, patches) + (shards,) * 15 + (P(),),
        check_vma=False,
    )
```

```python
import jax
import jax.numpy as jnp
from jax import lax
from jax.experimental import pallas as pl
from jax.experimental.pallas import tpu as pltpu
from jax.sharding import Mesh
from jax.sharding import PartitionSpec as P

HEADS = 16
HEAD_DIM = 64
STEP = 4

LN_EPS = 1e-06
BETA = 0.5
ADAM_EPS = 1e-06
DECAY = 0.01
RATE = 0.5
VEC_RATE = 0.2
GROUPS = 32

LOW = jnp.bfloat16
WIDE = jnp.float32
DATA = ("x", "y", "c")
EVERY = ("x", "y", "c", "z")
RING = 4
LANES = 128
VECS = 16
SUBLANES = 8
SCORE_SCALE = HEAD_DIM ** (-0.5)
MIB = 1 << 20


def send(block, axis, step):
    size = lax.axis_size(axis)
    return lax.ppermute(block, axis, [(i, (i + step) % size) for i in range(size)])


def together(*values):
    return lax.optimization_barrier(values)


class Gather:
    def __init__(self, low, high):
        self.own = [low, high]
        self.near = [send(low, "z", 1), send(high, "z", -1)]
        self.crossed = [send(high, "z", 1), send(low, "z", -1)]

    def relay(self):
        prev_low, next_high = self.near
        self.far = [send(prev_low, "z", 1), send(next_high, "z", -1)]

    def blocks(self):
        prev_low, next_high = self.near
        prev_high, next_low = self.crossed
        return [*self.own, next_low, next_high, *self.far, prev_low, prev_high]


def to_places(blocks):
    return [blocks[0]] + [send(blocks[RING - k], "z", RING - k) for k in range(1, RING)]


def scatter_z(right, left, staying, meanwhile=()):
    from_prev, from_next, staying, meanwhile = together(
        send(right, "z", 1), send(left, "z", -1), staying, meanwhile
    )
    own, after_low, before_high = staying
    half = after_low.shape[0]
    prev_low = send((after_low + from_prev[:half].astype(WIDE)).astype(LOW), "z", 1)
    next_high = send((before_high + from_next[:half].astype(WIDE)).astype(LOW), "z", -1)
    return [own, from_prev, from_next, prev_low, next_high], meanwhile


def sum_pairs(values, axis, apart, meanwhile=()):
    pairs = [(i, i ^ apart) for i in range(lax.axis_size(axis))]
    other, meanwhile = together(lax.ppermute(values, axis, pairs), meanwhile)
    return values + other, meanwhile


def send_split(block, phase, step):
    sizes = [lax.axis_size(axis) for axis in DATA]
    pairs = []
    for x in range(sizes[0]):
        for y in range(sizes[1]):
            for c in range(sizes[2]):
                if c == phase:
                    to = ((x + step) % sizes[0], y)
                else:
                    to = (x, (y + step) % sizes[1])
                pairs.append(
                    ((x * sizes[1] + y) * sizes[2] + c, (to[0] * sizes[1] + to[1]) * sizes[2] + c)
                )
    return lax.ppermute(block, DATA, pairs)


def dot(left, right, dims):
    return lax.dot_general(left, right, (dims, ((), ())), preferred_element_type=WIDE)


NN = ((1,), (0,))
NT = ((1,), (1,))
TN = ((0,), (0,))


def shape_of(shape, dtype):
    return jax.ShapeDtypeStruct(shape, dtype)


def takes(micros):
    return pl.CostEstimate(
        flops=int(micros * 1e9), bytes_accessed=int(micros * 3e6), transcendentals=0
    )


def whole_call(kernel, out_shape, scalars, arrays, scratch=(), limit=40, micros=1.0):
    in_specs = [pl.BlockSpec(memory_space=pltpu.SMEM)] * (scalars is not None)
    operands = ([scalars] if scalars is not None else []) + list(arrays)
    many = isinstance(out_shape, list)
    vmem = pl.BlockSpec(memory_space=pltpu.VMEM)
    return pl.pallas_call(
        kernel,
        out_shape=out_shape,
        in_specs=in_specs + [vmem] * len(arrays),
        out_specs=[vmem] * len(out_shape) if many else vmem,
        scratch_shapes=list(scratch),
        compiler_params=pltpu.CompilerParams(vmem_limit_bytes=limit * MIB),
        cost_estimate=takes(micros),
    )(*operands)


def staged_call(
    kernel, out_shape, scalars, arrays, scratch=(), limit=24, micros=1.0, last_rows=()
):
    count, total = len(arrays), len(arrays) + len(out_shape)
    last_rows = dict(last_rows)
    shapes = [(last_rows.get(k, array.shape[0]), *array.shape[1:]) for k, array in enumerate(arrays)]

    def body(*refs):
        scalar, refs = refs[:1], refs[1:]
        given, rest = refs[:total], refs[total:]
        held, sems, rest = rest[:total], rest[total], rest[total + 1 :]
        copies = [
            pltpu.make_async_copy(
                given[k].at[pl.ds(arrays[k].shape[0] - shapes[k][0], shapes[k][0])], held[k], sems.at[k]
            )
            if k < count
            else pltpu.make_async_copy(held[k], given[k], sems.at[k])
            for k in range(total)
        ]
        for copy in copies[:count]:
            copy.start()
        for copy in copies[:count]:
            copy.wait()
        kernel(*scalar, *held, *rest)
        for copy in copies[count:]:
            copy.start()
        for copy in copies[count:]:
            copy.wait()

    anywhere = pl.BlockSpec(memory_space=pl.ANY)
    holds = [pltpu.VMEM(shape, array.dtype) for shape, array in zip(shapes, arrays)]
    holds += [pltpu.VMEM(array.shape, array.dtype) for array in out_shape]
    return pl.pallas_call(
        body,
        out_shape=out_shape,
        in_specs=[pl.BlockSpec(memory_space=pltpu.SMEM)] + [anywhere] * count,
        out_specs=[anywhere] * len(out_shape),
        scratch_shapes=holds + [pltpu.SemaphoreType.DMA((total,))] + list(scratch),
        compiler_params=pltpu.CompilerParams(vmem_limit_bytes=limit * MIB),
        cost_estimate=takes(micros),
    )(scalars, *arrays)


def pick_kernel(where, qkv, up, vec, *outs):
    lanes, wide = qkv.shape[1] // (3 * RING), up.shape[1] // RING
    for step in range(RING):
        place = (where[3] + step) % RING
        for third in range(3):
            at = pl.multiple_of(third * lanes * RING + place * lanes, lanes)
            outs[step][:, third * lanes : (third + 1) * lanes] = qkv[:, pl.ds(at, lanes)]
        outs[step][:, 3 * lanes : 3 * lanes + LANES] = jnp.zeros((qkv.shape[0], LANES), WIDE)
        outs[step][:, 3 * lanes : 3 * lanes + vec.shape[1]] = vec[...]
        outs[step][:, 3 * lanes + LANES :] = up[:, pl.ds(pl.multiple_of(place * wide, wide), wide)]


def collect_kernel(where, own, first, second, third, out, keep, give, hold):
    core, place = where[2], where[3]
    columns = own.shape[1]
    for step, piece in enumerate((own, first, second, third)):
        hold[(place + step) % RING] = piece[...]
    lanes = out.shape[1] // RING
    for half in range(2):
        for target, side in ((keep, core), (give, 1 - core)):
            at = side * 2 + half
            target[half, :, :columns] = hold[at]
            target[half, :, columns:] = out[:, pl.ds(pl.multiple_of(at * lanes, lanes), lanes)]


def pair_kernel(where, mine, theirs, down, att, ffn):
    first = where[2] == 0
    wide = ffn.shape[2]
    narrow = 3 * (att.shape[2] - LANES) // 4 + LANES
    for half in range(2):
        low = jnp.where(first, mine[half], theirs[half])
        high = jnp.where(first, theirs[half], mine[half])
        block = jnp.concatenate([low, high], axis=0).astype(LOW)
        att[half, :, :narrow] = block[:, :narrow]
        att[half, :, narrow:] = block[:, narrow + wide :]
        ffn[half] = block[:, narrow : narrow + wide]
        rows = ffn.shape[1]
        ffn[2 + half] = down[half * rows : (half + 1) * rows].astype(LOW)


def chip_of(where, first, second):
    x, y, c = where[0], where[1], where[2]
    along_x = (x + jnp.where(c == 0, first, second)) % RING
    along_y = (y + jnp.where(c == 0, second, first)) % RING
    return along_x * RING + along_y


def place_kernel(where, *refs):
    out = refs[-1]
    for second in range(RING):
        for first in range(RING):
            out[:, chip_of(where, first, second)] = refs[second][first]


def weights_kernel(where, mine, theirs, qkv, out, vecs):
    first = where[2] == 0
    rows, columns = mine.shape
    lanes = out.shape[0]
    for half in range(2):
        block = (
            jnp.where(first, mine[...], theirs[...])
            if half == 0
            else jnp.where(first, theirs[...], mine[...])
        )
        qkv[half * rows : (half + 1) * rows] = block[:, : 3 * lanes]
        vec = block[:, 3 * lanes : 3 * lanes + LANES].astype(WIDE)
        vecs[:, half * rows : (half + 1) * rows] = vec.T[:VECS]
        for part in range(2):
            at = (2 * half + part) * lanes
            out[:, at : at + lanes] = block[part * lanes : (part + 1) * lanes, columns - lanes :]


def ffn_weights_kernel(where, mine, theirs, up, down):
    first = where[2] == 0
    for half in range(2):
        up[half] = jnp.where(first, mine[half], theirs[half])
        up[2 + half] = jnp.where(first, theirs[half], mine[half])
        down[:, half] = jnp.where(first, mine[2 + half], theirs[2 + half])
        down[:, 2 + half] = jnp.where(first, theirs[2 + half], mine[2 + half])


def along_ring(block, phase):
    return [block] + [send_split(block, phase, -k) for k in range(1, RING)]


def by_chip(where, blocks):
    parts, rows, columns = blocks[0].shape[1:]
    return whole_call(
        place_kernel,
        shape_of((parts, RING * RING, rows, columns), LOW),
        where,
        blocks,
        limit=6,
    )


def weight_pieces(where, qkv_master, up_master, vec_master):
    columns = 3 * (qkv_master.shape[1] // (3 * RING)) + LANES + up_master.shape[1] // RING
    pieces = whole_call(
        pick_kernel,
        [shape_of((qkv_master.shape[0], columns), WIDE)] * RING,
        where,
        [qkv_master, up_master, vec_master],
        limit=8,
    )
    return pieces


def weight_blocks(where, arrived, out_master, down_master):
    own, columns = arrived[0].shape
    lanes = out_master.shape[1] // RING
    wide = columns - 3 * lanes - LANES
    half = shape_of((2, own, columns + lanes), WIDE)
    keep, give = whole_call(
        collect_kernel,
        [half, half],
        where,
        [*arrived, out_master],
        [pltpu.VMEM((RING, own, columns), WIDE)],
        limit=4,
    )
    return whole_call(
        pair_kernel,
        [
            shape_of((2, 2 * own, 4 * lanes + LANES), LOW),
            shape_of((4, 2 * own, wide), LOW),
        ],
        where,
        [keep, send(give, "c", 1), down_master],
        limit=4,
    )


def attention_weights(where, mine, theirs):
    halves, chips, rows, columns = mine.shape
    lanes = (columns - LANES) // 4
    flat = (halves * chips * rows, columns)
    return whole_call(
        weights_kernel,
        [
            shape_of((2 * flat[0], 3 * lanes), LOW),
            shape_of((lanes, RING * lanes), LOW),
            shape_of((VECS, RING * lanes), WIDE),
        ],
        where,
        [mine.reshape(flat), theirs.reshape(flat)],
        limit=10,
    )


def ffn_weights(where, mine, theirs):
    parts, chips, rows, columns = mine.shape
    up, down = whole_call(
        ffn_weights_kernel,
        [shape_of((parts, chips, rows, columns), LOW), shape_of((chips, parts, rows, columns), LOW)],
        where,
        [mine, theirs],
        limit=12,
    )
    flat = (parts * chips * rows, columns)
    return up.reshape(flat), down.reshape(flat)


def arrange_kernel(where, kept, arrived, own, *gone):
    for second in range(RING):
        for first in range(RING):
            chip = chip_of(where, first, second)
            total = kept[chip] + arrived[chip].astype(WIDE)
            if first == 0:
                own[second] = total
            else:
                gone[first - 1][second] = total.astype(LOW)


def core_sum(where, kept, arrived, micros):
    piece = (RING, *kept.shape[1:])
    return whole_call(
        arrange_kernel,
        [shape_of(piece, WIDE)] + [shape_of(piece, LOW)] * 3,
        where,
        [kept, arrived],
        limit=20,
        micros=micros,
    )


def sum_kernel(*refs):
    att, ffn, out, gone = refs[0:4], refs[4:8], refs[8], refs[9:12]
    rows, wide = ffn[0].shape[1:]
    columns = att[0].shape[2]
    for k in range(RING):
        target = out if k == 0 else gone[k - 1]
        target[:, :wide] = sum(part[k].astype(WIDE) for part in ffn).astype(target.dtype)
        total = sum(part[k].astype(WIDE) for part in att).astype(target.dtype)
        target[:, wide : wide + columns] = total[:rows]
        target[:, wide + columns :] = total[rows:]


def back_along_ring(own, gone, phase):
    return [own] + [send_split(gone[k - 1], phase, k) for k in range(1, RING)]


def ring_sum(att, ffn):
    rows, wide = ffn[0].shape[1:]
    shape = (rows, wide + 2 * att[0].shape[2])
    return whole_call(
        sum_kernel,
        [shape_of(shape, WIDE)] + [shape_of(shape, LOW)] * 3,
        None,
        [*att, *ffn],
        limit=16,
        micros=1.5,
    )


def stats_of(values):
    centre = jnp.mean(values, -1, keepdims=True)
    centred = values - centre
    spread = jnp.mean(centred * centred, -1, keepdims=True)
    lane = lax.broadcasted_iota(jnp.int32, (1, LANES), 1)
    return jnp.where(lane == 0, centre, lax.rsqrt(spread + LN_EPS))


def normalise(values):
    centre = jnp.mean(values, -1, keepdims=True)
    centred = values - centre
    spread = jnp.mean(centred * centred, -1, keepdims=True)
    scale = lax.rsqrt(spread + LN_EPS)
    return centred * scale, scale


def normalise_back(grad, unit, scale, gain):
    grad_unit = grad * gain
    return scale * (
        grad_unit
        - jnp.mean(grad_unit, -1, keepdims=True)
        - unit * jnp.mean(grad_unit * unit, -1, keepdims=True)
    )


def images_kernel(counts, one, penalty):
    row = lax.broadcasted_iota(jnp.int32, one.shape, 0)
    lane = lax.broadcasted_iota(jnp.int32, one.shape, 1) % HEAD_DIM
    first_end = counts[0, 0]
    second_end = first_end + counts[0, 1]
    image = (row >= first_end).astype(jnp.int32) + (row >= second_end).astype(jnp.int32)
    one[...] = jnp.where(lane == image, 1.0, 0.0).astype(LOW)
    penalty[...] = jnp.where((lane == image) | (lane >= 3), 0.0, -1e30).astype(LOW)


def both(blocks, step):
    return jnp.concatenate([blocks[2 * step][...], blocks[2 * step + 1][...]])


def first_kernel(where, vecs, weight, *refs):
    blocks, (normed, qkv, stats) = refs[:8], refs[8:]
    rows = 2 * blocks[0].shape[0]
    lanes = weight.shape[1] // 3
    at = pl.ds(pl.multiple_of(where[3] * lanes, lanes), lanes)
    bias = jnp.concatenate([vecs[2:3, at], jnp.zeros((1, lanes), WIDE), vecs[3:4, at]], axis=1)
    for step in range(RING):
        here = rows_of(where, step, rows)
        values = both(blocks, step).astype(WIDE)
        stats[step * rows : (step + 1) * rows] = stats_of(values)
        here_stats = stats[step * rows : (step + 1) * rows]
        unit = (values - here_stats[:, 0:1]) * here_stats[:, 1:2]
        block = (unit * vecs[0:1] + vecs[1:2]).astype(LOW)
        normed[here] = block
        qkv[here] = (dot(block, weight[...], NN) + bias).astype(LOW)


def scores_of(query, key, one, penalty, mine):
    return dot(jnp.where(mine, query, one), jnp.where(mine, key, penalty), NT)


LEAVING = ((4, 5), (3, 6))
STAYING = ((0, 1), (2, 7))
SPOT = {
    block: (call, place)
    for call, pairs in enumerate((LEAVING, STAYING))
    for place, block in enumerate(pairs[0] + pairs[1])
}


def rows_of(where, step, rows):
    return pl.ds(pl.multiple_of((where[3] + step) % RING * rows, rows), rows)


def half_block(where, ref, block):
    half = ref.shape[0] // (2 * RING)
    device = (where[3] + block // 2) % RING
    return ref[pl.ds(pl.multiple_of((2 * device + block % 2) * half, half), half)]


def attend_kernel(pairs, where, query, key, value, one, penalty, out, attended, log_total, *refs):
    pieces, total = refs[:-1], refs[-1]
    block = query.shape[0] // RING
    half = block // 2
    lane = lax.broadcasted_iota(jnp.int32, (1, LANES), 1)
    first = pl.program_id(0) == 0
    for group, blocks in enumerate(pairs):
        at = pl.ds(group * block, block)
        scaled = jnp.concatenate([half_block(where, query, k) for k in blocks]) * LOW(SCORE_SCALE)
        chosen = jnp.concatenate([half_block(where, one, k) for k in blocks])
        parts, logs = [], []
        for head in range(2):
            mine = lane // HEAD_DIM == head
            scores = scores_of(scaled, key[...], chosen, penalty[...], mine)
            top = jnp.max(scores, -1, keepdims=True)
            exponent = jnp.exp(scores - top)
            sums = jnp.sum(exponent, -1, keepdims=True)
            parts.append(dot(exponent.astype(LOW), value[...], NN) * (1.0 / sums))
            logs.append(top + jnp.log(sums))
        rounded = jnp.where(lane < HEAD_DIM, parts[0], parts[1]).astype(LOW)
        attended[at] = rounded
        log_total[at] = jnp.where(lane < HEAD_DIM, logs[0], logs[1])
        product = dot(rounded, out[...], NN)
        total[group] = jnp.where(first, product, total[group] + product)

    @pl.when(pl.program_id(0) == pl.num_programs(0) - 1)
    def _():
        if len(pieces) == 2:
            right, left = pieces
            right[:half] = total[0, :half].astype(LOW)
            left[:half] = total[0, half:].astype(LOW)
            right[half:] = total[1, :half].astype(LOW)
            left[half:] = total[1, half:].astype(LOW)
        else:
            own, after_low, before_high = pieces
            own[...] = total[0]
            after_low[...] = total[1, :half]
            before_high[...] = total[1, half:]


def by_pair(shape, offset=0):
    return pl.BlockSpec((shape[0], LANES), lambda j: (0, offset + j))


def whole(array):
    return pl.BlockSpec(array.shape, lambda j: (0,) * len(array.shape))


SCALARS = pl.BlockSpec(memory_space=pltpu.SMEM)


def attend(where, blocks, qkv, one, penalty, out):
    rows, lanes = qkv.shape[0], qkv.shape[1] // 3
    pairs, width, block = lanes // LANES, out.shape[1], rows // RING
    if blocks is LEAVING:
        pieces = [shape_of((block, width), LOW)] * 2
    else:
        pieces = [shape_of((block, width), WIDE)] + [shape_of((block // 2, width), WIDE)] * 2
    some = (2 * block, lanes)

    def kernel(*refs):
        attend_kernel(blocks, *refs)

    return pl.pallas_call(
        kernel,
        grid=(pairs,),
        in_specs=[SCALARS]
        + [by_pair(qkv.shape, k * pairs) for k in range(3)]
        + [whole(one), whole(penalty), pl.BlockSpec((LANES, width), lambda j: (j, 0))],
        out_specs=[by_pair(some)] * 2 + [whole(piece) for piece in pieces],
        out_shape=[shape_of(some, LOW), shape_of(some, WIDE)] + pieces,
        scratch_shapes=[pltpu.VMEM((2, block, width), WIDE)],
        compiler_params=pltpu.CompilerParams(vmem_limit_bytes=20 * MIB),
        cost_estimate=takes(7.0),
    )(where, qkv, qkv, qkv, one, penalty, out)


def attend_back_kernel(steps, where, query, key, value, one, penalty, out, *refs):
    log_totals, attendeds, refs = refs[0:2], refs[2:4], refs[4:]
    pieces, refs = refs[: 2 * len(steps)], refs[2 * len(steps) :]
    earlier = refs[:3] if len(refs) == 9 else None
    grad_query, grad_key, grad_value, grad_out, key_sum, value_sum = refs[-6:]
    block = query.shape[0] // RING
    half = block // 2
    lane = lax.broadcasted_iota(jnp.int32, (1, LANES), 1)

    def kept(arrays, step):
        spots = [SPOT[2 * step + k] for k in range(2)]
        return jnp.concatenate(
            [arrays[call][place * half : (place + 1) * half] for call, place in spots]
        )

    for place, step in enumerate(steps):
        here = rows_of(where, step, block)
        scaled = query[here] * LOW(SCORE_SCALE)
        grad_low = both(pieces, place)
        grad = dot(grad_low, out[...], NT).astype(LOW)
        logs = kept(log_totals, step)
        own_attended = kept(attendeds, step)
        part_out = dot(own_attended, grad_low, TN)
        weighted = own_attended.astype(WIDE) * grad.astype(WIDE)
        parts = []
        for head in range(2):
            mine = lane // HEAD_DIM == head
            scores = scores_of(scaled, key[...], one[here], penalty[...], mine)
            probs = jnp.exp(scores - logs[:, head * HEAD_DIM : head * HEAD_DIM + 1])
            grad_probs = dot(jnp.where(mine, grad, LOW(0.0)), value[...], NT)
            inner = jnp.sum(jnp.where(mine, weighted, 0.0), -1, keepdims=True)
            grad_scores = (probs * (grad_probs - inner)).astype(LOW)
            parts.append(dot(grad_scores, key[...], NN))
            for_value = dot(probs.astype(LOW), grad, TN)
            for_key = dot(grad_scores, scaled, TN)
            if place == 0:
                key_sum[head] = for_key
                value_sum[head] = for_value
            else:
                key_sum[head] += for_key
                value_sum[head] += for_value
        grad_query[place * block : (place + 1) * block] = (
            jnp.where(lane < HEAD_DIM, parts[0], parts[1]) * SCORE_SCALE
        ).astype(LOW)
        if place == 0:
            grad_out[...] = part_out
        else:
            grad_out[...] += part_out
    for_key = jnp.where(lane < HEAD_DIM, key_sum[0], key_sum[1])
    for_value = jnp.where(lane < HEAD_DIM, value_sum[0], value_sum[1])
    if earlier is not None:
        for_key = for_key + earlier[0][...]
        for_value = for_value + earlier[1][...]
        grad_out[...] += earlier[2][...]
    grad_key[...] = for_key.astype(grad_key.dtype)
    grad_value[...] = for_value.astype(grad_value.dtype)


def attend_back(where, steps, qkv, one, penalty, out, log_totals, attendeds, pieces, earlier=()):
    rows, lanes = qkv.shape[0], qkv.shape[1] // 3
    pairs, width, block = lanes // LANES, out.shape[1], rows // RING
    out_rows = pl.BlockSpec((LANES, width), lambda j: (j, 0))
    sums = LOW if earlier else WIDE
    group = (rows, lanes)
    some = (len(steps) * block, lanes)

    def kernel(*refs):
        attend_back_kernel(steps, *refs)

    return pl.pallas_call(
        kernel,
        grid=(pairs,),
        in_specs=[SCALARS]
        + [by_pair(qkv.shape, k * pairs) for k in range(3)]
        + [whole(one), whole(penalty), out_rows]
        + [by_pair(array.shape) for array in (*log_totals, *attendeds)]
        + [whole(piece) for piece in pieces]
        + ([by_pair(group)] * 2 + [out_rows] if earlier else []),
        out_specs=[by_pair(some), by_pair(group), by_pair(group), out_rows],
        out_shape=[
            shape_of(some, LOW),
            shape_of(group, sums),
            shape_of(group, sums),
            shape_of((lanes, width), WIDE),
        ],
        scratch_shapes=[pltpu.VMEM((2, rows, LANES), WIDE)] * 2,
        compiler_params=pltpu.CompilerParams(vmem_limit_bytes=24 * MIB),
        cost_estimate=takes(5.0 * len(steps)),
    )(where, qkv, qkv, qkv, one, penalty, out, *log_totals, *attendeds, *pieces, *earlier)


NEAR = (0, 1, 3)
FAR = (2,)


def project_kernel(near, far, weight, own, after_low, before_high, right, left):
    rows = far.shape[0]
    half = rows // 2
    own[...] = dot(near[:rows], weight[...], NN)
    block = dot(near[rows : 2 * rows], weight[...], NN)
    after_low[...] = block[:half]
    right[half:] = block[half:].astype(LOW)
    block = dot(near[2 * rows :], weight[...], NN)
    left[half:] = block[:half].astype(LOW)
    before_high[...] = block[half:]
    block = dot(far[...], weight[...], NN)
    right[:half] = block[:half].astype(LOW)
    left[:half] = block[half:].astype(LOW)


def arrived_sum(own, from_prev, from_next, prev_low, next_high):
    half = prev_low.shape[0]
    low = prev_low[...].astype(WIDE) + from_next[half:].astype(WIDE)
    high = from_prev[half:].astype(WIDE) + next_high[...].astype(WIDE)
    return own[...] + jnp.concatenate([low, high])


def middle_kernel(tokens, vecs, *refs):
    arrivals, (middle, low, high) = refs[:5], refs[5:]
    half = low.shape[0]
    middle[...] = tokens[...].astype(WIDE) + (arrived_sum(*arrivals) + vecs[4:5])
    unit, _ = normalise(middle[...])
    normed = (unit * vecs[5:6] + vecs[6:7]).astype(LOW)
    low[...] = normed[:half]
    high[...] = normed[half:]


def hidden_rows(where, vecs, up, down, cotangents, pieces, place, outs):
    normed, hidden, grad_pre, column = outs
    rows = 2 * pieces[0].shape[0]
    at = pl.ds(place * rows, rows)
    block = both(pieces, place)
    normed[at] = block
    pre_act = dot(block, up[...], NN) + vecs[pl.ds(7 + where[3], 1)]
    below = 0.5 * (1.0 + lax.erf(pre_act * (0.5**0.5)))
    hidden[at] = (pre_act * below).astype(LOW)
    slope = below + pre_act * (jnp.exp(-0.5 * pre_act * pre_act) * 0.3989422804014327)
    grad = (dot(both(cotangents, place), down[...], NT) * slope).astype(LOW)
    grad_pre[at] = grad
    column[...] += jnp.sum(grad.astype(WIDE), 0, keepdims=True)
    return dot(grad, up[...], NT)


def hidden_near_kernel(where, vecs, up, down, *refs):
    cotangents, pieces, outs = refs[:6], refs[6:12], refs[12:16]
    own, after_low, before_high, after_high, before_low = refs[16:]
    half = pieces[0].shape[0]
    outs[3][...] = jnp.zeros(outs[3].shape, WIDE)
    for place in range(3):
        block = hidden_rows(where, vecs, up, down, cotangents, pieces, place, outs)
        if place == 0:
            own[...] = block
        elif place == 1:
            after_low[...] = block[:half]
            after_high[...] = block[half:].astype(LOW)
        else:
            before_low[...] = block[:half].astype(LOW)
            before_high[...] = block[half:]


def hidden_far_kernel(where, vecs, up, down, *refs):
    cotangents, pieces, refs = refs[:2], refs[2:4], refs[4:]
    column, after_high, before_low, outs, (right, left) = refs[0], refs[1], refs[2], refs[3:7], refs[7:]
    half = pieces[0].shape[0]
    outs[3][...] = column[...]
    block = hidden_rows(where, vecs, up, down, cotangents, pieces, 0, outs)
    right[:half] = block[:half].astype(LOW)
    left[:half] = block[half:].astype(LOW)
    right[half:] = after_high[...]
    left[half:] = before_low[...]


def by_core(where, hold, keep, give):
    for chip in range(keep.shape[0]):
        keep[chip] = hold[2 * chip + where[2]]
        give[chip] = hold[2 * chip + 1 - where[2]].astype(LOW)


def ffn_grads_kernel(where, *refs):
    normed, hidden, grad_pre, cotangents, refs = refs[:2], refs[2:4], refs[4:6], refs[6:14], refs[14:]
    keep, give, hold = refs
    width = normed[0].shape[1]
    part = width // RING
    cot = [jnp.concatenate([block[...] for block in part]) for part in (cotangents[:6], cotangents[6:])]
    for k in range(RING):
        here = slice(k * part, (k + 1) * part)
        block = sum(dot(normed[p][:, here], grad_pre[p][...], TN) for p in range(2))
        hold[:, :SUBLANES, k * width : (k + 1) * width] = block.reshape(-1, SUBLANES, width)
        block = sum(dot(hidden[p][:, here], cot[p], TN) for p in range(2))
        block = block.reshape(-1, RING, SUBLANES, width)
        owners = block.shape[0]
        for q in range(RING):
            hold[k * owners : (k + 1) * owners, SUBLANES:, q * width : (q + 1) * width] = block[:, q]
    by_core(where, hold, keep, give)


def grad_middle_kernel(middle, cotangent, vecs, *refs):
    arrivals, (grad_middle, low, high, sums) = refs[:5], refs[5:]
    half = low.shape[0]
    grad = arrived_sum(*arrivals)
    unit, scale = normalise(middle[...])
    cot = cotangent[...].astype(WIDE)
    total = cot + normalise_back(grad, unit, scale, vecs[5:6])
    grad_middle[...] = total
    rounded = total.astype(LOW)
    low[...] = rounded[:half]
    high[...] = rounded[half:]
    sums[...] = jnp.concatenate(
        [
            jnp.sum(rounded.astype(WIDE), 0, keepdims=True),
            jnp.sum(grad * unit, 0, keepdims=True),
            jnp.sum(grad, 0, keepdims=True),
            jnp.sum(cot, 0, keepdims=True),
            jnp.zeros((4, cot.shape[1]), WIDE),
        ]
    )


def query_rows(near, far, step):
    rows = far.shape[0]
    if step in FAR:
        return far[...]
    place = NEAR.index(step)
    return near[place * rows : (place + 1) * rows]


def back_product_kernel(where, weight, query_near, query_far, grad_key, grad_value, *refs):
    blocks, stats, (other_right, other_left) = refs[:8], refs[8], refs[9:11]
    pieces, sums = refs[11:16], refs[16]
    own, after_low, before_high, right, left = pieces
    right[own.shape[0] :] = other_right[...]
    left[own.shape[0] :] = other_left[...]
    lanes = query_far.shape[1]
    rows = own.shape[0]
    half = rows // 2
    for step in range(RING):
        here = rows_of(where, step, rows)
        block = dot(query_rows(query_near, query_far, step), weight[:, :lanes], NT)
        block += dot(grad_key[here], weight[:, lanes : 2 * lanes], NT)
        block += dot(grad_value[here], weight[:, 2 * lanes :], NT)
        if step == 0:
            own[...] = block
        elif step == 1:
            after_low[...] = block[:half]
            right[half:rows] = block[half:].astype(LOW)
        elif step == 2:
            right[:half] = block[:half].astype(LOW)
            left[:half] = block[half:].astype(LOW)
        else:
            before_high[...] = block[half:]
            left[half:rows] = block[:half].astype(LOW)
        row_stats = stats[step * rows : (step + 1) * rows]
        unit = (both(blocks, step).astype(WIDE) - row_stats[:, 0:1]) * row_stats[:, 1:2]
        pair = jnp.concatenate(
            [
                jnp.sum(block * unit, 0, keepdims=True),
                jnp.sum(block, 0, keepdims=True),
                jnp.zeros((6, block.shape[1]), WIDE),
            ]
        )
        if step == 0:
            sums[...] = pair
        else:
            sums[...] += pair


def grads_kernel(
    where,
    normed,
    query_near,
    query_far,
    grad_key,
    grad_value,
    grad_out,
    first_sums,
    sums,
    column,
    keep,
    give,
    vecs,
    hold,
):
    rows, lanes = query_far.shape
    queries = [query_rows(query_near, query_far, step) for step in range(RING)]
    vecs[...] = jnp.zeros(vecs.shape, WIDE)
    at = pl.ds(pl.multiple_of(where[3] * lanes, lanes), lanes)
    vecs[0:2] = first_sums[0:2]
    vecs[2:3, at] = sum(jnp.sum(block.astype(WIDE), 0, keepdims=True) for block in queries)
    vecs[3:4, at] = jnp.sum(grad_value[...].astype(WIDE), 0, keepdims=True)
    vecs[4:7] = sums[0:3]
    for k in range(RING):
        vecs[7 + k : 8 + k] = jnp.where(where[3] == k, column[...], 0.0)
    vecs[11:12] = sums[3:4]
    for part in range(RING):
        here = slice(part * lanes, (part + 1) * lanes)
        left = normed[:, here]
        block = jnp.concatenate(
            [sum(dot(normed[rows_of(where, k, rows), here], queries[k], TN) for k in range(RING))]
            + [dot(left, third[...], TN) for third in (grad_key, grad_value)]
            + [vecs[:, here].T, grad_out[:, here]],
            axis=1,
        )
        hold[:, part * SUBLANES : (part + 1) * SUBLANES] = block.reshape(
            -1, SUBLANES, block.shape[1]
        )
    by_core(where, hold, keep, give)


def relay_kernel(from_prev, from_next, after, before, other_after, other_before, forth, back):
    half = after.shape[0]
    for place, (right, left) in enumerate(((after, before), (other_after, other_before))):
        here, there = pl.ds(2 * place * half, half), pl.ds(place * half, half)
        forth[there] = (right[...] + from_prev[here].astype(WIDE)).astype(LOW)
        back[there] = (left[...] + from_next[here].astype(WIDE)).astype(LOW)


def outputs_kernel(
    tokens, grad_middle, middle, vecs, own, other, from_prev, from_next, prev, following, grad, out
):
    half = own.shape[0] // 2
    sums = []
    for place, mine in enumerate((own, other)):
        at = pl.ds((2 * place + 1) * half, half)
        here = pl.ds(place * half, half)
        low = prev[here].astype(WIDE) + from_next[at].astype(WIDE)
        high = from_prev[at].astype(WIDE) + following[here].astype(WIDE)
        sums.append(mine[...] + jnp.concatenate([low, high]))
    unit, scale = normalise(tokens[...].astype(WIDE))
    grad[...] = (grad_middle[...] + normalise_back(sums[0], unit, scale, vecs[0:1])).astype(LOW)
    out[...] = (middle[...] + (sums[1] + vecs[11:12])).astype(LOW)


def states_kernel(where, *refs):
    qkv, up, outs, hold = refs[0:3], refs[3:6], refs[6:10], refs[10]
    own, lanes, wide = qkv[0].shape[0], qkv[0].shape[1] // (3 * RING), up[0].shape[1] // RING
    hold[...] = jnp.zeros(hold.shape, WIDE)
    for step in range(RING):
        place = (where[3] + step) % RING
        for kind in range(3):
            at = pl.ds(pl.multiple_of(place * wide, wide), wide)
            hold[kind * own : (kind + 1) * own] = up[kind][:, at]
            there = slice((3 + kind) * own, (4 + kind) * own)
            for third in range(3):
                at = pl.ds(pl.multiple_of(third * lanes * RING + place * lanes, lanes), lanes)
                hold[there, third * lanes : (third + 1) * lanes] = qkv[kind][:, at]
        outs[step][...] = hold[...].astype(LOW)


def adam_step(grad_mean, moment, square, weight, decay_rate):
    moment_new = BETA * moment + (1.0 - BETA) * grad_mean
    square_new = BETA * square + (1.0 - BETA) * grad_mean * grad_mean
    correct = 1.0 - BETA**STEP
    direction = (
        moment_new / correct / (jnp.sqrt(square_new / correct) + ADAM_EPS) + decay_rate * weight
    )
    return (moment_new, square_new, direction)


def row_of(values):
    lane = lax.broadcasted_iota(jnp.int32, (1, LANES), 1)
    return sum(jnp.where(lane == k, value, 0.0) for k, value in enumerate(values))


def ring_totals(parts):
    return (parts[0][...] + parts[1][...].astype(WIDE)) + (
        parts[2][...].astype(WIDE) + parts[3][...].astype(WIDE)
    )


def rows_sums(sums, ffn_sums, lanes):
    own, wide = ffn_sums.shape[0] // 2, ffn_sums.shape[1] // RING
    out_sum = jnp.concatenate(
        [sums[part * own : (part + 1) * own, -lanes:] for part in range(RING)], axis=1
    )
    down_sum = jnp.concatenate(
        [ffn_sums[own:, part * wide : (part + 1) * wide] for part in range(RING)]
    )
    return out_sum, down_sum


def norms_kernel(where, *refs):
    arrived, states, plain = refs[0:4], refs[4:8], refs[8:14]
    pieces, outs, sums, ffn_sums = refs[14:18], refs[18:24], refs[24], refs[25]
    own, wide = ffn_sums.shape[0] // 2, ffn_sums.shape[1] // RING
    lanes = (sums.shape[1] - LANES) // 4
    narrow = sums.shape[1] - lanes
    totals = ring_totals(arrived)
    width, columns = ffn_sums.shape[1], sums.shape[1]
    ffn_sums[...] = totals[:, :width]
    sums[: 2 * own] = totals[:, width : width + columns]
    sums[2 * own :] = totals[:, width + columns :]
    squares = [jnp.zeros((1, 1), WIDE)] * 8

    def add(k, weight, moment, square, grad, targets=()):
        results = adam_step(grad / GROUPS, moment, square, weight, DECAY)
        for target, result in zip(targets, results):
            target[...] = result
        direction = results[2]
        squares[k] = squares[k] + jnp.sum(weight * weight, keepdims=True)
        squares[4 + k] = squares[4 + k] + jnp.sum(direction * direction, keepdims=True)

    for step in range(RING):
        place = (where[3] + step) % RING
        at = pl.ds(pl.multiple_of(place * wide, wide), wide)
        here = pl.ds(pl.multiple_of(place * own, own), own)
        state = states[step][...].astype(WIDE)
        for k, grad in enumerate((ffn_sums[:own, at], sums[here, : 3 * lanes])):
            kinds = (
                state[(3 * k + kind) * own : (3 * k + kind + 1) * own, : grad.shape[1]]
                for kind in range(3)
            )
            add(2 - 2 * k, *kinds, grad)
    for k, grad in enumerate(rows_sums(sums, ffn_sums, lanes)):
        kinds = (plain[3 * k + kind][...] for kind in range(3))
        add(1 + 2 * k, *kinds, grad, outs[3 * k : 3 * k + 3])
    row = row_of([jnp.zeros((1, 1), WIDE)] * VECS + squares)
    for step in range(RING):
        place = (where[3] + step) % RING
        at = pl.ds(pl.multiple_of(place * wide, wide), wide)
        here = pl.ds(pl.multiple_of(place * own, own), own)
        pieces[step][:, :narrow] = sums[here, :narrow]
        pieces[step][:, 3 * lanes : narrow] += row
        pieces[step][:, narrow:] = ffn_sums[:own, at]


def row_kernel(where, *refs):
    pieces, row, hold = refs[:RING], refs[RING], refs[RING + 1]
    for step, piece in enumerate(pieces):
        lanes = (piece.shape[1] - LANES) // 7
        hold[(where[3] + step) % RING] = piece[0:1, 3 * lanes : 3 * lanes + LANES]
    row[...] = (hold[0] + hold[1]) + (hold[2] + hold[3])


def adam_kernel(where, *refs):
    home, refs = refs[:RING], refs[RING:]
    weights, moments, squares, outs = refs[0:3], refs[3:6], refs[6:9], refs[9:18]
    sums = refs[18:20]
    lanes, wide = sums[0].shape[1] // (3 * RING), sums[1].shape[1] // RING
    for step in range(RING):
        place = (where[3] + step) % RING
        for third in range(3):
            at = pl.multiple_of(third * lanes * RING + place * lanes, lanes)
            sums[0][:, pl.ds(at, lanes)] = home[step][:, third * lanes : (third + 1) * lanes]
        at = pl.ds(pl.multiple_of(place * wide, wide), wide)
        sums[1][:, at] = home[step][:, 3 * lanes + LANES :]
    columns = weights[2].shape[1]
    vec_sum = sum(home[step][:, 3 * lanes : 3 * lanes + LANES] for step in range(RING))
    for k, grad in enumerate((sums[0][...], sums[1][...], vec_sum[:, :columns])):
        weight = weights[k][...]
        moment, square, direction = adam_step(
            grad / GROUPS, moments[k][...], squares[k][...], weight, DECAY if k < 2 else 0.0
        )
        outs[3 * k][...] = moment
        outs[3 * k + 1][...] = square
        outs[3 * k + 2][...] = direction if k < 2 else weight - VEC_RATE * direction


def update_kernel(where, row, *refs):
    weights, directions, news, norms = refs[0:4], refs[4:8], refs[8:12], refs[12]
    root = jnp.sqrt(row[...])
    for k in range(4):
        weight_norm, update_norm = root[:, VECS + k : VECS + k + 1], root[:, VECS + 4 + k : VECS + 5 + k]
        norms[k : k + 1, 0:1] = weight_norm
        norms[k : k + 1, 1:2] = update_norm
        news[k][...] = weights[k][...] - RATE * (weight_norm / update_norm) * directions[k][...]


def on_device(
    tokens,
    cotangent,
    seg_counts,
    qkv_master,
    out_master,
    up_master,
    down_master,
    qkv_first,
    out_first,
    up_first,
    down_first,
    qkv_second,
    out_second,
    up_second,
    down_second,
    vec_master,
    vec_first,
    vec_second,
):
    where = jnp.stack([lax.axis_index(axis) for axis in EVERY]).astype(jnp.int32)
    rows, width = tokens.shape
    own = qkv_master.shape[0]
    lanes = width // RING
    hidden_lanes = up_master.shape[1] // RING
    chips = lax.axis_size("x") * lax.axis_size("y")
    group = rows * RING
    half = rows // 2
    wide_rows, half_rows = shape_of((rows, width), WIDE), shape_of((half, width), LOW)
    low_rows, group_low = shape_of((rows, width), LOW), shape_of((group, width), LOW)

    token_rows = Gather(tokens[:half], tokens[half:])
    arrived = to_places(weight_pieces(where, qkv_master, up_master, vec_master))
    arrived, token_rows.near = together(arrived, token_rows.near)
    token_rows.relay()
    att_block, ffn_block = weight_blocks(where, arrived, out_master, down_master)
    att_ring = along_ring(att_block, 0)
    states = staged_call(
        states_kernel,
        [shape_of((6 * own, width), LOW)] * RING,
        where,
        [qkv_master, qkv_first, qkv_second, up_master, up_first, up_second],
        [pltpu.VMEM((6 * own, width), WIDE)],
        limit=12,
    )
    states = to_places(together(att_block, states)[1])
    att_ring, token_rows.crossed, token_rows.far, ffn_block, cot = together(
        att_ring, token_rows.crossed, token_rows.far, ffn_block, cotangent
    )
    token_blocks = token_rows.blocks()
    att_ring = along_ring(jnp.stack(att_ring), 1)
    cot_rows = Gather(cot[:half], cot[half:])
    ffn_ring = along_ring(ffn_block, 0)
    att_ring, ffn_ring, states = together(att_ring, ffn_ring, states)
    att_mine = by_chip(where, att_ring)
    att_theirs = send(att_mine, "c", 1)
    ffn_ring = along_ring(jnp.stack(ffn_ring), 1)
    w_qkv, w_out, vecs = attention_weights(where, att_mine, att_theirs)
    w_qkv, cot_rows.near = together(w_qkv, cot_rows.near)
    cot_rows.relay()
    one, penalty = whole_call(
        images_kernel, [shape_of((group, LANES), LOW)] * 2, seg_counts, [], limit=8
    )

    normed, qkv, stats = whole_call(
        first_kernel,
        [group_low, shape_of((group, 3 * lanes), LOW), shape_of((group, LANES), WIDE)],
        where,
        [vecs, w_qkv, *token_blocks],
        limit=10,
        micros=3.0,
    )
    attended, log_total, right, left = attend(where, LEAVING, qkv, one, penalty, w_out)
    right, left, qkv_again, ffn_ring, cot_rows.far, cot_rows.crossed = together(
        right, left, qkv, ffn_ring, cot_rows.far, cot_rows.crossed
    )
    cot_blocks = cot_rows.blocks()
    attended_too, log_total_too, *staying = attend(where, STAYING, qkv_again, one, penalty, w_out)
    arrivals, _ = scatter_z(right, left, staying)
    ffn_mine = by_chip(where, ffn_ring)
    ffn_theirs = send(ffn_mine, "c", 1)
    middle, *mid_halves = whole_call(
        middle_kernel,
        [wide_rows, half_rows, half_rows],
        None,
        [tokens, vecs, *arrivals],
        limit=6,
    )

    mid_rows = Gather(*mid_halves)
    w_up, w_down = ffn_weights(where, ffn_mine, ffn_theirs)
    w_up, w_down, mid_rows.near = together(w_up, w_down, mid_rows.near)
    mid_rows.relay()
    mid_blocks = mid_rows.blocks()
    near, far = [0, 1, 2, 3, 6, 7], [4, 5]
    wide_half = shape_of((half, width), WIDE)
    some = shape_of((3 * rows, hidden_lanes), LOW)
    column = shape_of((1, hidden_lanes), WIDE)
    near_outs = whole_call(
        hidden_near_kernel,
        [some] * 3 + [column, wide_rows, wide_half, wide_half, half_rows, half_rows],
        where,
        [vecs, w_up, w_down, *(cot_blocks[k] for k in near), *(mid_blocks[k] for k in near)],
        limit=20,
        micros=6.5,
    )
    near_outs, far_blocks = together(near_outs, [mid_blocks[k] for k in far])
    *near_rows, up_column, wide_own, after_low, before_high, after_high, before_low = near_outs
    *far_rows, up_column, right, left = whole_call(
        hidden_far_kernel,
        [low_rows] * 3 + [column, low_rows, low_rows],
        where,
        [vecs, w_up, w_down, *(cot_blocks[k] for k in far), *far_blocks]
        + [up_column, after_high, before_low],
        limit=14,
        micros=3.0,
    )
    ffn_piece = (chips, 2 * own, RING * width)
    ffn_keep, ffn_give = whole_call(
        ffn_grads_kernel,
        [shape_of(ffn_piece, WIDE), shape_of(ffn_piece, LOW)],
        where,
        [block for pair in zip(near_rows, far_rows) for block in pair]
        + [cot_blocks[k] for k in near + far],
        [pltpu.VMEM((2 * chips, *ffn_piece[1:]), WIDE)],
        limit=32,
        micros=6.5,
    )
    arrivals, (ffn_keep, ffn_give) = scatter_z(
        right, left, [wide_own, after_low, before_high], (ffn_keep, ffn_give)
    )
    ffn_own, *ffn_gone = core_sum(where, ffn_keep, send(ffn_give, "c", 1), 2.0)
    ffn_arrived = back_along_ring(ffn_own, ffn_gone, 0)
    arrivals, ffn_own = together(arrivals, ffn_own)
    grad_middle, *grad_halves, mid_sums = whole_call(
        grad_middle_kernel,
        [wide_rows, half_rows, half_rows, shape_of((8, width), WIDE)],
        None,
        [middle, cotangent, vecs, *arrivals],
        limit=8,
    )
    grad_rows = Gather(*grad_halves)
    out_own, out_after, out_before, out_right, out_left = whole_call(
        project_kernel,
        [wide_rows, wide_half, wide_half, low_rows, low_rows],
        None,
        [near_rows[1], far_rows[1], w_down],
        limit=12,
        micros=2.5,
    )
    grad_rows.near, out_own = together(grad_rows.near, out_own)
    grad_rows.relay()

    grad_blocks = grad_rows.blocks()
    logs, attendeds = (log_total, log_total_too), (attended, attended_too)
    near_outs = attend_back(
        where, NEAR, qkv, one, penalty, w_out, logs, attendeds, [grad_blocks[k] for k in near]
    )
    near_outs, far_blocks = together(near_outs, [grad_blocks[k] for k in far])
    query_near, *earlier = near_outs
    query_far, grad_key, grad_value, grad_out = attend_back(
        where, FAR, qkv, one, penalty, w_out, logs, attendeds, far_blocks, earlier
    )
    query_far, ffn_arrived = together(query_far, ffn_arrived)
    two_low = shape_of((2 * rows, width), LOW)
    normed_own, normed_after, normed_before, right, left, first_sums = whole_call(
        back_product_kernel,
        [wide_rows, wide_half, wide_half, two_low, two_low, shape_of((8, width), WIDE)],
        where,
        [w_qkv, query_near, query_far, grad_key, grad_value, *token_blocks]
        + [stats, out_right, out_left],
        limit=14,
        micros=3.0,
    )
    columns = 4 * lanes + LANES
    piece = (chips, RING * own, columns)
    att_keep, att_give = whole_call(
        grads_kernel,
        [shape_of(piece, WIDE), shape_of(piece, LOW)],
        where,
        [normed, query_near, query_far, grad_key, grad_value]
        + [grad_out, first_sums, mid_sums, up_column],
        [pltpu.VMEM((LANES, width), WIDE), pltpu.VMEM((2 * chips, *piece[1:]), WIDE)],
        limit=24,
        micros=3.0,
    )

    att_got = send(att_give, "c", 1)
    right, left, att_keep = together(right, left, att_keep)
    from_prev, from_next = send(right, "z", 1), send(left, "z", -1)
    att_own, *att_gone = core_sum(where, att_keep, att_got, 1.0)
    att_arrived = back_along_ring(att_own, att_gone, 0)
    sums_own, *sums_gone = ring_sum(att_arrived, ffn_arrived)
    sums_arrived = back_along_ring(sums_own, sums_gone, 1)
    home_piece = shape_of((own, 3 * lanes + LANES + hidden_lanes), WIDE)
    kinds = [
        shape_of(weight.shape, WIDE)
        for weight in (qkv_master, out_master, up_master, down_master, vec_master)
    ]
    *pieces, out_first_new, out_second_new, out_dir, down_first_new, down_second_new, down_dir = (
        whole_call(
            norms_kernel,
            [home_piece] * RING + [kinds[1]] * 3 + [kinds[3]] * 3,
            where,
            [*sums_arrived, *states]
            + [out_master, out_first, out_second, down_master, down_first, down_second],
            [pltpu.VMEM(piece[1:], WIDE), pltpu.VMEM(ffn_piece[1:], WIDE)],
            limit=14,
            micros=3.0,
        )
    )
    home = to_places(pieces)
    from_prev, from_next, pieces = together(from_prev, from_next, pieces)
    forth, back = whole_call(
        relay_kernel,
        [low_rows, low_rows],
        None,
        [from_prev, from_next, normed_after, normed_before, out_after, out_before],
        limit=10,
    )
    home, forth, back = together(home, forth, back)
    forth, back = send(forth, "z", 1), send(back, "z", -1)
    row = whole_call(
        row_kernel,
        shape_of((1, LANES), WIDE),
        where,
        home,
        [pltpu.VMEM((RING, 1, LANES), WIDE)],
        limit=4,
    )
    row, _ = sum_pairs(row, "x", 1)
    stepped =whole_call(
        adam_kernel,
        [kinds[0]] * 3 + [kinds[2]] * 3 + [kinds[4]] * 3,
        where,
        [*home, qkv_master, up_master, vec_master, qkv_first, up_first, vec_first]
        + [qkv_second, up_second, vec_second],
        [pltpu.VMEM(qkv_master.shape, WIDE), pltpu.VMEM(up_master.shape, WIDE)],
        limit=10,
    )
    row, stepped = sum_pairs(row, "x", 2, stepped)
    (
        qkv_first_new,
        qkv_second_new,
        qkv_dir,
        up_first_new,
        up_second_new,
        up_dir,
        vec_first_new,
        vec_second_new,
        vec_new,
    ) = stepped
    outputs = whole_call(
        outputs_kernel,
        [low_rows, low_rows],
        None,
        [tokens, grad_middle, middle, vecs, normed_own, out_own, from_prev, from_next, forth, back],
        limit=14,
    )
    row, _ = sum_pairs(row, "y", 1)
    row, outputs = sum_pairs(row, "y", 2, outputs)
    row, _ = sum_pairs(row, "c", 1)
    input_grad, layer_out = outputs
    *new_mats, matrix_norms = whole_call(
        update_kernel,
        kinds[:4] + [shape_of((4, 2), WIDE)],
        where,
        [row, qkv_master, out_master, up_master, down_master, qkv_dir, out_dir, up_dir, down_dir],
        limit=8,
    )
    return (
        layer_out,
        input_grad,
        *new_mats,
        qkv_first_new,
        out_first_new,
        up_first_new,
        down_first_new,
        qkv_second_new,
        out_second_new,
        up_second_new,
        down_second_new,
        vec_new,
        vec_first_new,
        vec_second_new,
        matrix_norms,
    )


def solution(mesh):
    sizes = (4, 4, 2, 4)
    physical = Mesh(mesh.devices.reshape(sizes), EVERY)
    patches = P(EVERY, None)
    shards = P(("z", *DATA), None)
    return jax.shard_map(
        on_device,
        mesh=physical,
        in_specs=(patches, patches, P(DATA, None)) + (shards,) * 15,
        out_specs=(patches, patches) + (shards,) * 15 + (P(),),
        check_vma=False,
    )
```

```python
import jax
import jax.numpy as jnp
from jax import lax
from jax.experimental import pallas as pl
from jax.experimental.pallas import tpu as pltpu
from jax.sharding import Mesh
from jax.sharding import PartitionSpec as P

HEADS = 16
HEAD_DIM = 64
STEP = 4

LN_EPS = 1e-06
BETA = 0.5
ADAM_EPS = 1e-06
DECAY = 0.01
RATE = 0.5
VEC_RATE = 0.2
GROUPS = 32

LOW = jnp.bfloat16
WIDE = jnp.float32
DATA = ("x", "y", "c")
EVERY = ("x", "y", "c", "z")
RING = 4
LANES = 128
VECS = 16
SUBLANES = 8
SCORE_SCALE = HEAD_DIM ** (-0.5)
MIB = 1 << 20


def send(block, axis, step):
    size = lax.axis_size(axis)
    return lax.ppermute(block, axis, [(i, (i + step) % size) for i in range(size)])


def together(*values):
    return lax.optimization_barrier(values)


class Gather:
    def __init__(self, low, high):
        self.own = [low, high]
        self.near = [send(low, "z", 1), send(high, "z", -1)]
        self.crossed = [send(high, "z", 1), send(low, "z", -1)]

    def relay(self):
        prev_low, next_high = self.near
        self.far = [send(prev_low, "z", 1), send(next_high, "z", -1)]

    def blocks(self):
        prev_low, next_high = self.near
        prev_high, next_low = self.crossed
        return [*self.own, next_low, next_high, *self.far, prev_low, prev_high]


def to_places(blocks):
    return [blocks[0]] + [send(blocks[RING - k], "z", RING - k) for k in range(1, RING)]


def scatter_z(right, left, staying, meanwhile=()):
    from_prev, from_next, staying, meanwhile = together(
        send(right, "z", 1), send(left, "z", -1), staying, meanwhile
    )
    own, after_low, before_high = staying
    half = after_low.shape[0]
    prev_low = send((after_low + from_prev[:half].astype(WIDE)).astype(LOW), "z", 1)
    next_high = send((before_high + from_next[:half].astype(WIDE)).astype(LOW), "z", -1)
    return [own, from_prev, from_next, prev_low, next_high], meanwhile


def sum_pairs(values, axis, apart, meanwhile=()):
    pairs = [(i, i ^ apart) for i in range(lax.axis_size(axis))]
    other, meanwhile = together(lax.ppermute(values, axis, pairs), meanwhile)
    return values + other, meanwhile


def send_split(block, phase, step):
    sizes = [lax.axis_size(axis) for axis in DATA]
    pairs = []
    for x in range(sizes[0]):
        for y in range(sizes[1]):
            for c in range(sizes[2]):
                if c == phase:
                    to = ((x + step) % sizes[0], y)
                else:
                    to = (x, (y + step) % sizes[1])
                pairs.append(
                    ((x * sizes[1] + y) * sizes[2] + c, (to[0] * sizes[1] + to[1]) * sizes[2] + c)
                )
    return lax.ppermute(block, DATA, pairs)


def dot(left, right, dims):
    return lax.dot_general(left, right, (dims, ((), ())), preferred_element_type=WIDE)


NN = ((1,), (0,))
NT = ((1,), (1,))
TN = ((0,), (0,))


def shape_of(shape, dtype):
    return jax.ShapeDtypeStruct(shape, dtype)


def takes(micros):
    return pl.CostEstimate(
        flops=int(micros * 1e9), bytes_accessed=int(micros * 3e6), transcendentals=0
    )


def whole_call(kernel, out_shape, scalars, arrays, scratch=(), limit=40, micros=1.0):
    in_specs = [pl.BlockSpec(memory_space=pltpu.SMEM)] * (scalars is not None)
    operands = ([scalars] if scalars is not None else []) + list(arrays)
    many = isinstance(out_shape, list)
    vmem = pl.BlockSpec(memory_space=pltpu.VMEM)
    return pl.pallas_call(
        kernel,
        out_shape=out_shape,
        in_specs=in_specs + [vmem] * len(arrays),
        out_specs=[vmem] * len(out_shape) if many else vmem,
        scratch_shapes=list(scratch),
        compiler_params=pltpu.CompilerParams(vmem_limit_bytes=limit * MIB),
        cost_estimate=takes(micros),
    )(*operands)


def staged_call(
    kernel, out_shape, scalars, arrays, scratch=(), limit=24, micros=1.0, last_rows=()
):
    count, total = len(arrays), len(arrays) + len(out_shape)
    last_rows = dict(last_rows)
    shapes = [(last_rows.get(k, array.shape[0]), *array.shape[1:]) for k, array in enumerate(arrays)]

    def body(*refs):
        scalar, refs = refs[:1], refs[1:]
        given, rest = refs[:total], refs[total:]
        held, sems, rest = rest[:total], rest[total], rest[total + 1 :]
        copies = [
            pltpu.make_async_copy(
                given[k].at[pl.ds(arrays[k].shape[0] - shapes[k][0], shapes[k][0])], held[k], sems.at[k]
            )
            if k < count
            else pltpu.make_async_copy(held[k], given[k], sems.at[k])
            for k in range(total)
        ]
        for copy in copies[:count]:
            copy.start()
        for copy in copies[:count]:
            copy.wait()
        kernel(*scalar, *held, *rest)
        for copy in copies[count:]:
            copy.start()
        for copy in copies[count:]:
            copy.wait()

    anywhere = pl.BlockSpec(memory_space=pl.ANY)
    holds = [pltpu.VMEM(shape, array.dtype) for shape, array in zip(shapes, arrays)]
    holds += [pltpu.VMEM(array.shape, array.dtype) for array in out_shape]
    return pl.pallas_call(
        body,
        out_shape=out_shape,
        in_specs=[pl.BlockSpec(memory_space=pltpu.SMEM)] + [anywhere] * count,
        out_specs=[anywhere] * len(out_shape),
        scratch_shapes=holds + [pltpu.SemaphoreType.DMA((total,))] + list(scratch),
        compiler_params=pltpu.CompilerParams(vmem_limit_bytes=limit * MIB),
        cost_estimate=takes(micros),
    )(scalars, *arrays)


def pick_kernel(where, qkv, up, vec, *outs):
    lanes, wide = qkv.shape[1] // (3 * RING), up.shape[1] // RING
    for step in range(RING):
        place = (where[3] + step) % RING
        for third in range(3):
            at = pl.multiple_of(third * lanes * RING + place * lanes, lanes)
            outs[step][:, third * lanes : (third + 1) * lanes] = qkv[:, pl.ds(at, lanes)]
        outs[step][:, 3 * lanes : 3 * lanes + LANES] = jnp.zeros((qkv.shape[0], LANES), WIDE)
        outs[step][:, 3 * lanes : 3 * lanes + vec.shape[1]] = vec[...]
        outs[step][:, 3 * lanes + LANES :] = up[:, pl.ds(pl.multiple_of(place * wide, wide), wide)]


def collect_kernel(where, own, first, second, third, out, keep, give, hold):
    core, place = where[2], where[3]
    columns = own.shape[1]
    for step, piece in enumerate((own, first, second, third)):
        hold[(place + step) % RING] = piece[...]
    lanes = out.shape[1] // RING
    for half in range(2):
        for target, side in ((keep, core), (give, 1 - core)):
            at = side * 2 + half
            target[half, :, :columns] = hold[at]
            target[half, :, columns:] = out[:, pl.ds(pl.multiple_of(at * lanes, lanes), lanes)]


def pair_kernel(where, mine, theirs, down, att, ffn):
    first = where[2] == 0
    wide = ffn.shape[2]
    narrow = 3 * (att.shape[2] - LANES) // 4 + LANES
    for half in range(2):
        low = jnp.where(first, mine[half], theirs[half])
        high = jnp.where(first, theirs[half], mine[half])
        block = jnp.concatenate([low, high], axis=0).astype(LOW)
        att[half, :, :narrow] = block[:, :narrow]
        att[half, :, narrow:] = block[:, narrow + wide :]
        ffn[half] = block[:, narrow : narrow + wide]
        rows = ffn.shape[1]
        ffn[2 + half] = down[half * rows : (half + 1) * rows].astype(LOW)


def chip_of(where, first, second):
    x, y, c = where[0], where[1], where[2]
    along_x = (x + jnp.where(c == 0, first, second)) % RING
    along_y = (y + jnp.where(c == 0, second, first)) % RING
    return along_x * RING + along_y


def place_kernel(where, *refs):
    out = refs[-1]
    for second in range(RING):
        for first in range(RING):
            out[:, chip_of(where, first, second)] = refs[second][first]


def weights_kernel(where, mine, theirs, qkv, out, vecs):
    first = where[2] == 0
    rows, columns = mine.shape
    lanes = out.shape[0]
    for half in range(2):
        block = (
            jnp.where(first, mine[...], theirs[...])
            if half == 0
            else jnp.where(first, theirs[...], mine[...])
        )
        qkv[half * rows : (half + 1) * rows] = block[:, : 3 * lanes]
        vec = block[:, 3 * lanes : 3 * lanes + LANES].astype(WIDE)
        vecs[:, half * rows : (half + 1) * rows] = vec.T[:VECS]
        for part in range(2):
            at = (2 * half + part) * lanes
            out[:, at : at + lanes] = block[part * lanes : (part + 1) * lanes, columns - lanes :]


def ffn_weights_kernel(where, mine, theirs, up, down):
    first = where[2] == 0
    for half in range(2):
        up[half] = jnp.where(first, mine[half], theirs[half])
        up[2 + half] = jnp.where(first, theirs[half], mine[half])
        down[:, half] = jnp.where(first, mine[2 + half], theirs[2 + half])
        down[:, 2 + half] = jnp.where(first, theirs[2 + half], mine[2 + half])


def along_ring(block, phase):
    return [block] + [send_split(block, phase, -k) for k in range(1, RING)]


def by_chip(where, blocks):
    parts, rows, columns = blocks[0].shape[1:]
    return whole_call(
        place_kernel,
        shape_of((parts, RING * RING, rows, columns), LOW),
        where,
        blocks,
        limit=6,
    )


def weight_pieces(where, qkv_master, up_master, vec_master):
    columns = 3 * (qkv_master.shape[1] // (3 * RING)) + LANES + up_master.shape[1] // RING
    pieces = whole_call(
        pick_kernel,
        [shape_of((qkv_master.shape[0], columns), WIDE)] * RING,
        where,
        [qkv_master, up_master, vec_master],
        limit=8,
    )
    return pieces


def weight_blocks(where, arrived, out_master, down_master):
    own, columns = arrived[0].shape
    lanes = out_master.shape[1] // RING
    wide = columns - 3 * lanes - LANES
    half = shape_of((2, own, columns + lanes), WIDE)
    keep, give = whole_call(
        collect_kernel,
        [half, half],
        where,
        [*arrived, out_master],
        [pltpu.VMEM((RING, own, columns), WIDE)],
        limit=4,
    )
    return whole_call(
        pair_kernel,
        [
            shape_of((2, 2 * own, 4 * lanes + LANES), LOW),
            shape_of((4, 2 * own, wide), LOW),
        ],
        where,
        [keep, send(give, "c", 1), down_master],
        limit=4,
    )


def attention_weights(where, mine, theirs):
    halves, chips, rows, columns = mine.shape
    lanes = (columns - LANES) // 4
    flat = (halves * chips * rows, columns)
    return whole_call(
        weights_kernel,
        [
            shape_of((2 * flat[0], 3 * lanes), LOW),
            shape_of((lanes, RING * lanes), LOW),
            shape_of((VECS, RING * lanes), WIDE),
        ],
        where,
        [mine.reshape(flat), theirs.reshape(flat)],
        limit=10,
    )


def ffn_weights(where, mine, theirs):
    parts, chips, rows, columns = mine.shape
    up, down = whole_call(
        ffn_weights_kernel,
        [shape_of((parts, chips, rows, columns), LOW), shape_of((chips, parts, rows, columns), LOW)],
        where,
        [mine, theirs],
        limit=12,
    )
    flat = (parts * chips * rows, columns)
    return up.reshape(flat), down.reshape(flat)


def arrange_kernel(where, kept, arrived, own, *gone):
    for second in range(RING):
        for first in range(RING):
            chip = chip_of(where, first, second)
            total = kept[chip] + arrived[chip].astype(WIDE)
            if first == 0:
                own[second] = total
            else:
                gone[first - 1][second] = total.astype(LOW)


def core_sum(where, kept, arrived, micros):
    piece = (RING, *kept.shape[1:])
    return whole_call(
        arrange_kernel,
        [shape_of(piece, WIDE)] + [shape_of(piece, LOW)] * 3,
        where,
        [kept, arrived],
        limit=20,
        micros=micros,
    )


def sum_kernel(*refs):
    att, ffn, out, gone = refs[0:4], refs[4:8], refs[8], refs[9:12]
    rows, wide = ffn[0].shape[1:]
    columns = att[0].shape[2]
    for k in range(RING):
        target = out if k == 0 else gone[k - 1]
        target[:, :wide] = sum(part[k].astype(WIDE) for part in ffn).astype(target.dtype)
        total = sum(part[k].astype(WIDE) for part in att).astype(target.dtype)
        target[:, wide : wide + columns] = total[:rows]
        target[:, wide + columns :] = total[rows:]


def back_along_ring(own, gone, phase):
    return [own] + [send_split(gone[k - 1], phase, k) for k in range(1, RING)]


def ring_sum(att, ffn):
    rows, wide = ffn[0].shape[1:]
    shape = (rows, wide + 2 * att[0].shape[2])
    return whole_call(
        sum_kernel,
        [shape_of(shape, WIDE)] + [shape_of(shape, LOW)] * 3,
        None,
        [*att, *ffn],
        limit=16,
        micros=1.5,
    )


def stats_of(values):
    centre = jnp.mean(values, -1, keepdims=True)
    centred = values - centre
    spread = jnp.mean(centred * centred, -1, keepdims=True)
    lane = lax.broadcasted_iota(jnp.int32, (1, LANES), 1)
    return jnp.where(lane == 0, centre, lax.rsqrt(spread + LN_EPS))


def normalise(values):
    centre = jnp.mean(values, -1, keepdims=True)
    centred = values - centre
    spread = jnp.mean(centred * centred, -1, keepdims=True)
    scale = lax.rsqrt(spread + LN_EPS)
    return centred * scale, scale


def normalise_back(grad, unit, scale, gain):
    grad_unit = grad * gain
    return scale * (
        grad_unit
        - jnp.mean(grad_unit, -1, keepdims=True)
        - unit * jnp.mean(grad_unit * unit, -1, keepdims=True)
    )


def images_kernel(counts, one, penalty):
    row = lax.broadcasted_iota(jnp.int32, one.shape, 0)
    lane = lax.broadcasted_iota(jnp.int32, one.shape, 1) % HEAD_DIM
    first_end = counts[0, 0]
    second_end = first_end + counts[0, 1]
    image = (row >= first_end).astype(jnp.int32) + (row >= second_end).astype(jnp.int32)
    one[...] = jnp.where(lane == image, 1.0, 0.0).astype(LOW)
    penalty[...] = jnp.where((lane == image) | (lane >= 3), 0.0, -1e30).astype(LOW)


def both(blocks, step):
    return jnp.concatenate([blocks[2 * step][...], blocks[2 * step + 1][...]])


def first_kernel(where, vecs, weight, *refs):
    blocks, (normed, qkv, stats) = refs[:8], refs[8:]
    rows = 2 * blocks[0].shape[0]
    lanes = weight.shape[1] // 3
    at = pl.ds(pl.multiple_of(where[3] * lanes, lanes), lanes)
    bias = jnp.concatenate([vecs[2:3, at], jnp.zeros((1, lanes), WIDE), vecs[3:4, at]], axis=1)
    for step in range(RING):
        here = rows_of(where, step, rows)
        values = both(blocks, step).astype(WIDE)
        stats[step * rows : (step + 1) * rows] = stats_of(values)
        here_stats = stats[step * rows : (step + 1) * rows]
        unit = (values - here_stats[:, 0:1]) * here_stats[:, 1:2]
        block = (unit * vecs[0:1] + vecs[1:2]).astype(LOW)
        normed[here] = block
        qkv[here] = (dot(block, weight[...], NN) + bias).astype(LOW)


def scores_of(query, key, one, penalty, mine):
    return dot(jnp.where(mine, query, one), jnp.where(mine, key, penalty), NT)


LEAVING = ((4, 5), (3, 6))
STAYING = ((0, 1), (2, 7))
SPOT = {
    block: (call, place)
    for call, pairs in enumerate((LEAVING, STAYING))
    for place, block in enumerate(pairs[0] + pairs[1])
}


def rows_of(where, step, rows):
    return pl.ds(pl.multiple_of((where[3] + step) % RING * rows, rows), rows)


def half_block(where, ref, block):
    half = ref.shape[0] // (2 * RING)
    device = (where[3] + block // 2) % RING
    return ref[pl.ds(pl.multiple_of((2 * device + block % 2) * half, half), half)]


def attend_kernel(
    pairs, where, query, key, value, one, penalty, out, attended, log_total, exact, *refs
):
    pieces, total = refs[:-1], refs[-1]
    block = query.shape[0] // RING
    half = block // 2
    lane = lax.broadcasted_iota(jnp.int32, (1, LANES), 1)
    first = pl.program_id(0) == 0
    for group, blocks in enumerate(pairs):
        at = pl.ds(group * block, block)
        scaled = jnp.concatenate([half_block(where, query, k) for k in blocks]) * LOW(SCORE_SCALE)
        chosen = jnp.concatenate([half_block(where, one, k) for k in blocks])
        parts, logs = [], []
        for head in range(2):
            mine = lane // HEAD_DIM == head
            scores = scores_of(scaled, key[...], chosen, penalty[...], mine)
            top = jnp.max(scores, -1, keepdims=True)
            exponent = jnp.exp(scores - top)
            sums = jnp.sum(exponent, -1, keepdims=True)
            parts.append(dot(exponent.astype(LOW), value[...], NN) * (1.0 / sums))
            logs.append(top + jnp.log(sums))
        exact[at] = jnp.where(lane < HEAD_DIM, parts[0], parts[1])
        rounded = exact[at].astype(LOW)
        attended[at] = rounded
        log_total[at] = jnp.where(lane < HEAD_DIM, logs[0], logs[1])
        product = dot(rounded, out[...], NN)
        total[group] = jnp.where(first, product, total[group] + product)

    @pl.when(pl.program_id(0) == pl.num_programs(0) - 1)
    def _():
        if len(pieces) == 2:
            right, left = pieces
            right[:half] = total[0, :half].astype(LOW)
            left[:half] = total[0, half:].astype(LOW)
            right[half:] = total[1, :half].astype(LOW)
            left[half:] = total[1, half:].astype(LOW)
        else:
            own, after_low, before_high = pieces
            own[...] = total[0]
            after_low[...] = total[1, :half]
            before_high[...] = total[1, half:]


def by_pair(shape, offset=0):
    return pl.BlockSpec((shape[0], LANES), lambda j: (0, offset + j))


def whole(array):
    return pl.BlockSpec(array.shape, lambda j: (0,) * len(array.shape))


SCALARS = pl.BlockSpec(memory_space=pltpu.SMEM)


def attend(where, blocks, qkv, one, penalty, out):
    rows, lanes = qkv.shape[0], qkv.shape[1] // 3
    pairs, width, block = lanes // LANES, out.shape[1], rows // RING
    if blocks is LEAVING:
        pieces = [shape_of((block, width), LOW)] * 2
    else:
        pieces = [shape_of((block, width), WIDE)] + [shape_of((block // 2, width), WIDE)] * 2
    some = (2 * block, lanes)

    def kernel(*refs):
        attend_kernel(blocks, *refs)

    return pl.pallas_call(
        kernel,
        grid=(pairs,),
        in_specs=[SCALARS]
        + [by_pair(qkv.shape, k * pairs) for k in range(3)]
        + [whole(one), whole(penalty), pl.BlockSpec((LANES, width), lambda j: (j, 0))],
        out_specs=[by_pair(some)] * 3 + [whole(piece) for piece in pieces],
        out_shape=[shape_of(some, LOW)] + [shape_of(some, WIDE)] * 2 + pieces,
        scratch_shapes=[pltpu.VMEM((2, block, width), WIDE)],
        compiler_params=pltpu.CompilerParams(vmem_limit_bytes=20 * MIB),
        cost_estimate=takes(7.0),
    )(where, qkv, qkv, qkv, one, penalty, out)


def attend_back_kernel(steps, where, query, key, value, one, penalty, out, *refs):
    log_totals, attendeds, exacts, refs = refs[0:2], refs[2:4], refs[4:6], refs[6:]
    pieces, refs = refs[: 2 * len(steps)], refs[2 * len(steps) :]
    earlier = refs[:3] if len(refs) == 9 else None
    grad_query, grad_key, grad_value, grad_out, key_sum, value_sum = refs[-6:]
    block = query.shape[0] // RING
    half = block // 2
    lane = lax.broadcasted_iota(jnp.int32, (1, LANES), 1)

    def kept(arrays, step):
        spots = [SPOT[2 * step + k] for k in range(2)]
        return jnp.concatenate(
            [arrays[call][place * half : (place + 1) * half] for call, place in spots]
        )

    for place, step in enumerate(steps):
        here = rows_of(where, step, block)
        scaled = query[here] * LOW(SCORE_SCALE)
        grad_low = both(pieces, place)
        grad = dot(grad_low, out[...], NT).astype(LOW)
        logs = kept(log_totals, step)
        part_out = dot(kept(attendeds, step), grad_low, TN)
        weighted = kept(exacts, step) * grad.astype(WIDE)
        parts = []
        for head in range(2):
            mine = lane // HEAD_DIM == head
            scores = scores_of(scaled, key[...], one[here], penalty[...], mine)
            probs = jnp.exp(scores - logs[:, head * HEAD_DIM : head * HEAD_DIM + 1])
            grad_probs = dot(jnp.where(mine, grad, LOW(0.0)), value[...], NT)
            inner = jnp.sum(jnp.where(mine, weighted, 0.0), -1, keepdims=True)
            grad_scores = (probs * (grad_probs - inner)).astype(LOW)
            parts.append(dot(grad_scores, key[...], NN))
            for_value = dot(probs.astype(LOW), grad, TN)
            for_key = dot(grad_scores, scaled, TN)
            if place == 0:
                key_sum[head] = for_key
                value_sum[head] = for_value
            else:
                key_sum[head] += for_key
                value_sum[head] += for_value
        grad_query[place * block : (place + 1) * block] = (
            jnp.where(lane < HEAD_DIM, parts[0], parts[1]) * SCORE_SCALE
        ).astype(LOW)
        if place == 0:
            grad_out[...] = part_out
        else:
            grad_out[...] += part_out
    for_key = jnp.where(lane < HEAD_DIM, key_sum[0], key_sum[1])
    for_value = jnp.where(lane < HEAD_DIM, value_sum[0], value_sum[1])
    if earlier is not None:
        for_key = for_key + earlier[0][...]
        for_value = for_value + earlier[1][...]
        grad_out[...] += earlier[2][...]
    grad_key[...] = for_key.astype(grad_key.dtype)
    grad_value[...] = for_value.astype(grad_value.dtype)


def attend_back(where, steps, qkv, one, penalty, out, kept, pieces, earlier=()):
    rows, lanes = qkv.shape[0], qkv.shape[1] // 3
    pairs, width, block = lanes // LANES, out.shape[1], rows // RING
    out_rows = pl.BlockSpec((LANES, width), lambda j: (j, 0))
    sums = LOW if earlier else WIDE
    group = (rows, lanes)
    some = (len(steps) * block, lanes)

    def kernel(*refs):
        attend_back_kernel(steps, *refs)

    return pl.pallas_call(
        kernel,
        grid=(pairs,),
        in_specs=[SCALARS]
        + [by_pair(qkv.shape, k * pairs) for k in range(3)]
        + [whole(one), whole(penalty), out_rows]
        + [by_pair(array.shape) for array in kept]
        + [whole(piece) for piece in pieces]
        + ([by_pair(group)] * 2 + [out_rows] if earlier else []),
        out_specs=[by_pair(some), by_pair(group), by_pair(group), out_rows],
        out_shape=[
            shape_of(some, LOW),
            shape_of(group, sums),
            shape_of(group, sums),
            shape_of((lanes, width), WIDE),
        ],
        scratch_shapes=[pltpu.VMEM((2, rows, LANES), WIDE)] * 2,
        compiler_params=pltpu.CompilerParams(vmem_limit_bytes=24 * MIB),
        cost_estimate=takes(5.0 * len(steps)),
    )(where, qkv, qkv, qkv, one, penalty, out, *kept, *pieces, *earlier)


NEAR = (0, 1, 3)
FAR = (2,)


def project_kernel(near, far, weight, own, after_low, before_high, right, left):
    rows = far.shape[0]
    half = rows // 2
    own[...] = dot(near[:rows], weight[...], NN)
    block = dot(near[rows : 2 * rows], weight[...], NN)
    after_low[...] = block[:half]
    right[half:] = block[half:].astype(LOW)
    block = dot(near[2 * rows :], weight[...], NN)
    left[half:] = block[:half].astype(LOW)
    before_high[...] = block[half:]
    block = dot(far[...], weight[...], NN)
    right[:half] = block[:half].astype(LOW)
    left[:half] = block[half:].astype(LOW)


def arrived_sum(own, from_prev, from_next, prev_low, next_high):
    half = prev_low.shape[0]
    low = prev_low[...].astype(WIDE) + from_next[half:].astype(WIDE)
    high = from_prev[half:].astype(WIDE) + next_high[...].astype(WIDE)
    return own[...] + jnp.concatenate([low, high])


def middle_kernel(tokens, vecs, *refs):
    arrivals, (middle, low, high) = refs[:5], refs[5:]
    half = low.shape[0]
    middle[...] = tokens[...].astype(WIDE) + (arrived_sum(*arrivals) + vecs[4:5])
    unit, _ = normalise(middle[...])
    normed = (unit * vecs[5:6] + vecs[6:7]).astype(LOW)
    low[...] = normed[:half]
    high[...] = normed[half:]


def hidden_rows(where, vecs, up, down, cotangents, pieces, place, outs):
    normed, hidden, grad_pre, column = outs
    rows = 2 * pieces[0].shape[0]
    at = pl.ds(place * rows, rows)
    block = both(pieces, place)
    normed[at] = block
    pre_act = dot(block, up[...], NN) + vecs[pl.ds(7 + where[3], 1)]
    below = 0.5 * (1.0 + lax.erf(pre_act * (0.5**0.5)))
    hidden[at] = (pre_act * below).astype(LOW)
    slope = below + pre_act * (jnp.exp(-0.5 * pre_act * pre_act) * 0.3989422804014327)
    grad = (dot(both(cotangents, place), down[...], NT) * slope).astype(LOW)
    grad_pre[at] = grad
    column[...] += jnp.sum(grad.astype(WIDE), 0, keepdims=True)
    return dot(grad, up[...], NT)


def hidden_near_kernel(where, vecs, up, down, *refs):
    cotangents, pieces, outs = refs[:6], refs[6:12], refs[12:16]
    own, after_low, before_high, after_high, before_low = refs[16:]
    half = pieces[0].shape[0]
    outs[3][...] = jnp.zeros(outs[3].shape, WIDE)
    for place in range(3):
        block = hidden_rows(where, vecs, up, down, cotangents, pieces, place, outs)
        if place == 0:
            own[...] = block
        elif place == 1:
            after_low[...] = block[:half]
            after_high[...] = block[half:].astype(LOW)
        else:
            before_low[...] = block[:half].astype(LOW)
            before_high[...] = block[half:]


def hidden_far_kernel(where, vecs, up, down, *refs):
    cotangents, pieces, refs = refs[:2], refs[2:4], refs[4:]
    column, after_high, before_low, outs, (right, left) = refs[0], refs[1], refs[2], refs[3:7], refs[7:]
    half = pieces[0].shape[0]
    outs[3][...] = column[...]
    block = hidden_rows(where, vecs, up, down, cotangents, pieces, 0, outs)
    right[:half] = block[:half].astype(LOW)
    left[:half] = block[half:].astype(LOW)
    right[half:] = after_high[...]
    left[half:] = before_low[...]


def by_core(where, hold, keep, give):
    for chip in range(keep.shape[0]):
        keep[chip] = hold[2 * chip + where[2]]
        give[chip] = hold[2 * chip + 1 - where[2]].astype(LOW)


def ffn_grads_kernel(where, *refs):
    normed, hidden, grad_pre, cotangents, refs = refs[:2], refs[2:4], refs[4:6], refs[6:14], refs[14:]
    keep, give, hold = refs
    width = normed[0].shape[1]
    part = width // RING
    cot = [jnp.concatenate([block[...] for block in part]) for part in (cotangents[:6], cotangents[6:])]
    for k in range(RING):
        here = slice(k * part, (k + 1) * part)
        block = sum(dot(normed[p][:, here], grad_pre[p][...], TN) for p in range(2))
        hold[:, :SUBLANES, k * width : (k + 1) * width] = block.reshape(-1, SUBLANES, width)
        block = sum(dot(hidden[p][:, here], cot[p], TN) for p in range(2))
        block = block.reshape(-1, RING, SUBLANES, width)
        owners = block.shape[0]
        for q in range(RING):
            hold[k * owners : (k + 1) * owners, SUBLANES:, q * width : (q + 1) * width] = block[:, q]
    by_core(where, hold, keep, give)


def grad_middle_kernel(middle, cotangent, vecs, *refs):
    arrivals, (grad_middle, low, high, sums) = refs[:5], refs[5:]
    half = low.shape[0]
    grad = arrived_sum(*arrivals)
    unit, scale = normalise(middle[...])
    cot = cotangent[...].astype(WIDE)
    total = cot + normalise_back(grad, unit, scale, vecs[5:6])
    grad_middle[...] = total
    rounded = total.astype(LOW)
    low[...] = rounded[:half]
    high[...] = rounded[half:]
    sums[...] = jnp.concatenate(
        [
            jnp.sum(rounded.astype(WIDE), 0, keepdims=True),
            jnp.sum(grad * unit, 0, keepdims=True),
            jnp.sum(grad, 0, keepdims=True),
            jnp.sum(cot, 0, keepdims=True),
            jnp.zeros((4, cot.shape[1]), WIDE),
        ]
    )


def query_rows(near, far, step):
    rows = far.shape[0]
    if step in FAR:
        return far[...]
    place = NEAR.index(step)
    return near[place * rows : (place + 1) * rows]


def back_product_kernel(where, weight, query_near, query_far, grad_key, grad_value, *refs):
    blocks, stats, (other_right, other_left) = refs[:8], refs[8], refs[9:11]
    pieces, sums = refs[11:16], refs[16]
    own, after_low, before_high, right, left = pieces
    right[own.shape[0] :] = other_right[...]
    left[own.shape[0] :] = other_left[...]
    lanes = query_far.shape[1]
    rows = own.shape[0]
    half = rows // 2
    for step in range(RING):
        here = rows_of(where, step, rows)
        block = dot(query_rows(query_near, query_far, step), weight[:, :lanes], NT)
        block += dot(grad_key[here], weight[:, lanes : 2 * lanes], NT)
        block += dot(grad_value[here], weight[:, 2 * lanes :], NT)
        if step == 0:
            own[...] = block
        elif step == 1:
            after_low[...] = block[:half]
            right[half:rows] = block[half:].astype(LOW)
        elif step == 2:
            right[:half] = block[:half].astype(LOW)
            left[:half] = block[half:].astype(LOW)
        else:
            before_high[...] = block[half:]
            left[half:rows] = block[:half].astype(LOW)
        row_stats = stats[step * rows : (step + 1) * rows]
        unit = (both(blocks, step).astype(WIDE) - row_stats[:, 0:1]) * row_stats[:, 1:2]
        pair = jnp.concatenate(
            [
                jnp.sum(block * unit, 0, keepdims=True),
                jnp.sum(block, 0, keepdims=True),
                jnp.zeros((6, block.shape[1]), WIDE),
            ]
        )
        if step == 0:
            sums[...] = pair
        else:
            sums[...] += pair


def grads_kernel(
    where,
    normed,
    query_near,
    query_far,
    grad_key,
    grad_value,
    grad_out,
    first_sums,
    sums,
    column,
    keep,
    give,
    vecs,
    hold,
):
    rows, lanes = query_far.shape
    queries = [query_rows(query_near, query_far, step) for step in range(RING)]
    vecs[...] = jnp.zeros(vecs.shape, WIDE)
    at = pl.ds(pl.multiple_of(where[3] * lanes, lanes), lanes)
    vecs[0:2] = first_sums[0:2]
    vecs[2:3, at] = sum(jnp.sum(block.astype(WIDE), 0, keepdims=True) for block in queries)
    vecs[3:4, at] = jnp.sum(grad_value[...].astype(WIDE), 0, keepdims=True)
    vecs[4:7] = sums[0:3]
    for k in range(RING):
        vecs[7 + k : 8 + k] = jnp.where(where[3] == k, column[...], 0.0)
    vecs[11:12] = sums[3:4]
    for part in range(RING):
        here = slice(part * lanes, (part + 1) * lanes)
        left = normed[:, here]
        block = jnp.concatenate(
            [sum(dot(normed[rows_of(where, k, rows), here], queries[k], TN) for k in range(RING))]
            + [dot(left, third[...], TN) for third in (grad_key, grad_value)]
            + [vecs[:, here].T, grad_out[:, here]],
            axis=1,
        )
        hold[:, part * SUBLANES : (part + 1) * SUBLANES] = block.reshape(
            -1, SUBLANES, block.shape[1]
        )
    by_core(where, hold, keep, give)


def relay_kernel(from_prev, from_next, after, before, other_after, other_before, forth, back):
    half = after.shape[0]
    for place, (right, left) in enumerate(((after, before), (other_after, other_before))):
        here, there = pl.ds(2 * place * half, half), pl.ds(place * half, half)
        forth[there] = (right[...] + from_prev[here].astype(WIDE)).astype(LOW)
        back[there] = (left[...] + from_next[here].astype(WIDE)).astype(LOW)


def outputs_kernel(
    tokens, grad_middle, middle, vecs, own, other, from_prev, from_next, prev, following, grad, out
):
    half = own.shape[0] // 2
    sums = []
    for place, mine in enumerate((own, other)):
        at = pl.ds((2 * place + 1) * half, half)
        here = pl.ds(place * half, half)
        low = prev[here].astype(WIDE) + from_next[at].astype(WIDE)
        high = from_prev[at].astype(WIDE) + following[here].astype(WIDE)
        sums.append(mine[...] + jnp.concatenate([low, high]))
    unit, scale = normalise(tokens[...].astype(WIDE))
    grad[...] = (grad_middle[...] + normalise_back(sums[0], unit, scale, vecs[0:1])).astype(LOW)
    out[...] = (middle[...] + (sums[1] + vecs[11:12])).astype(LOW)


def states_kernel(where, *refs):
    qkv, up, outs, hold = refs[0:3], refs[3:6], refs[6:10], refs[10]
    own, lanes, wide = qkv[0].shape[0], qkv[0].shape[1] // (3 * RING), up[0].shape[1] // RING
    hold[...] = jnp.zeros(hold.shape, WIDE)
    for step in range(RING):
        place = (where[3] + step) % RING
        for kind in range(3):
            at = pl.ds(pl.multiple_of(place * wide, wide), wide)
            hold[kind * own : (kind + 1) * own] = up[kind][:, at]
            there = slice((3 + kind) * own, (4 + kind) * own)
            for third in range(3):
                at = pl.ds(pl.multiple_of(third * lanes * RING + place * lanes, lanes), lanes)
                hold[there, third * lanes : (third + 1) * lanes] = qkv[kind][:, at]
        outs[step][...] = hold[...].astype(LOW)


def adam_step(grad_mean, moment, square, weight, decay_rate):
    moment_new = BETA * moment + (1.0 - BETA) * grad_mean
    square_new = BETA * square + (1.0 - BETA) * grad_mean * grad_mean
    correct = 1.0 - BETA**STEP
    direction = (
        moment_new / correct / (jnp.sqrt(square_new / correct) + ADAM_EPS) + decay_rate * weight
    )
    return (moment_new, square_new, direction)


def row_of(values):
    lane = lax.broadcasted_iota(jnp.int32, (1, LANES), 1)
    return sum(jnp.where(lane == k, value, 0.0) for k, value in enumerate(values))


def ring_totals(parts):
    return (parts[0][...] + parts[1][...].astype(WIDE)) + (
        parts[2][...].astype(WIDE) + parts[3][...].astype(WIDE)
    )


def rows_sums(sums, ffn_sums, lanes):
    own, wide = ffn_sums.shape[0] // 2, ffn_sums.shape[1] // RING
    out_sum = jnp.concatenate(
        [sums[part * own : (part + 1) * own, -lanes:] for part in range(RING)], axis=1
    )
    down_sum = jnp.concatenate(
        [ffn_sums[own:, part * wide : (part + 1) * wide] for part in range(RING)]
    )
    return out_sum, down_sum


def norms_kernel(where, *refs):
    arrived, states, plain = refs[0:4], refs[4:8], refs[8:14]
    pieces, outs, sums, ffn_sums = refs[14:18], refs[18:24], refs[24], refs[25]
    own, wide = ffn_sums.shape[0] // 2, ffn_sums.shape[1] // RING
    lanes = (sums.shape[1] - LANES) // 4
    narrow = sums.shape[1] - lanes
    totals = ring_totals(arrived)
    width, columns = ffn_sums.shape[1], sums.shape[1]
    ffn_sums[...] = totals[:, :width]
    sums[: 2 * own] = totals[:, width : width + columns]
    sums[2 * own :] = totals[:, width + columns :]
    squares = [jnp.zeros((1, 1), WIDE)] * 8

    def add(k, weight, moment, square, grad, targets=()):
        results = adam_step(grad / GROUPS, moment, square, weight, DECAY)
        for target, result in zip(targets, results):
            target[...] = result
        direction = results[2]
        squares[k] = squares[k] + jnp.sum(weight * weight, keepdims=True)
        squares[4 + k] = squares[4 + k] + jnp.sum(direction * direction, keepdims=True)

    for step in range(RING):
        place = (where[3] + step) % RING
        at = pl.ds(pl.multiple_of(place * wide, wide), wide)
        here = pl.ds(pl.multiple_of(place * own, own), own)
        state = states[step][...].astype(WIDE)
        for k, grad in enumerate((ffn_sums[:own, at], sums[here, : 3 * lanes])):
            kinds = (
                state[(3 * k + kind) * own : (3 * k + kind + 1) * own, : grad.shape[1]]
                for kind in range(3)
            )
            add(2 - 2 * k, *kinds, grad)
    for k, grad in enumerate(rows_sums(sums, ffn_sums, lanes)):
        kinds = (plain[3 * k + kind][...] for kind in range(3))
        add(1 + 2 * k, *kinds, grad, outs[3 * k : 3 * k + 3])
    row = row_of([jnp.zeros((1, 1), WIDE)] * VECS + squares)
    for step in range(RING):
        place = (where[3] + step) % RING
        at = pl.ds(pl.multiple_of(place * wide, wide), wide)
        here = pl.ds(pl.multiple_of(place * own, own), own)
        pieces[step][:, :narrow] = sums[here, :narrow]
        pieces[step][:, 3 * lanes : narrow] += row
        pieces[step][:, narrow:] = ffn_sums[:own, at]


def row_kernel(where, *refs):
    pieces, row, hold = refs[:RING], refs[RING], refs[RING + 1]
    for step, piece in enumerate(pieces):
        lanes = (piece.shape[1] - LANES) // 7
        hold[(where[3] + step) % RING] = piece[0:1, 3 * lanes : 3 * lanes + LANES]
    row[...] = (hold[0] + hold[1]) + (hold[2] + hold[3])


def adam_kernel(where, *refs):
    home, refs = refs[:RING], refs[RING:]
    weights, moments, squares, outs = refs[0:3], refs[3:6], refs[6:9], refs[9:18]
    sums = refs[18:20]
    lanes, wide = sums[0].shape[1] // (3 * RING), sums[1].shape[1] // RING
    for step in range(RING):
        place = (where[3] + step) % RING
        for third in range(3):
            at = pl.multiple_of(third * lanes * RING + place * lanes, lanes)
            sums[0][:, pl.ds(at, lanes)] = home[step][:, third * lanes : (third + 1) * lanes]
        at = pl.ds(pl.multiple_of(place * wide, wide), wide)
        sums[1][:, at] = home[step][:, 3 * lanes + LANES :]
    columns = weights[2].shape[1]
    vec_sum = sum(home[step][:, 3 * lanes : 3 * lanes + LANES] for step in range(RING))
    for k, grad in enumerate((sums[0][...], sums[1][...], vec_sum[:, :columns])):
        weight = weights[k][...]
        moment, square, direction = adam_step(
            grad / GROUPS, moments[k][...], squares[k][...], weight, DECAY if k < 2 else 0.0
        )
        outs[3 * k][...] = moment
        outs[3 * k + 1][...] = square
        outs[3 * k + 2][...] = direction if k < 2 else weight - VEC_RATE * direction


def update_kernel(where, row, *refs):
    weights, directions, news, norms = refs[0:4], refs[4:8], refs[8:12], refs[12]
    root = jnp.sqrt(row[...])
    for k in range(4):
        weight_norm, update_norm = root[:, VECS + k : VECS + k + 1], root[:, VECS + 4 + k : VECS + 5 + k]
        norms[k : k + 1, 0:1] = weight_norm
        norms[k : k + 1, 1:2] = update_norm
        news[k][...] = weights[k][...] - RATE * (weight_norm / update_norm) * directions[k][...]


def on_device(
    tokens,
    cotangent,
    seg_counts,
    qkv_master,
    out_master,
    up_master,
    down_master,
    qkv_first,
    out_first,
    up_first,
    down_first,
    qkv_second,
    out_second,
    up_second,
    down_second,
    vec_master,
    vec_first,
    vec_second,
):
    where = jnp.stack([lax.axis_index(axis) for axis in EVERY]).astype(jnp.int32)
    rows, width = tokens.shape
    own = qkv_master.shape[0]
    lanes = width // RING
    hidden_lanes = up_master.shape[1] // RING
    chips = lax.axis_size("x") * lax.axis_size("y")
    group = rows * RING
    half = rows // 2
    wide_rows, half_rows = shape_of((rows, width), WIDE), shape_of((half, width), LOW)
    low_rows, group_low = shape_of((rows, width), LOW), shape_of((group, width), LOW)

    token_rows = Gather(tokens[:half], tokens[half:])
    arrived = to_places(weight_pieces(where, qkv_master, up_master, vec_master))
    arrived, token_rows.near = together(arrived, token_rows.near)
    token_rows.relay()
    att_block, ffn_block = weight_blocks(where, arrived, out_master, down_master)
    att_ring = along_ring(att_block, 0)
    states = staged_call(
        states_kernel,
        [shape_of((6 * own, width), LOW)] * RING,
        where,
        [qkv_master, qkv_first, qkv_second, up_master, up_first, up_second],
        [pltpu.VMEM((6 * own, width), WIDE)],
        limit=12,
    )
    states = to_places(together(att_block, states)[1])
    att_ring, token_rows.crossed, token_rows.far, ffn_block, cot = together(
        att_ring, token_rows.crossed, token_rows.far, ffn_block, cotangent
    )
    token_blocks = token_rows.blocks()
    att_ring = along_ring(jnp.stack(att_ring), 1)
    cot_rows = Gather(cot[:half], cot[half:])
    ffn_ring = along_ring(ffn_block, 0)
    att_ring, ffn_ring, states = together(att_ring, ffn_ring, states)
    att_mine = by_chip(where, att_ring)
    att_theirs = send(att_mine, "c", 1)
    ffn_ring = along_ring(jnp.stack(ffn_ring), 1)
    w_qkv, w_out, vecs = attention_weights(where, att_mine, att_theirs)
    w_qkv, cot_rows.near = together(w_qkv, cot_rows.near)
    cot_rows.relay()
    one, penalty = whole_call(
        images_kernel, [shape_of((group, LANES), LOW)] * 2, seg_counts, [], limit=8
    )

    normed, qkv, stats = whole_call(
        first_kernel,
        [group_low, shape_of((group, 3 * lanes), LOW), shape_of((group, LANES), WIDE)],
        where,
        [vecs, w_qkv, *token_blocks],
        limit=10,
        micros=3.0,
    )
    attended, log_total, exact, right, left = attend(where, LEAVING, qkv, one, penalty, w_out)
    right, left, qkv_again, ffn_ring, cot_rows.far, cot_rows.crossed = together(
        right, left, qkv, ffn_ring, cot_rows.far, cot_rows.crossed
    )
    cot_blocks = cot_rows.blocks()
    attended_too, log_total_too, exact_too, *staying = attend(where, STAYING, qkv_again, one, penalty, w_out)
    arrivals, _ = scatter_z(right, left, staying)
    ffn_mine = by_chip(where, ffn_ring)
    ffn_theirs = send(ffn_mine, "c", 1)
    middle, *mid_halves = whole_call(
        middle_kernel,
        [wide_rows, half_rows, half_rows],
        None,
        [tokens, vecs, *arrivals],
        limit=6,
    )

    mid_rows = Gather(*mid_halves)
    w_up, w_down = ffn_weights(where, ffn_mine, ffn_theirs)
    w_up, w_down, mid_rows.near = together(w_up, w_down, mid_rows.near)
    mid_rows.relay()
    mid_blocks = mid_rows.blocks()
    near, far = [0, 1, 2, 3, 6, 7], [4, 5]
    wide_half = shape_of((half, width), WIDE)
    some = shape_of((3 * rows, hidden_lanes), LOW)
    column = shape_of((1, hidden_lanes), WIDE)
    near_outs = whole_call(
        hidden_near_kernel,
        [some] * 3 + [column, wide_rows, wide_half, wide_half, half_rows, half_rows],
        where,
        [vecs, w_up, w_down, *(cot_blocks[k] for k in near), *(mid_blocks[k] for k in near)],
        limit=20,
        micros=6.5,
    )
    near_outs, far_blocks = together(near_outs, [mid_blocks[k] for k in far])
    *near_rows, up_column, wide_own, after_low, before_high, after_high, before_low = near_outs
    *far_rows, up_column, right, left = whole_call(
        hidden_far_kernel,
        [low_rows] * 3 + [column, low_rows, low_rows],
        where,
        [vecs, w_up, w_down, *(cot_blocks[k] for k in far), *far_blocks]
        + [up_column, after_high, before_low],
        limit=14,
        micros=3.0,
    )
    ffn_piece = (chips, 2 * own, RING * width)
    ffn_keep, ffn_give = whole_call(
        ffn_grads_kernel,
        [shape_of(ffn_piece, WIDE), shape_of(ffn_piece, LOW)],
        where,
        [block for pair in zip(near_rows, far_rows) for block in pair]
        + [cot_blocks[k] for k in near + far],
        [pltpu.VMEM((2 * chips, *ffn_piece[1:]), WIDE)],
        limit=32,
        micros=6.5,
    )
    arrivals, (ffn_keep, ffn_give) = scatter_z(
        right, left, [wide_own, after_low, before_high], (ffn_keep, ffn_give)
    )
    ffn_own, *ffn_gone = core_sum(where, ffn_keep, send(ffn_give, "c", 1), 2.0)
    ffn_arrived = back_along_ring(ffn_own, ffn_gone, 0)
    arrivals, ffn_own = together(arrivals, ffn_own)
    grad_middle, *grad_halves, mid_sums = whole_call(
        grad_middle_kernel,
        [wide_rows, half_rows, half_rows, shape_of((8, width), WIDE)],
        None,
        [middle, cotangent, vecs, *arrivals],
        limit=8,
    )
    grad_rows = Gather(*grad_halves)
    out_own, out_after, out_before, out_right, out_left = whole_call(
        project_kernel,
        [wide_rows, wide_half, wide_half, low_rows, low_rows],
        None,
        [near_rows[1], far_rows[1], w_down],
        limit=12,
        micros=2.5,
    )
    grad_rows.near, out_own = together(grad_rows.near, out_own)
    grad_rows.relay()

    grad_blocks = grad_rows.blocks()
    kept = [log_total, log_total_too, attended, attended_too, exact, exact_too]
    near_outs = attend_back(
        where, NEAR, qkv, one, penalty, w_out, kept, [grad_blocks[k] for k in near]
    )
    near_outs, far_blocks = together(near_outs, [grad_blocks[k] for k in far])
    query_near, *earlier = near_outs
    query_far, grad_key, grad_value, grad_out = attend_back(
        where, FAR, qkv, one, penalty, w_out, kept, far_blocks, earlier
    )
    query_far, ffn_arrived = together(query_far, ffn_arrived)
    two_low = shape_of((2 * rows, width), LOW)
    normed_own, normed_after, normed_before, right, left, first_sums = whole_call(
        back_product_kernel,
        [wide_rows, wide_half, wide_half, two_low, two_low, shape_of((8, width), WIDE)],
        where,
        [w_qkv, query_near, query_far, grad_key, grad_value, *token_blocks]
        + [stats, out_right, out_left],
        limit=14,
        micros=3.0,
    )
    columns = 4 * lanes + LANES
    piece = (chips, RING * own, columns)
    att_keep, att_give = whole_call(
        grads_kernel,
        [shape_of(piece, WIDE), shape_of(piece, LOW)],
        where,
        [normed, query_near, query_far, grad_key, grad_value]
        + [grad_out, first_sums, mid_sums, up_column],
        [pltpu.VMEM((LANES, width), WIDE), pltpu.VMEM((2 * chips, *piece[1:]), WIDE)],
        limit=24,
        micros=3.0,
    )

    att_got = send(att_give, "c", 1)
    right, left, att_keep = together(right, left, att_keep)
    from_prev, from_next = send(right, "z", 1), send(left, "z", -1)
    att_own, *att_gone = core_sum(where, att_keep, att_got, 1.0)
    att_arrived = back_along_ring(att_own, att_gone, 0)
    sums_own, *sums_gone = ring_sum(att_arrived, ffn_arrived)
    sums_arrived = back_along_ring(sums_own, sums_gone, 1)
    home_piece = shape_of((own, 3 * lanes + LANES + hidden_lanes), WIDE)
    kinds = [
        shape_of(weight.shape, WIDE)
        for weight in (qkv_master, out_master, up_master, down_master, vec_master)
    ]
    *pieces, out_first_new, out_second_new, out_dir, down_first_new, down_second_new, down_dir = (
        whole_call(
            norms_kernel,
            [home_piece] * RING + [kinds[1]] * 3 + [kinds[3]] * 3,
            where,
            [*sums_arrived, *states]
            + [out_master, out_first, out_second, down_master, down_first, down_second],
            [pltpu.VMEM(piece[1:], WIDE), pltpu.VMEM(ffn_piece[1:], WIDE)],
            limit=14,
            micros=3.0,
        )
    )
    home = to_places(pieces)
    from_prev, from_next, pieces = together(from_prev, from_next, pieces)
    forth, back = whole_call(
        relay_kernel,
        [low_rows, low_rows],
        None,
        [from_prev, from_next, normed_after, normed_before, out_after, out_before],
        limit=10,
    )
    home, forth, back = together(home, forth, back)
    forth, back = send(forth, "z", 1), send(back, "z", -1)
    row = whole_call(
        row_kernel,
        shape_of((1, LANES), WIDE),
        where,
        home,
        [pltpu.VMEM((RING, 1, LANES), WIDE)],
        limit=4,
    )
    row, _ = sum_pairs(row, "x", 1)
    stepped =whole_call(
        adam_kernel,
        [kinds[0]] * 3 + [kinds[2]] * 3 + [kinds[4]] * 3,
        where,
        [*home, qkv_master, up_master, vec_master, qkv_first, up_first, vec_first]
        + [qkv_second, up_second, vec_second],
        [pltpu.VMEM(qkv_master.shape, WIDE), pltpu.VMEM(up_master.shape, WIDE)],
        limit=10,
    )
    row, stepped = sum_pairs(row, "x", 2, stepped)
    (
        qkv_first_new,
        qkv_second_new,
        qkv_dir,
        up_first_new,
        up_second_new,
        up_dir,
        vec_first_new,
        vec_second_new,
        vec_new,
    ) = stepped
    outputs = whole_call(
        outputs_kernel,
        [low_rows, low_rows],
        None,
        [tokens, grad_middle, middle, vecs, normed_own, out_own, from_prev, from_next, forth, back],
        limit=14,
    )
    row, _ = sum_pairs(row, "y", 1)
    row, outputs = sum_pairs(row, "y", 2, outputs)
    row, _ = sum_pairs(row, "c", 1)
    input_grad, layer_out = outputs
    *new_mats, matrix_norms = whole_call(
        update_kernel,
        kinds[:4] + [shape_of((4, 2), WIDE)],
        where,
        [row, qkv_master, out_master, up_master, down_master, qkv_dir, out_dir, up_dir, down_dir],
        limit=8,
    )
    return (
        layer_out,
        input_grad,
        *new_mats,
        qkv_first_new,
        out_first_new,
        up_first_new,
        down_first_new,
        qkv_second_new,
        out_second_new,
        up_second_new,
        down_second_new,
        vec_new,
        vec_first_new,
        vec_second_new,
        matrix_norms,
    )


def solution(mesh):
    sizes = (4, 4, 2, 4)
    physical = Mesh(mesh.devices.reshape(sizes), EVERY)
    patches = P(EVERY, None)
    shards = P(("z", *DATA), None)
    return jax.shard_map(
        on_device,
        mesh=physical,
        in_specs=(patches, patches, P(DATA, None)) + (shards,) * 15,
        out_specs=(patches, patches) + (shards,) * 15 + (P(),),
        check_vma=False,
    )
```
